32 devices in a mesh: seq: 16 (over z, y, x), shard: 2 (over core).
Axes of the slice: x: 2, y: 2, z: 4, core: 2. Of those that a mesh axis runs over, the one named last changes fastest.
Arguments:
- tokens: bfloat16 [2, 2048, 768], P('shard', 'seq'), may hold values from -6 to 6
- cotangent: bfloat16 [2, 2048, 768], P('shard', 'seq'), may hold values from -6 to 6
- lengths: int32 [2], replicated, may hold values from 1921 to 2048
- qkv_weight: bfloat16 [768, 2304], P('shard'), may hold values from -0.21875 to 0.21875
- query_bias: bfloat16 [768], P('shard'), may hold values from -1.75 to 1.75
- value_bias: bfloat16 [768], P('shard'), may hold values from -1.75 to 1.75
- out_weight: bfloat16 [768, 768], P('shard'), may hold values from -6 to 6
- out_bias: bfloat16 [768], P('shard'), may hold values from -1.75 to 1.75
- first_gain: bfloat16 [768], P('shard'), may hold values from 0.5 to 1.5
- first_shift: bfloat16 [768], P('shard'), may hold values from -1.75 to 1.75
- up_weight: bfloat16 [768, 3072], P('shard'), may hold values from -0.21875 to 0.21875
- up_bias: bfloat16 [3072], P('shard'), may hold values from -1.75 to 1.75
- down_weight: bfloat16 [3072, 768], P('shard'), may hold values from -0.109375 to 0.109375
- down_bias: bfloat16 [768], P('shard'), may hold values from -1.75 to 1.75
- second_gain: bfloat16 [768], P('shard'), may hold values from 0.5 to 1.5
- second_shift: bfloat16 [768], P('shard'), may hold values from -1.75 to 1.75
Outputs:
- layer_out: bfloat16 [2, 2048, 768], P('shard', 'seq')
- input_grad: float32 [2, 2048, 768], P('shard', 'seq')
- qkv_weight_grad: float32 [768, 2304], P('shard')
- query_bias_grad: float32 [768], P('shard')
- value_bias_grad: float32 [768], P('shard')
- out_weight_grad: float32 [768, 768], P('shard')
- out_bias_grad: float32 [768], P('shard')
- first_gain_grad: float32 [768], P('shard')
- first_shift_grad: float32 [768], P('shard')
- up_weight_grad: float32 [768, 3072], P('shard')
- up_bias_grad: float32 [3072], P('shard')
- down_weight_grad: float32 [3072, 768], P('shard')
- down_bias_grad: float32 [768], P('shard')
- second_gain_grad: float32 [768], P('shard')
- second_shift_grad: float32 [768], P('shard')
The draws below stay inside these ranges and needn't reach their ends.
All inputs are finite; a program needn't handle non-finite values.
Results may differ from the reference program's by a relative error of at most 0.035.
Values may be sent and summed in bfloat16 or wider, within the bound.
No kernel may reach another device: no remote copies, remote signals or barrier semaphores. Data moves between devices by JAX's collectives and lax.ppermute only.
A program may use at most 192 MiB of HBM per device.

```python
import math
import jax
import jax.numpy as jnp
from jax import lax

D = 768
HEADS = 12
HEAD_DIM = 64
FF = 3072
TOK_DEV = 128
SEQS = 2
SEQ_LEN = 2048


def level_of(stream_key, extent, cuts, smallest, top_value):
    level = 1.0
    for axis_at, shards_of in cuts:
        heights = jax.random.uniform(jax.random.fold_in(jax.random.fold_in(stream_key, 6), axis_at), (shards_of,), jnp.float32, smallest / len(cuts), top_value / len(cuts))
        level = level * jnp.repeat(jnp.exp(heights), extent[axis_at] // shards_of).reshape((-1,) + (1,) * (len(extent) - 1 - axis_at))
    return level


def gaussian(key, dims, width, most, cuts=(), kind=jnp.bfloat16):
    loudness = level_of(key, dims, cuts, -0.22, 0.18) if cuts else 1.0
    drawn = jax.random.normal(key, dims, jnp.float32) * width * loudness
    return jnp.minimum(jnp.maximum(drawn, -most), most).astype(kind)


def setup_inputs(seed: int = 0) -> dict:
    key_of = jax.random.split(jax.random.key(seed), 17)
    tokens = gaussian(key_of[0], (SEQS, SEQ_LEN, D), 1.0, 6.0, ((0, 2), (1, 16)))
    cotangent = gaussian(key_of[1], (SEQS, SEQ_LEN, D), 1.0, 6.0, ((0, 2), (1, 16)))
    lengths = jax.random.randint(key_of[2], (SEQS,), SEQ_LEN - TOK_DEV + 1, SEQ_LEN + 1).astype(jnp.int32)
    qkv_weight = gaussian(key_of[3], (D, 3 * D), D ** -0.5, 0.21875, ((0, 2),))
    query_bias = gaussian(key_of[4], (D,), 0.3, 1.75, ((0, 2),))
    value_bias = gaussian(key_of[5], (D,), 0.3, 1.75, ((0, 2),))
    out_weight = gaussian(key_of[6], (D, D), (0.6 * (SEQ_LEN / D) ** 0.5), 6.0, ((0, 2),))
    out_bias = gaussian(key_of[7], (D,), 0.3, 1.75, ((0, 2),))
    first_gain = jnp.clip(1.0 + 0.1 * jax.random.normal(key_of[8], (D,), jnp.float32), 0.5, 1.5).astype(jnp.bfloat16)
    first_shift = gaussian(key_of[9], (D,), 0.3, 1.75, ((0, 2),))
    up_weight = gaussian(key_of[10], (D, FF), D ** -0.5, 0.21875, ((0, 2),))
    up_bias = gaussian(key_of[11], (FF,), 0.3, 1.75, ((0, 2),))
    down_weight = gaussian(key_of[12], (FF, D), FF ** -0.5, 0.109375, ((0, 2),))
    down_bias = gaussian(key_of[13], (D,), 0.3, 1.75, ((0, 2),))
    second_gain = jnp.clip(1.0 + 0.1 * jax.random.normal(key_of[14], (D,), jnp.float32), 0.5, 1.5).astype(jnp.bfloat16)
    second_shift = gaussian(key_of[15], (D,), 0.3, 1.75, ((0, 2),))
    return dict(tokens=tokens, cotangent=cotangent, lengths=lengths, qkv_weight=qkv_weight, query_bias=query_bias, value_bias=value_bias, out_weight=out_weight, out_bias=out_bias, first_gain=first_gain, first_shift=first_shift, up_weight=up_weight, up_bias=up_bias, down_weight=down_weight, down_bias=down_bias, second_gain=second_gain, second_shift=second_shift)


@jax.custom_vjp
def low(v):
    return lax.optimization_barrier(v.astype(jnp.bfloat16)).astype(jnp.float32)

@jax.custom_vjp
def low_back(v):
    return v

def low_keep(v):
    return (low(v), None)

def low_pass(kept, grad):
    return (grad,)

def back_keep(v):
    return (v, None)

def back_low(kept, grad):
    return (low(grad),)
low.defvjp(low_keep, low_pass)
low_back.defvjp(back_keep, back_low)
EPSILON = 1e-12
HIGHEST = lax.Precision.HIGHEST

def matmul(left, right):
    return jnp.dot(left, right, precision=HIGHEST, preferred_element_type=jnp.float32)

def layer_norm(hidden, gain, shift):
    center = hidden - lax.optimization_barrier(jnp.mean(hidden, axis=-1, keepdims=True))
    spread = lax.optimization_barrier(jnp.mean(center * center, axis=-1, keepdims=True))
    return center * lax.rsqrt(spread + EPSILON) * gain + shift

def attend(queries, key_rows, value_rows, length):
    block_rows = math.gcd(SEQ_LEN, 512)
    places = jnp.arange(SEQ_LEN, dtype=jnp.int32)
    usable = (places < length)[None, None, :]

    def one_block(query_rows):
        scores = low_back(jnp.einsum('qhd,khd->hqk', query_rows, key_rows, precision=HIGHEST) * 0.125)
        masked = jnp.where(usable, scores, -1e+30)
        weights = low(jax.nn.softmax(masked, axis=-1))
        return jnp.einsum('hqk,khd->qhd', weights, value_rows, precision=HIGHEST)
    grouped = queries.reshape(SEQ_LEN // block_rows, block_rows, HEADS, HEAD_DIM)
    result = lax.map(jax.checkpoint(one_block), grouped)
    return result.reshape(SEQ_LEN, HEADS * HEAD_DIM)

def forward(lengths, tokens, qkv_weight, query_bias, value_bias, out_weight, out_bias, first_gain, first_shift, up_weight, up_bias, down_weight, down_bias, second_gain, second_shift):
    flat_rows = tokens.reshape(SEQS * SEQ_LEN, D)
    zero_bias = jnp.zeros_like(query_bias)
    joined = matmul(flat_rows, qkv_weight) + jnp.concatenate([query_bias, zero_bias, value_bias])
    joined = low_back(low(joined)).reshape(SEQS, SEQ_LEN, 3, HEADS, HEAD_DIM)
    pieces = []
    for member in range(SEQS):
        pieces.append(attend(joined[member, :, 0], joined[member, :, 1], joined[member, :, 2], lengths[member]))
    context = low_back(low(jnp.concatenate(pieces, axis=0)))
    branch = low_back(matmul(context, out_weight) + out_bias)
    normed_one = low(layer_norm(flat_rows + branch, first_gain, first_shift))
    inner_sum = low_back(matmul(normed_one, up_weight) + up_bias)
    active = low(jax.nn.gelu(inner_sum, approximate=False))
    second = low_back(matmul(active, down_weight) + down_bias)
    return layer_norm(normed_one + second, second_gain, second_shift)

def reference(tokens, cotangent, lengths, qkv_weight, query_bias, value_bias, out_weight, out_bias, first_gain, first_shift, up_weight, up_bias, down_weight, down_bias, second_gain, second_shift):
    params = [item.astype(jnp.float32) for item in (tokens, qkv_weight, query_bias, value_bias, out_weight, out_bias, first_gain, first_shift, up_weight, up_bias, down_weight, down_bias, second_gain, second_shift)]
    result, pullback = jax.vjp(partial_forward(lengths), *params)
    grads = pullback(cotangent.reshape(SEQS * SEQ_LEN, D).astype(jnp.float32))
    layer_out = result.reshape(SEQS, SEQ_LEN, D).astype(jnp.bfloat16)
    input_grad = grads[0].reshape(SEQS, SEQ_LEN, D)
    return (layer_out, input_grad, grads[1], grads[2], grads[3], grads[4], grads[5], grads[6], grads[7], grads[8], grads[9], grads[10], grads[11], grads[12], grads[13])

def partial_forward(lengths):

    def wrapped(*params):
        return forward(lengths, *params)
    return wrapped
```

```python
import functools

import jax
import jax.numpy as jnp
from jax import lax
from jax.experimental import pallas as pl
from jax.experimental.pallas import tpu as pltpu
from jax.sharding import PartitionSpec as P

HEADS = 12
HEAD_DIM = 64
GROUPS = 4
GROUP_HEADS = HEADS // GROUPS
GROUP_WIDTH = GROUP_HEADS * HEAD_DIM
EPSILON = 1e-12
MASKED = -1e30
F32 = jnp.float32
BF16 = jnp.bfloat16


def dot(left, right, dims=((1,), (0,))):
    return lax.dot_general(left, right, (dims, ((), ())), preferred_element_type=F32)


class Places:
    def __init__(self, size):
        self.size = size
        self.plane_size = size // GROUPS
        self.rest = self.plane_size // 4
        index = lambda g, q, m: (g * 4 + q) * self.rest + m
        groups, quarters, members = range(GROUPS), range(4), range(self.rest)
        self.columns = [[index(g, q, m) for g in groups] for q in quarters for m in members]
        self.planes = [[index(g, q, m) for q in quarters for m in members] for g in groups]
        self.fours = [[index(g, q, m) for q in quarters] for g in groups for m in members]
        self.rests = [[index(g, q, m) for m in members] for g in groups for q in quarters]

    def gather(self, block, groups):
        return lax.all_gather(block, "seq", axis=0, axis_index_groups=groups)

    def exchange(self, blocks, groups):
        return lax.all_to_all(blocks, "seq", 0, 0, axis_index_groups=groups, tiled=True)

    def swap(self, block, bits):
        return lax.ppermute(block, "seq", [(i, i ^ bits) for i in range(self.size)])

    def scatter_sum(self, blocks, groups):
        return jnp.sum(self.exchange(blocks, groups).astype(F32), axis=0)


def layer_norm(hidden, gain, shift):
    center = hidden - jnp.mean(hidden, axis=-1, keepdims=True)
    spread = jnp.mean(center * center, axis=-1, keepdims=True)
    return center * lax.rsqrt(spread + EPSILON) * gain + shift


def gelu_exact(values):
    return jax.nn.gelu(values, approximate=False)


ROWS = 128


def attend_kernel(pieces, chunks, *refs):
    q_ref = refs[0]
    key_refs, value_refs, bias_refs = (refs[1 + i * pieces : 1 + (i + 1) * pieces] for i in range(3))
    context_ref, log_ref = refs[1 + 3 * pieces :]
    rows = q_ref.shape[0]
    chunk = key_refs[0].shape[0] // chunks
    for block in range(rows // ROWS):
        at = slice(block * ROWS, (block + 1) * ROWS)
        for head in range(GROUP_HEADS):
            columns = slice(head * HEAD_DIM, (head + 1) * HEAD_DIM)
            query = q_ref[at, columns] * jnp.asarray(0.125, BF16)

            def step(index, state):
                highest, total, mix = state
                start = pl.multiple_of(index * chunk, chunk)
                here = pl.ds(start, chunk)
                scores = [
                    dot(query, k[here, columns], ((1,), (1,))) + b[:, here]
                    for k, b in zip(key_refs, bias_refs)
                ]
                peak = functools.reduce(
                    jnp.maximum, [jnp.max(s, axis=1, keepdims=True) for s in scores]
                )
                raised = jnp.maximum(highest, peak)
                weights = [jnp.exp(s - raised) for s in scores]
                factor = jnp.exp(highest - raised)
                total = total * factor + sum(jnp.sum(w, axis=1, keepdims=True) for w in weights)
                mix = mix * factor + sum(
                    dot(w.astype(BF16), v[here, columns]) for w, v in zip(weights, value_refs)
                )
                return raised, total, mix

            state = (
                jnp.full((ROWS, 1), MASKED, F32),
                jnp.zeros((ROWS, 1), F32),
                jnp.zeros((ROWS, HEAD_DIM), F32),
            )
            if chunks == 1:
                state = step(0, state)
            else:
                state = lax.fori_loop(0, chunks, step, state)
            highest, total, mix = state
            context_ref[at, columns] = mix / total
            log_ref[at, head : head + 1] = highest + jnp.log(total)


def attend(query, keys, values, bias, chunks):
    rows = query.shape[0]
    return pl.pallas_call(
        functools.partial(attend_kernel, len(keys), chunks),
        out_shape=(
            jax.ShapeDtypeStruct((rows, GROUP_WIDTH), F32),
            jax.ShapeDtypeStruct((rows, 128), F32),
        ),
        compiler_params=pltpu.CompilerParams(vmem_limit_bytes=60 * 2**20),
        name="attend",
    )(query, *keys, *values, *bias)


def attend_grad_kernel(pieces, chunks, *refs):
    q_ref, context_ref, grad_ref, log_ref = refs[:4]
    key_refs, value_refs, bias_refs = (refs[4 + i * pieces : 4 + (i + 1) * pieces] for i in range(3))
    query_grad_ref = refs[4 + 3 * pieces]
    key_value_refs = refs[5 + 3 * pieces :]
    rows = q_ref.shape[0]
    chunk = key_refs[0].shape[0] // chunks
    for head in range(GROUP_HEADS):
        columns = slice(head * HEAD_DIM, (head + 1) * HEAD_DIM)
        key_rows = slice(head * HEAD_DIM, (head + 1) * HEAD_DIM)
        value_rows = slice(GROUP_WIDTH + head * HEAD_DIM, GROUP_WIDTH + (head + 1) * HEAD_DIM)
        query = q_ref[:, columns] * jnp.asarray(0.125, BF16)
        grad = grad_ref[:, columns]
        correction = jnp.sum(grad.astype(F32) * context_ref[:, columns], axis=1, keepdims=True)
        log_total = log_ref[:, head : head + 1]
        query_turned = query.T
        grad_turned = grad.T

        def step(index, query_grad):
            start = pl.multiple_of(index * chunk, chunk)
            here = pl.ds(start, chunk)
            for k, v, b, out in zip(key_refs, value_refs, bias_refs, key_value_refs):
                key = k[here, columns]
                probs = jnp.exp(dot(query, key, ((1,), (1,))) + b[:, here] - log_total)
                probs_grad = dot(grad, v[here, columns], ((1,), (1,)))
                score_grad = (probs * (probs_grad - correction)).astype(BF16)
                query_grad = query_grad + dot(score_grad, key)
                out[key_rows, here] = dot(query_turned, score_grad).astype(BF16)
                out[value_rows, here] = dot(grad_turned, probs.astype(BF16)).astype(BF16)
            return query_grad

        total = jnp.zeros((rows, HEAD_DIM), F32)
        total = step(0, total) if chunks == 1 else lax.fori_loop(0, chunks, step, total)
        query_grad_ref[:, columns] = (total * 0.125).astype(BF16)


def attend_grad(query, context, grad, log_total, keys, values, bias, chunks):
    rows = query.shape[0]
    return pl.pallas_call(
        functools.partial(attend_grad_kernel, len(keys), chunks),
        out_shape=(jax.ShapeDtypeStruct((rows, GROUP_WIDTH), BF16),)
        + tuple(jax.ShapeDtypeStruct((2 * GROUP_WIDTH, k.shape[0]), BF16) for k in keys),
        compiler_params=pltpu.CompilerParams(vmem_limit_bytes=60 * 2**20),
        name="attend_grad",
    )(query, context, grad, log_total, *keys, *values, *bias)


def body(
    tokens,
    cotangent,
    lengths,
    qkv_weight,
    query_bias,
    value_bias,
    out_weight,
    out_bias,
    first_gain,
    first_shift,
    up_weight,
    up_bias,
    down_weight,
    down_bias,
    second_gain,
    second_shift,
):
    row_count, model_width = tokens.shape[1], tokens.shape[2]
    hidden_width = up_weight.shape[1]
    places = Places(lax.axis_size("seq"))
    plane_size = places.plane_size
    rank = lax.axis_index("seq")
    core = lax.axis_index("shard")
    group, position = rank // plane_size, rank % plane_size
    length = lengths[core]
    inputs = tokens[0]
    column_rows = GROUPS * row_count
    half = model_width // 2

    def both(block):
        return lax.all_gather(block, "shard", axis=0, tiled=True)

    at = group * GROUP_WIDTH
    own_columns = lambda w: jnp.concatenate(
        [lax.dynamic_slice_in_dim(w, at + i * model_width, GROUP_WIDTH, w.ndim - 1) for i in range(3)],
        axis=-1,
    )
    group_weight = both(own_columns(qkv_weight))
    vectors = [query_bias, value_bias, out_bias, first_gain, first_shift, down_bias, second_gain, second_shift]
    stacked = jnp.concatenate([jnp.stack(vectors), up_bias.reshape(-1, half)])
    stacked = lax.all_gather(stacked, "shard", axis=0).astype(F32)
    whole = jnp.transpose(stacked[:, : len(vectors)], (1, 0, 2)).reshape(len(vectors), model_width)
    (query_offset, value_offset, out_offset, gain_one, shift_one, down_offset, gain_two, shift_two) = whole
    up_offset = stacked[:, len(vectors) :].reshape(hidden_width)
    out_matrix = both(out_weight)
    up_matrix = both(up_weight)
    down_matrix = both(down_weight)

    column_inputs = places.gather(inputs, places.columns).reshape(column_rows, model_width)
    zero_bias = jnp.zeros_like(query_offset)
    offset = own_columns(jnp.concatenate([query_offset, zero_bias, value_offset]))
    joined = (dot(column_inputs, group_weight) + offset).astype(BF16)
    query = joined[:, :GROUP_WIDTH]
    key = joined[:, GROUP_WIDTH : 2 * GROUP_WIDTH]
    value = joined[:, 2 * GROUP_WIDTH :]

    def masks(who):
        starts = (jnp.arange(GROUPS)[:, None] * plane_size + who) * row_count
        tokens_at = starts[:, :, None] + jnp.arange(row_count)
        return jnp.where(tokens_at.transpose(1, 0, 2).reshape(1, -1) < length, 0.0, MASKED).astype(F32)

    if plane_size == 4:
        chunks = 1
        key_one, value_two = places.swap(key, 1), places.swap(value, 2)
        key_two, key_three = places.swap(key, 2), places.swap(key_one, 2)
        value_one, value_three = places.swap(value, 1), places.swap(value_two, 1)
        keys = (key, key_one, key_two, key_three)
        values = (value, value_one, value_two, value_three)
        bias = tuple(masks((position ^ i)[None]) for i in range(4))
    else:
        chunks = plane_size // 4
        keys = (places.gather(key, places.planes).reshape(-1, GROUP_WIDTH),)
        values = (places.gather(value, places.planes).reshape(-1, GROUP_WIDTH),)
        bias = (masks(jnp.arange(plane_size)),)
    context, log_total = attend(query, keys, values, bias, chunks)

    def to_tokens(block):
        blocks = places.exchange(block.reshape(GROUPS, row_count, GROUP_WIDTH), places.columns)
        return jnp.transpose(blocks, (1, 0, 2)).reshape(row_count, model_width)

    def to_heads(block):
        blocks = jnp.transpose(block.reshape(row_count, GROUPS, GROUP_WIDTH), (1, 0, 2))
        return places.exchange(blocks, places.columns).reshape(column_rows, GROUP_WIDTH)

    context_low = to_tokens(context.astype(BF16))
    branch = dot(context_low, out_matrix) + out_offset
    residual_one = inputs.astype(F32) + branch
    normed_one, norm_pull_one = jax.vjp(layer_norm, residual_one, gain_one, shift_one)
    normed_low = normed_one.astype(BF16)
    inner_sum = dot(normed_low, up_matrix) + up_offset
    active, gelu_pull = jax.vjp(gelu_exact, inner_sum)
    active_low = active.astype(BF16)
    second = dot(active_low, down_matrix) + down_offset
    residual_two = normed_low.astype(F32) + second
    outputs, norm_pull_two = jax.vjp(layer_norm, residual_two, gain_two, shift_two)
    residual_two_grad, gain_two_grad, shift_two_grad = norm_pull_two(cotangent[0].astype(F32))
    second_low = residual_two_grad.astype(BF16)
    down_bias_grad = jnp.sum(second_low.astype(F32), axis=0)
    active_grad = dot(second_low, down_matrix, ((1,), (1,)))
    inner_low = gelu_pull(active_grad)[0].astype(BF16)
    up_bias_grad = jnp.sum(inner_low.astype(F32), axis=0)
    normed_grad = dot(inner_low, up_matrix, ((1,), (1,))) + residual_two_grad
    residual_one_grad, gain_one_grad, shift_one_grad = norm_pull_one(normed_grad)
    branch_low = residual_one_grad.astype(BF16)
    out_bias_grad = jnp.sum(branch_low.astype(F32), axis=0)
    context_grad = to_heads(dot(branch_low, out_matrix, ((1,), (1,))).astype(BF16))

    def core_sum(grad):
        rows = grad.shape[0] // 2
        mine = lax.dynamic_slice_in_dim(grad, core * rows, rows, 0)
        other = lax.dynamic_slice_in_dim(grad, (1 - core) * rows, rows, 0)
        received = lax.ppermute(other, "shard", [(0, 1), (1, 0)])
        return (mine.astype(F32) + received.astype(F32)).astype(BF16)

    def four_sum(blocks):
        total = places.scatter_sum(blocks, places.fours)
        if places.rest > 1:
            total = lax.psum(total, "seq", axis_index_groups=places.rests)
        return total.astype(BF16)

    def all_sum(grad):
        rows, columns = grad.shape
        part = four_sum(grad.reshape(4, rows // 4, columns))
        part = jnp.transpose(part.reshape(rows // 4, GROUPS, columns // GROUPS), (1, 0, 2))
        part = places.scatter_sum(part, places.columns).astype(BF16)
        part = jnp.transpose(places.gather(part, places.columns), (1, 0, 2)).reshape(rows // 4, columns)
        return places.gather(part, places.fours).reshape(rows, columns).astype(F32)

    up_grad = all_sum(core_sum(dot(normed_low, inner_low, ((0,), (0,))).astype(BF16)))
    down_grad = all_sum(core_sum(dot(active_low, second_low, ((0,), (0,))).astype(BF16)))
    out_grad = all_sum(core_sum(dot(context_low, branch_low, ((0,), (0,))).astype(BF16)))
    vector_grads = jnp.concatenate(
        [
            jnp.stack([out_bias_grad, gain_one_grad, shift_one_grad, down_bias_grad, gain_two_grad, shift_two_grad]),
            up_bias_grad.reshape(-1, model_width),
        ]
    )
    vector_grads = lax.psum(vector_grads, ("seq", "shard"))
    halves = lax.dynamic_slice_in_dim(vector_grads[:6], core * half, half, 1)
    up_bias_out = lax.dynamic_slice_in_dim(vector_grads[6:].reshape(-1), core * (hidden_width // 2), hidden_width // 2, 0)

    parts = attend_grad(query, context, context_grad, log_total, keys, values, bias, chunks)
    query_grad, key_value_grads = parts[0], parts[1:]
    if plane_size == 4:
        own, one, two, three = key_value_grads
        one_in, two_in, three_in = places.swap(one, 1), places.swap(two, 2), places.swap(three, 3)
        key_value = own.astype(F32) + one_in.astype(F32) + two_in.astype(F32) + three_in.astype(F32)
    else:
        blocks = key_value_grads[0].reshape(2 * GROUP_WIDTH, plane_size, column_rows)
        key_value = places.scatter_sum(jnp.transpose(blocks, (1, 0, 2)), places.planes)
    joined_grad = jnp.concatenate([query_grad, key_value.T.astype(BF16)], axis=1)
    bias_part = jnp.sum(joined_grad.astype(F32), axis=0)
    weight_part = core_sum(dot(column_inputs, joined_grad, ((0,), (0,))).astype(BF16))
    weight_part = four_sum(weight_part.reshape(4, half // 4, -1))
    input_part = dot(joined_grad, group_weight, ((1,), (1,))).astype(BF16)
    input_part = places.scatter_sum(input_part.reshape(GROUPS, row_count, model_width), places.columns)
    input_grad = residual_one_grad + input_part
    weight_whole = places.gather(places.gather(weight_part, places.columns), places.fours)
    weight_whole = weight_whole.reshape(4, GROUPS, half // 4, 3, GROUP_WIDTH)
    qkv_grad = jnp.transpose(weight_whole, (0, 2, 3, 1, 4)).reshape(half, 3 * model_width).astype(F32)
    spread = jnp.zeros((GROUPS, 3 * GROUP_WIDTH), F32)
    spread = lax.dynamic_update_slice_in_dim(spread, bias_part[None], group, 0)
    spread = lax.psum(spread, ("seq", "shard")).reshape(GROUPS, 3, GROUP_WIDTH)
    query_bias_grad = lax.dynamic_slice_in_dim(spread[:, 0].reshape(model_width), core * half, half, 0)
    value_bias_grad = lax.dynamic_slice_in_dim(spread[:, 2].reshape(model_width), core * half, half, 0)

    shape = (1, row_count, model_width)
    return (
        outputs.astype(BF16).reshape(shape),
        input_grad.reshape(shape),
        qkv_grad,
        query_bias_grad,
        value_bias_grad,
        out_grad,
        halves[0],
        halves[1],
        halves[2],
        up_grad,
        up_bias_out,
        down_grad,
        halves[3],
        halves[4],
        halves[5],
    )


def solution(mesh):
    rows, halves, whole = P("shard", "seq", None), P("shard", None), P("shard")
    in_specs = (rows, rows, P(), halves, whole, whole, halves, whole, whole, whole, halves, whole, halves, whole, whole, whole)
    out_specs = (rows, rows, halves, whole, whole, halves, whole, whole, whole, halves, whole, halves, whole, whole, whole)
    return jax.shard_map(body, mesh=mesh, in_specs=in_specs, out_specs=out_specs, check_vma=False)
```

```python
import functools

import jax
import jax.numpy as jnp
from jax import lax
from jax.experimental import pallas as pl
from jax.experimental.pallas import tpu as pltpu
from jax.sharding import PartitionSpec as P

HEADS = 12
HEAD_DIM = 64
GROUPS = 4
GROUP_HEADS = HEADS // GROUPS
WIDTH = GROUP_HEADS * HEAD_DIM
EPSILON = 1e-12
MASKED = -1e30
F32 = jnp.float32
BF16 = jnp.bfloat16
MIB = 2**20
ROWS = 128
TURNED = ((1,), (1,))
FIRST = ((1,), (0,))


def dot(left, right, dims=FIRST):
    return lax.dot_general(left, right, (dims, ((), ())), preferred_element_type=F32)


def kernel_call(kernel, name, outs, args, vmem, micros, smem=0, anywhere=(), scratch=()):
    spaces = [
        pl.BlockSpec(memory_space=pltpu.SMEM if i < smem else pl.ANY if i in anywhere else pltpu.VMEM)
        for i in range(len(args))
    ]
    return pl.pallas_call(
        kernel,
        out_shape=outs,
        in_specs=spaces,
        scratch_shapes=list(scratch),
        compiler_params=pltpu.CompilerParams(vmem_limit_bytes=vmem * MIB),
        cost_estimate=pl.CostEstimate(flops=0, bytes_accessed=int(micros * 3_500_000), transcendentals=0),
        name=name,
    )(*args)


def shaped(shape, dtype=BF16):
    return jax.ShapeDtypeStruct(shape, dtype)


class Places:
    def __init__(self, size):
        self.size = size
        self.plane_size = size // GROUPS
        self.rest = self.plane_size // 4
        index = lambda g, q, m: (g * 4 + q) * self.rest + m
        groups, quarters, members = range(GROUPS), range(4), range(self.rest)
        self.columns = [[index(g, q, m) for g in groups] for q in quarters for m in members]
        self.planes = [[index(g, q, m) for q in quarters for m in members] for g in groups]
        self.fours = [[index(g, q, m) for q in quarters] for g in groups for m in members]
        self.rests = [[index(g, q, m) for m in members] for g in groups for q in quarters]

    def swap(self, block, bits):
        return lax.ppermute(block, "seq", [(i, i ^ bits) for i in range(self.size)])

    def column_swap(self, block, turn):
        return self.swap(block, turn * self.plane_size)

    def four_swap(self, block, turn):
        return self.swap(block, turn * self.rest)

    def exchange(self, blocks, groups):
        return lax.all_to_all(blocks, "seq", 0, 0, axis_index_groups=groups, tiled=True)


def project_kernel(x0, x1, x2, x3, weight, offset, query_ref, key_value_ref):
    for i, x in enumerate((x0, x1, x2, x3)):
        at = slice(i * ROWS, (i + 1) * ROWS)
        joined = (dot(x[...], weight[...]) + offset[...]).astype(BF16)
        query_ref[at, :] = joined[:, :WIDTH] * jnp.asarray(0.125, BF16)
        key_value_ref[at, :] = joined[:, WIDTH:]


def attend_kernel(pieces, chunks, *refs):
    q_ref = refs[0]
    key_value_refs, bias_refs = refs[1 : 1 + pieces], refs[1 + pieces : 1 + 2 * pieces]
    context_ref, log_ref = refs[1 + 2 * pieces : 3 + 2 * pieces]
    low_refs = refs[3 + 2 * pieces :]
    rows = q_ref.shape[0]
    chunk = key_value_refs[0].shape[0] // chunks
    for block in range(rows // ROWS):
        at = slice(block * ROWS, (block + 1) * ROWS)
        for head in range(GROUP_HEADS):
            columns = slice(head * HEAD_DIM, (head + 1) * HEAD_DIM)
            value_columns = slice(WIDTH + head * HEAD_DIM, WIDTH + (head + 1) * HEAD_DIM)
            query = q_ref[at, columns]

            def step(index, state):
                highest, total, mix = state
                here = pl.ds(pl.multiple_of(index * chunk, chunk), chunk)
                scores = [dot(query, k[here, columns], TURNED) + b[:, here] for k, b in zip(key_value_refs, bias_refs)]
                peak = functools.reduce(jnp.maximum, [jnp.max(s, axis=1, keepdims=True) for s in scores])
                raised = jnp.maximum(highest, peak)
                weights = [jnp.exp(s - raised) for s in scores]
                factor = jnp.exp(highest - raised)
                total = total * factor + sum(jnp.sum(w, axis=1, keepdims=True) for w in weights)
                mix = mix * factor + sum(
                    dot(w.astype(BF16), v[here, value_columns]) for w, v in zip(weights, key_value_refs)
                )
                return raised, total, mix

            state = (
                jnp.full((ROWS, 1), MASKED, F32),
                jnp.zeros((ROWS, 1), F32),
                jnp.zeros((ROWS, HEAD_DIM), F32),
            )
            highest, total, mix = step(0, state) if chunks == 1 else lax.fori_loop(0, chunks, step, state)
            context = mix / total
            context_ref[at, columns] = context
            low_refs[block][:, columns] = context.astype(BF16)
            log_ref[at, head : head + 1] = highest + jnp.log(total)


def attend(query, key_values, bias, chunks):
    rows = query.shape[0]
    outs = (shaped((rows, WIDTH), F32), shaped((rows, 128), F32)) + (shaped((ROWS, WIDTH)),) * GROUPS
    kernel = functools.partial(attend_kernel, len(key_values), chunks)
    found = kernel_call(kernel, "attend", outs, (query, *key_values, *bias), 24 if chunks == 1 else 60, 9)
    return found[0], found[1], found[2:]


def attend_grad_kernel(pieces, chunks, *refs):
    q_ref, context_ref, log_ref = refs[:3]
    grad_refs = refs[3:7]
    key_value_refs, bias_refs = refs[7 : 7 + pieces], refs[7 + pieces : 7 + 2 * pieces]
    query_grad_ref = refs[7 + 2 * pieces]
    out_refs = refs[8 + 2 * pieces :]
    rows = q_ref.shape[0]
    chunk = key_value_refs[0].shape[0] // chunks
    for head in range(GROUP_HEADS):
        columns = slice(head * HEAD_DIM, (head + 1) * HEAD_DIM)
        value_columns = slice(WIDTH + head * HEAD_DIM, WIDTH + (head + 1) * HEAD_DIM)
        query = q_ref[:, columns]
        grad = jnp.concatenate([g[:, columns] for g in grad_refs], axis=0)
        correction = jnp.sum(grad.astype(F32) * context_ref[:, columns], axis=1, keepdims=True)
        log_total = log_ref[:, head : head + 1]
        query_turned = query.T
        grad_turned = grad.T

        def step(index, query_grad):
            here = pl.ds(pl.multiple_of(index * chunk, chunk), chunk)
            for both, b, out in zip(key_value_refs, bias_refs, out_refs):
                key = both[here, columns]
                probs = jnp.exp(dot(query, key, TURNED) + b[:, here] - log_total)
                probs_grad = dot(grad, both[here, value_columns], TURNED)
                score_grad = (probs * (probs_grad - correction)).astype(BF16)
                query_grad = query_grad + dot(score_grad, key)
                out[columns, here] = dot(query_turned, score_grad).astype(BF16)
                out[value_columns, here] = dot(grad_turned, probs.astype(BF16)).astype(BF16)
            return query_grad

        total = jnp.zeros((rows, HEAD_DIM), F32)
        total = step(0, total) if chunks == 1 else lax.fori_loop(0, chunks, step, total)
        query_grad_ref[:, columns] = (total * 0.125).astype(BF16)


def attend_grad(query, context, grads, log_total, key_values, bias, chunks):
    rows = query.shape[0]
    outs = (shaped((rows, WIDTH)),) + tuple(shaped((2 * WIDTH, k.shape[0])) for k in key_values)
    kernel = functools.partial(attend_grad_kernel, len(key_values), chunks)
    args = (query, context, log_total, *grads, *key_values, *bias)
    found = kernel_call(kernel, "attend_grad", outs, args, 32 if chunks == 1 else 60, 11)
    return found[0], found[1:]


def normalize(hidden):
    center = hidden - jnp.mean(hidden, axis=1, keepdims=True)
    scale = lax.rsqrt(jnp.mean(center * center, axis=1, keepdims=True) + EPSILON)
    return center * scale, scale


def normalize_grad(grad, normal, scale):
    return scale * (
        grad
        - jnp.mean(grad, axis=1, keepdims=True)
        - normal * jnp.mean(grad * normal, axis=1, keepdims=True)
    )


def column_sum(values):
    return jnp.sum(values, axis=0, keepdims=True)


def dense_kernel(width, spot, c0, c1, c2, c3, x_ref, grad_ref, vectors, up_offset, out_hbm, up_hbm, down_hbm, *rest):
    (layer_ref, one_grad_ref, normed_ref, active_ref, second_ref, inner_ref, branch_ref, sums_ref) = rest[:8]
    context_grads = rest[8:12]
    out_w, up_w, down_w, slope, sems = rest[12:]
    copies = [
        pltpu.make_async_copy(source, target, sems.at[i])
        for i, (source, target) in enumerate(((out_hbm, out_w), (up_hbm, up_w), (down_hbm, down_w)))
    ]
    for copy in copies:
        copy.start()
    hidden = up_w.shape[1]
    half = width // 2
    out_offset, gain_one, shift_one, down_offset, gain_two, shift_two = (vectors[i : i + 1, :] for i in range(2, 8))
    group = spot[0]

    def turned(i):
        return pl.ds(pl.multiple_of((group ^ i) * WIDTH, WIDTH), WIDTH)

    copies[0].wait()
    branch = sum(dot(c[...], out_w[turned(i), :]) for i, c in enumerate((c0, c1, c2, c3))) + out_offset
    normal_one, scale_one = normalize(x_ref[...].astype(F32) + branch)
    normed_low = (normal_one * gain_one + shift_one).astype(BF16)
    normed_ref[...] = normed_low
    copies[1].wait()
    copies[2].wait()
    step = 768
    second = jnp.zeros((ROWS, width), F32) + down_offset
    for start in range(0, hidden, step):
        at = slice(start, start + step)
        inner = dot(normed_low, up_w[:, at]) + up_offset[:, at]
        share = 0.5 + 0.5 * lax.erf(inner * 0.7071067811865476)
        density = 0.3989422804014327 * jnp.exp(-0.5 * inner * inner)
        slope[:, at] = share + inner * density
        active = (inner * share).astype(BF16)
        active_ref[:, at] = active
        second = second + dot(active, down_w[at, :])
    normal_two, scale_two = normalize(normed_low.astype(F32) + second)
    layer_ref[...] = (normal_two * gain_two + shift_two).astype(BF16)
    grad = grad_ref[...].astype(F32)
    gain_two_grad, shift_two_grad = column_sum(grad * normal_two), column_sum(grad)
    two_grad = normalize_grad(grad * gain_two, normal_two, scale_two)
    second_low = two_grad.astype(BF16)
    second_ref[...] = second_low
    down_bias_grad = column_sum(second_low.astype(F32))
    normed_grad = two_grad
    for start in range(0, hidden, step):
        at = slice(start, start + step)
        inner_low = (dot(second_low, down_w[at, :], TURNED) * slope[:, at]).astype(BF16)
        inner_ref[:, at] = inner_low
        up_sum = column_sum(inner_low.astype(F32))
        for piece in range(step // half):
            place = start // half + piece
            per_core = hidden // 2 // half
            sums_ref[place // per_core, 6 + place % per_core : 7 + place % per_core, :] = up_sum[
                :, piece * half : (piece + 1) * half
            ]
        normed_grad = normed_grad + dot(inner_low, up_w[:, at], TURNED)
    gain_one_grad, shift_one_grad = column_sum(normed_grad * normal_one), column_sum(normed_grad)
    one_grad = normalize_grad(normed_grad * gain_one, normal_one, scale_one)
    one_grad_ref[...] = one_grad
    branch_low = one_grad.astype(BF16)
    branch_ref[...] = branch_low
    for i, ref in enumerate(context_grads):
        ref[...] = dot(branch_low, out_w[turned(i), :], TURNED).astype(BF16)
    out_bias_grad = column_sum(branch_low.astype(F32))
    sums = (out_bias_grad, gain_one_grad, shift_one_grad, down_bias_grad, gain_two_grad, shift_two_grad)
    for core in range(2):
        for i, total in enumerate(sums):
            sums_ref[core, i : i + 1, :] = total[:, core * half : (core + 1) * half]
        sums_ref[core, 10:16, :] = jnp.zeros((6, half), F32)


def dense(spot, contexts, inputs, grad, vectors, up_offset, out_matrix, up_matrix, down_matrix):
    width, hidden = up_matrix.shape
    outs = (
        shaped((ROWS, width)),
        shaped((ROWS, width), F32),
        shaped((ROWS, width)),
        shaped((ROWS, hidden)),
        shaped((ROWS, width)),
        shaped((ROWS, hidden)),
        shaped((ROWS, width)),
        shaped((2, 16, width // 2), F32),
    ) + (shaped((ROWS, WIDTH)),) * GROUPS
    scratch = (
        pltpu.VMEM(out_matrix.shape, BF16),
        pltpu.VMEM(up_matrix.shape, BF16),
        pltpu.VMEM(down_matrix.shape, BF16),
        pltpu.VMEM((ROWS, hidden), F32),
        pltpu.SemaphoreType.DMA((3,)),
    )
    args = (spot, *contexts, inputs, grad, vectors, up_offset, out_matrix, up_matrix, down_matrix)
    return kernel_call(
        functools.partial(dense_kernel, width), "dense", outs, args, 40, 18, 1, (9, 10, 11), scratch
    )


def up_grad_kernel(own, spot, normed, inner, *rest):
    received, out_ref, normed_turned = rest if own else (None, *rest)
    normed_turned[...] = normed[...].T
    rows = out_ref.shape[0]
    core = spot[2] if own else 1 - spot[2]
    left = normed_turned[pl.ds(pl.multiple_of(core * rows, rows), rows), :]
    for start in range(0, out_ref.shape[1], 768):
        at = slice(start, start + 768)
        value = dot(left, inner[:, at])
        if own:
            value = value + received[:, at].astype(F32)
        out_ref[:, at] = value.astype(BF16)


def up_grad_part(spot, normed, inner, received=None):
    width, hidden = normed.shape[1], inner.shape[1]
    args = (spot, normed, inner) + (() if received is None else (received,))
    return kernel_call(
        functools.partial(up_grad_kernel, received is not None),
        "up_grad",
        shaped((width // 2, hidden)),
        args,
        16,
        4,
        1,
        (),
        (pltpu.VMEM((width, ROWS), BF16),),
    )


TALL, SHORT, EXTRA = 96, 24, 8


def down_grad_kernel(own, spot, active, second, c0, c1, c2, c3, branch, sums, *rest):
    received, out_ref, active_turned, context_turned = rest if own else (None, *rest)
    active_turned[...] = active[...].T
    group = spot[0]
    for i, c in enumerate((c0, c1, c2, c3)):
        context_turned[pl.ds(pl.multiple_of((group ^ i) * WIDTH, WIDTH), WIDTH), :] = c[...].T
    core = spot[2] if own else 1 - spot[2]
    tall, short = active_turned.shape[0] // 2, context_turned.shape[0] // 2
    context_half = context_turned[pl.ds(pl.multiple_of(core * short, short), short), :]
    totals = sums[core]
    extra = jnp.concatenate([totals[:EXTRA], totals[EXTRA:]], axis=1)
    for quarter in range(4):
        left = active_turned[pl.ds(pl.multiple_of(core * tall + quarter * (tall // 4), 16), tall // 4), :]
        down = dot(left, second[...])
        out = dot(context_half[quarter * (short // 4) : (quarter + 1) * (short // 4), :], branch[...])
        for g in range(GROUPS):
            value = jnp.concatenate(
                [down[g * TALL : (g + 1) * TALL], out[g * SHORT : (g + 1) * SHORT], extra], axis=0
            )
            if own:
                value = value + received[quarter, g].astype(F32)
            out_ref[quarter, g] = value.astype(BF16)


def down_grad_part(spot, active, second, contexts, branch, sums, received=None):
    width, hidden = second.shape[1], active.shape[1]
    args = (spot, active, second, *contexts, branch, sums) + (() if received is None else (received,))
    return kernel_call(
        functools.partial(down_grad_kernel, received is not None),
        "down_grad",
        shaped((4, GROUPS, TALL + SHORT + EXTRA, width)),
        args,
        24,
        5,
        1,
        (),
        (pltpu.VMEM((hidden, ROWS), BF16), pltpu.VMEM((width, ROWS), BF16)),
    )


BIAS_ROWS = 16


def joined_grad_kernel(pieces, spot, query_grad, *rest):
    key_values = rest[:pieces]
    inputs = rest[pieces : pieces + 4]
    weight = rest[pieces + 4]
    other_ref, own_ref = rest[pieces + 5 : pieces + 7]
    input_grads = rest[pieces + 7 : pieces + 11]
    joined, turned = rest[pieces + 11 :]
    total = sum(k[...].astype(F32) for k in key_values)
    joined[:, :WIDTH] = query_grad[...]
    joined[:, WIDTH:] = total.T.astype(BF16)
    for i, ref in enumerate(input_grads):
        ref[...] = dot(joined[i * ROWS : (i + 1) * ROWS, :], weight[...], TURNED).astype(BF16)
    for i, x in enumerate(inputs):
        turned[:, i * ROWS : (i + 1) * ROWS] = x[...].T
    sums = jnp.concatenate(
        [column_sum(joined[...].astype(F32)), jnp.zeros((BIAS_ROWS - 1, 3 * WIDTH), F32)], axis=0
    ).astype(BF16)
    half = turned.shape[0] // 2
    for ref, core in ((other_ref, 1 - spot[2]), (own_ref, spot[2])):
        value = dot(turned[pl.ds(pl.multiple_of(core * half, half), half), :], joined[...]).astype(BF16)
        for quarter in range(4):
            ref[quarter, : half // 4, :] = value[quarter * (half // 4) : (quarter + 1) * (half // 4)]
            ref[quarter, half // 4 :, :] = sums


def joined_grads(spot, query_grad, key_values, inputs, weight):
    width = weight.shape[0]
    part = shaped((4, width // 8 + BIAS_ROWS, 3 * WIDTH))
    outs = (part, part) + (shaped((ROWS, width)),) * GROUPS
    scratch = (pltpu.VMEM((GROUPS * ROWS, 3 * WIDTH), BF16), pltpu.VMEM((width, GROUPS * ROWS), BF16))
    args = (spot, query_grad, *key_values, *inputs, weight)
    kernel = functools.partial(joined_grad_kernel, len(key_values))
    found = kernel_call(kernel, "joined_grad", outs, args, 24, 6, 1, (), scratch)
    return found[0], found[1], found[2:]


def place_down_kernel(spot, p0, p1, p2, p3, down_ref, out_ref):
    group, quarter = spot[0], spot[1]
    for i, piece in enumerate((p0, p1, p2, p3)):
        for g in range(GROUPS):
            block = piece[group ^ g]
            tall = (quarter ^ i) * (GROUPS * TALL) + g * TALL
            down_ref[pl.ds(pl.multiple_of(tall, 8), TALL), :] = block[:TALL].astype(F32)
            short = (quarter ^ i) * (GROUPS * SHORT) + g * SHORT
            out_ref[pl.ds(pl.multiple_of(short, 8), SHORT), :] = block[TALL : TALL + SHORT].astype(F32)


def place_joined_kernel(spot, p0, p1, p2, p3, weight_ref, bias_ref):
    group, quarter, core = spot[0], spot[1], spot[2]
    width = weight_ref.shape[1] // 3
    rows = p0.shape[1] - BIAS_ROWS
    for i, piece in enumerate((p0, p1, p2, p3)):
        blocks = [piece[group ^ g].astype(F32) for g in range(GROUPS)]
        for part in range(3):
            value = jnp.concatenate([b[:, part * WIDTH : (part + 1) * WIDTH] for b in blocks], axis=1)
            at = pl.ds(pl.multiple_of((quarter ^ i) * rows, 16), rows)
            weight_ref[at, part * width : (part + 1) * width] = value[:rows]
            if i == 0:
                line = value[rows : rows + 1]
                bias_ref[part : part + 1, :] = jnp.where(core == 0, line[:, : width // 2], line[:, width // 2 :])


def body(
    tokens,
    cotangent,
    lengths,
    qkv_weight,
    query_bias,
    value_bias,
    out_weight,
    out_bias,
    first_gain,
    first_shift,
    up_weight,
    up_bias,
    down_weight,
    down_bias,
    second_gain,
    second_shift,
):
    row_count, model_width = tokens.shape[1], tokens.shape[2]
    hidden_width = up_weight.shape[1]
    places = Places(lax.axis_size("seq"))
    plane_size, rest = places.plane_size, places.rest
    rank = lax.axis_index("seq")
    core = lax.axis_index("shard")
    group, position = rank // plane_size, rank % plane_size
    quarter = position // rest
    spot = jnp.stack([group, quarter, core]).astype(jnp.int32)
    length = lengths[core]
    inputs = tokens[0]
    column_rows = GROUPS * row_count
    half = model_width // 2
    turns = range(1, GROUPS)

    column_inputs = (inputs, *(places.column_swap(inputs, i) for i in turns))

    def both(block):
        return lax.all_gather(block, "shard", axis=0, tiled=True)

    def own_columns(w):
        at = group * WIDTH
        parts = [lax.dynamic_slice_in_dim(w, at + i * model_width, WIDTH, w.ndim - 1) for i in range(3)]
        return jnp.concatenate(parts, axis=-1)

    group_weight = both(own_columns(qkv_weight))
    vectors = [query_bias, value_bias, out_bias, first_gain, first_shift, down_bias, second_gain, second_shift]
    stacked = jnp.concatenate([jnp.stack(vectors), up_bias.reshape(-1, half)])
    stacked = lax.all_gather(stacked, "shard", axis=0).astype(F32)
    whole = jnp.transpose(stacked[:, : len(vectors)], (1, 0, 2)).reshape(len(vectors), model_width)
    up_offset = stacked[:, len(vectors) :].reshape(1, hidden_width)
    out_matrix = both(out_weight)
    up_matrix = both(up_weight)
    down_matrix = both(down_weight)

    offset = own_columns(jnp.concatenate([whole[0], jnp.zeros_like(whole[0]), whole[1]])).reshape(1, -1)
    query, key_value = kernel_call(
        project_kernel,
        "project",
        (shaped((column_rows, WIDTH)), shaped((column_rows, 2 * WIDTH))),
        (*column_inputs, group_weight, offset),
        16,
        2,
    )

    def masks(who):
        groups = group ^ jnp.arange(GROUPS)
        starts = (groups[None, :] * plane_size + who[:, None]) * row_count
        tokens_at = starts[:, :, None] + jnp.arange(row_count)
        return jnp.where(tokens_at.reshape(1, -1) < length, 0.0, MASKED).astype(F32)

    if plane_size == 4:
        chunks = 1
        key_values = (key_value, *(places.swap(key_value, i) for i in turns))
        bias = tuple(masks((position ^ i)[None]) for i in range(4))
    else:
        chunks = plane_size // 4
        gathered = lax.all_gather(key_value, "seq", axis=0, axis_index_groups=places.planes)
        key_values = (gathered.reshape(-1, 2 * WIDTH),)
        bias = (masks(jnp.arange(plane_size)),)
    context, log_total, context_lows = attend(query, key_values, bias, chunks)
    contexts = (context_lows[0], *(places.column_swap(context_lows[i], i) for i in turns))

    found = dense(spot, contexts, inputs, cotangent[0], whole, up_offset, out_matrix, up_matrix, down_matrix)
    layer_out, one_grad, normed_low, active, second_low, inner_low, branch_low, sums = found[:8]
    context_grads = found[8:]
    context_grads = (context_grads[0], *(places.column_swap(context_grads[i], i) for i in turns))

    def to_other(block):
        return lax.ppermute(block, "shard", [(0, 1), (1, 0)])

    up_part = up_grad_part(spot, normed_low, inner_low, to_other(up_grad_part(spot, normed_low, inner_low)))
    up_grad = lax.psum(up_part, "seq").astype(F32)

    down_args = (spot, active, second_low, contexts, branch_low, sums)
    down_part = down_grad_part(*down_args, to_other(down_grad_part(*down_args)))

    def four_sum(blocks):
        total = jnp.sum(places.exchange(blocks, places.fours).astype(F32), axis=0)
        if rest > 1:
            total = lax.psum(total, "seq", axis_index_groups=places.rests)
        return total.astype(BF16)

    def gather_all(part):
        column = jnp.stack([part, *(places.column_swap(part, i) for i in turns)])
        return (column, *(places.four_swap(column, i) for i in turns))

    down_sum = four_sum(down_part)
    down_sum = jnp.sum(places.exchange(down_sum, places.columns).astype(F32), axis=0)
    down_pieces = gather_all(down_sum.astype(BF16))
    down_grad, out_grad = kernel_call(
        place_down_kernel,
        "place_down",
        (shaped((hidden_width // 2, model_width), F32), shaped((half, model_width), F32)),
        (spot, *down_pieces),
        24,
        5,
        1,
    )
    extra = down_sum[TALL + SHORT :]
    up_bias_grad = jnp.concatenate([extra[6, :half], extra[7, :half], extra[0, half:], extra[1, half:]])

    query_grad, parts = attend_grad(query, context, context_grads, log_total, key_values, bias, chunks)
    if plane_size == 4:
        key_value_grads = (parts[0], *(places.swap(parts[i], i) for i in turns))
    else:
        blocks = parts[0].reshape(2 * WIDTH, plane_size, column_rows)
        blocks = places.exchange(jnp.transpose(blocks, (1, 0, 2)), places.planes)
        key_value_grads = (jnp.sum(blocks.astype(F32), axis=0),)
    other, own, input_parts = joined_grads(spot, query_grad, key_value_grads, column_inputs, group_weight)
    input_parts = (input_parts[0], *(places.column_swap(input_parts[i], i) for i in turns))
    input_grad = one_grad + sum(p.astype(F32) for p in input_parts)
    joined_part = (own.astype(F32) + to_other(other).astype(F32)).astype(BF16)
    joined_pieces = gather_all(four_sum(joined_part))
    qkv_grad, bias_grad = kernel_call(
        place_joined_kernel,
        "place_joined",
        (shaped((half, 3 * model_width), F32), shaped((8, half), F32)),
        (spot, *joined_pieces),
        24,
        5,
        1,
    )

    shape = (1, row_count, model_width)
    return (
        layer_out.reshape(shape),
        input_grad.reshape(shape),
        qkv_grad,
        bias_grad[0],
        bias_grad[2],
        out_grad,
        extra[0, :half],
        extra[1, :half],
        extra[2, :half],
        up_grad,
        up_bias_grad,
        down_grad,
        extra[3, :half],
        extra[4, :half],
        extra[5, :half],
    )


def solution(mesh):
    rows, halves, whole = P("shard", "seq", None), P("shard", None), P("shard")
    in_specs = (rows, rows, P(), halves, whole, whole, halves, whole, whole, whole, halves, whole, halves, whole, whole, whole)
    out_specs = (rows, rows, halves, whole, whole, halves, whole, whole, whole, halves, whole, halves, whole, whole, whole)
    return jax.shard_map(body, mesh=mesh, in_specs=in_specs, out_specs=out_specs, check_vma=False)
```

```python
import functools

import jax
import jax.numpy as jnp
from jax import lax
from jax.experimental import pallas as pl
from jax.experimental.pallas import tpu as pltpu
from jax.sharding import PartitionSpec as P

HEADS = 12
HEAD_DIM = 64
GROUPS = 4
GROUP_HEADS = HEADS // GROUPS
WIDTH = GROUP_HEADS * HEAD_DIM
EPSILON = 1e-12
MASKED = -1e30
F32 = jnp.float32
BF16 = jnp.bfloat16
MIB = 2**20
ROWS = 128
TURNED = ((1,), (1,))
FIRST = ((1,), (0,))


def dot(left, right, dims=FIRST):
    return lax.dot_general(left, right, (dims, ((), ())), preferred_element_type=F32)


def kernel_call(kernel, name, outs, args, vmem, micros, smem=0, anywhere=(), scratch=()):
    spaces = [
        pl.BlockSpec(memory_space=pltpu.SMEM if i < smem else pl.ANY if i in anywhere else pltpu.VMEM)
        for i in range(len(args))
    ]
    return pl.pallas_call(
        kernel,
        out_shape=outs,
        in_specs=spaces,
        scratch_shapes=list(scratch),
        compiler_params=pltpu.CompilerParams(vmem_limit_bytes=vmem * MIB),
        cost_estimate=pl.CostEstimate(flops=0, bytes_accessed=int(micros * 3_500_000), transcendentals=0),
        name=name,
    )(*args)


def shaped(shape, dtype=BF16):
    return jax.ShapeDtypeStruct(shape, dtype)


class Places:
    def __init__(self, size):
        self.size = size
        self.plane_size = size // GROUPS
        self.rest = self.plane_size // 4
        index = lambda g, q, m: (g * 4 + q) * self.rest + m
        groups, quarters, members = range(GROUPS), range(4), range(self.rest)
        self.columns = [[index(g, q, m) for g in groups] for q in quarters for m in members]
        self.planes = [[index(g, q, m) for q in quarters for m in members] for g in groups]
        self.fours = [[index(g, q, m) for q in quarters] for g in groups for m in members]
        self.sixteens = [[index(g, q, m) for g in groups for q in quarters] for m in members]
        self.rests = [[index(g, q, m) for m in members] for g in groups for q in quarters]

    def swap(self, block, bits):
        return lax.ppermute(block, "seq", [(i, i ^ bits) for i in range(self.size)])

    def column_swap(self, block, turn):
        return self.swap(block, turn * self.plane_size)

    def four_swap(self, block, turn):
        return self.swap(block, turn * self.rest)

    def exchange(self, blocks, groups):
        return lax.all_to_all(blocks, "seq", 0, 0, axis_index_groups=groups, tiled=True)


def project_kernel(x0, x1, x2, x3, weight, offset, query_ref, key_value_ref):
    for i, x in enumerate((x0, x1, x2, x3)):
        at = slice(i * ROWS, (i + 1) * ROWS)
        joined = (dot(x[...], weight[...]) + offset[...]).astype(BF16)
        query_ref[at, :] = joined[:, :WIDTH] * jnp.asarray(0.125, BF16)
        key_value_ref[at, :] = joined[:, WIDTH:]


def attend_kernel(pieces, chunks, *refs):
    q_ref = refs[0]
    key_value_refs, bias_refs = refs[1 : 1 + pieces], refs[1 + pieces : 1 + 2 * pieces]
    context_ref, log_ref = refs[1 + 2 * pieces : 3 + 2 * pieces]
    low_refs = refs[3 + 2 * pieces :]
    rows = q_ref.shape[0]
    chunk = key_value_refs[0].shape[0] // chunks
    for block in range(rows // ROWS):
        at = slice(block * ROWS, (block + 1) * ROWS)
        for head in range(GROUP_HEADS):
            columns = slice(head * HEAD_DIM, (head + 1) * HEAD_DIM)
            value_columns = slice(WIDTH + head * HEAD_DIM, WIDTH + (head + 1) * HEAD_DIM)
            query = q_ref[at, columns]

            def step(index, state):
                highest, total, mix = state
                here = pl.ds(pl.multiple_of(index * chunk, chunk), chunk)
                scores = [dot(query, k[here, columns], TURNED) + b[:, here] for k, b in zip(key_value_refs, bias_refs)]
                peak = functools.reduce(jnp.maximum, [jnp.max(s, axis=1, keepdims=True) for s in scores])
                raised = jnp.maximum(highest, peak)
                weights = [jnp.exp(s - raised) for s in scores]
                factor = jnp.exp(highest - raised)
                total = total * factor + sum(jnp.sum(w, axis=1, keepdims=True) for w in weights)
                mix = mix * factor + sum(
                    dot(w.astype(BF16), v[here, value_columns]) for w, v in zip(weights, key_value_refs)
                )
                return raised, total, mix

            state = (
                jnp.full((ROWS, 1), MASKED, F32),
                jnp.zeros((ROWS, 1), F32),
                jnp.zeros((ROWS, HEAD_DIM), F32),
            )
            highest, total, mix = step(0, state) if chunks == 1 else lax.fori_loop(0, chunks, step, state)
            context = mix / total
            context_ref[at, columns] = context
            low_refs[block][:, columns] = context.astype(BF16)
            log_ref[at, head : head + 1] = highest + jnp.log(total)


def attend(query, key_values, bias, chunks):
    rows = query.shape[0]
    outs = (shaped((rows, WIDTH), F32), shaped((rows, 128), F32)) + (shaped((ROWS, WIDTH)),) * GROUPS
    kernel = functools.partial(attend_kernel, len(key_values), chunks)
    found = kernel_call(kernel, "attend", outs, (query, *key_values, *bias), 24 if chunks == 1 else 60, 9)
    return found[0], found[1], found[2:]


def attend_grad_kernel(pieces, chunks, *refs):
    q_ref, context_ref, log_ref = refs[:3]
    grad_refs = refs[3:7]
    key_value_refs, bias_refs = refs[7 : 7 + pieces], refs[7 + pieces : 7 + 2 * pieces]
    query_grad_ref = refs[7 + 2 * pieces]
    out_refs = refs[8 + 2 * pieces :]
    rows = q_ref.shape[0]
    chunk = key_value_refs[0].shape[0] // chunks
    for head in range(GROUP_HEADS):
        columns = slice(head * HEAD_DIM, (head + 1) * HEAD_DIM)
        value_columns = slice(WIDTH + head * HEAD_DIM, WIDTH + (head + 1) * HEAD_DIM)
        query = q_ref[:, columns]
        grad = jnp.concatenate([g[:, columns] for g in grad_refs], axis=0)
        correction = jnp.sum(grad.astype(F32) * context_ref[:, columns], axis=1, keepdims=True)
        log_total = log_ref[:, head : head + 1]
        query_turned = query.T
        grad_turned = grad.T

        def step(index, query_grad):
            here = pl.ds(pl.multiple_of(index * chunk, chunk), chunk)
            for both, b, out in zip(key_value_refs, bias_refs, out_refs):
                key = both[here, columns]
                probs = jnp.exp(dot(query, key, TURNED) + b[:, here] - log_total)
                probs_grad = dot(grad, both[here, value_columns], TURNED)
                score_grad = (probs * (probs_grad - correction)).astype(BF16)
                query_grad = query_grad + dot(score_grad, key)
                out[columns, here] = dot(query_turned, score_grad).astype(BF16)
                out[value_columns, here] = dot(grad_turned, probs.astype(BF16)).astype(BF16)
            return query_grad

        total = jnp.zeros((rows, HEAD_DIM), F32)
        total = step(0, total) if chunks == 1 else lax.fori_loop(0, chunks, step, total)
        query_grad_ref[:, columns] = (total * 0.125).astype(BF16)


def attend_grad(query, context, grads, log_total, key_values, bias, chunks):
    rows = query.shape[0]
    outs = (shaped((rows, WIDTH)),) + tuple(shaped((2 * WIDTH, k.shape[0])) for k in key_values)
    kernel = functools.partial(attend_grad_kernel, len(key_values), chunks)
    args = (query, context, log_total, *grads, *key_values, *bias)
    found = kernel_call(kernel, "attend_grad", outs, args, 32 if chunks == 1 else 60, 11)
    return found[0], found[1:]


def normalize(hidden):
    center = hidden - jnp.mean(hidden, axis=1, keepdims=True)
    scale = lax.rsqrt(jnp.mean(center * center, axis=1, keepdims=True) + EPSILON)
    return center * scale, scale


def normalize_grad(grad, normal, scale):
    return scale * (
        grad
        - jnp.mean(grad, axis=1, keepdims=True)
        - normal * jnp.mean(grad * normal, axis=1, keepdims=True)
    )


def column_sum(values):
    return jnp.sum(values, axis=0, keepdims=True)


TALL, SHORT, EXTRA = 96, 24, 8


def dense_kernel(width, spot, c0, c1, c2, c3, x_ref, grad_ref, vectors, up_offset, out_hbm, up_hbm, down_hbm, *rest):
    layer_ref, one_grad_ref = rest[:2]
    context_grads, up_parts, down_parts = rest[2:6], rest[6:10], rest[10:14]
    out_w, up_w, down_w, slope, active_ref, inner_ref, sums_ref, sems = rest[14:]
    copies = [
        pltpu.make_async_copy(source, target, sems.at[i])
        for i, (source, target) in enumerate(((out_hbm, out_w), (up_hbm, up_w), (down_hbm, down_w)))
    ]
    for copy in copies:
        copy.start()
    hidden = up_w.shape[1]
    half = width // 2
    out_offset, gain_one, shift_one, down_offset, gain_two, shift_two = (vectors[i : i + 1, :] for i in range(2, 8))
    group, quarter = spot[0], spot[1]
    contexts = (c0, c1, c2, c3)

    def turned(i):
        return pl.ds(pl.multiple_of((group ^ i) * WIDTH, WIDTH), WIDTH)

    copies[0].wait()
    branch = sum(dot(c[...], out_w[turned(i), :]) for i, c in enumerate(contexts)) + out_offset
    normal_one, scale_one = normalize(x_ref[...].astype(F32) + branch)
    normed_low = (normal_one * gain_one + shift_one).astype(BF16)
    for ref in up_parts:
        ref[:, :width] = normed_low
    copies[1].wait()
    copies[2].wait()
    step = 768
    second = jnp.zeros((ROWS, width), F32) + down_offset
    for start in range(0, hidden, step):
        at = slice(start, start + step)
        inner = dot(normed_low, up_w[:, at]) + up_offset[:, at]
        share = 0.5 + 0.5 * lax.erf(inner * 0.7071067811865476)
        density = 0.3989422804014327 * jnp.exp(-0.5 * inner * inner)
        slope[:, at] = share + inner * density
        active = (inner * share).astype(BF16)
        active_ref[:, at] = active
        second = second + dot(active, down_w[at, :])
    normal_two, scale_two = normalize(normed_low.astype(F32) + second)
    layer_ref[...] = (normal_two * gain_two + shift_two).astype(BF16)
    grad = grad_ref[...].astype(F32)
    gain_two_grad, shift_two_grad = column_sum(grad * normal_two), column_sum(grad)
    two_grad = normalize_grad(grad * gain_two, normal_two, scale_two)
    second_low = two_grad.astype(BF16)
    down_bias_grad = column_sum(second_low.astype(F32))
    normed_grad = two_grad
    for start in range(0, hidden, step):
        at = slice(start, start + step)
        inner_low = (dot(second_low, down_w[at, :], TURNED) * slope[:, at]).astype(BF16)
        inner_ref[:, at] = inner_low
        up_sum = column_sum(inner_low.astype(F32))
        for piece in range(step // half):
            place = start // half + piece
            per_core = hidden // 2 // half
            row, core = 6 + place % per_core, place // per_core
            sums_ref[row : row + 1, core * half : (core + 1) * half] = up_sum[:, piece * half : (piece + 1) * half]
        normed_grad = normed_grad + dot(inner_low, up_w[:, at], TURNED)
    gain_one_grad, shift_one_grad = column_sum(normed_grad * normal_one), column_sum(normed_grad)
    one_grad = normalize_grad(normed_grad * gain_one, normal_one, scale_one)
    one_grad_ref[...] = one_grad
    branch_low = one_grad.astype(BF16)
    for i, ref in enumerate(context_grads):
        ref[...] = dot(branch_low, out_w[turned(i), :], TURNED).astype(BF16)
    out_bias_grad = column_sum(branch_low.astype(F32))
    sums = (out_bias_grad, gain_one_grad, shift_one_grad, down_bias_grad, gain_two_grad, shift_two_grad)
    for i, total in enumerate(sums):
        sums_ref[i : i + 1, :] = total
    sums_ref[10:16, :] = jnp.zeros((6, width), F32)
    share = hidden // 8
    for i in range(4):
        for core in range(2):
            at = pl.ds(pl.multiple_of(core * (hidden // 2) + (quarter ^ i) * share, share), share)
            to = slice(width + core * share, width + (core + 1) * share)
            up_parts[i][:, to] = inner_ref[:, at]
            down_parts[i][:ROWS, to] = active_ref[:, at]
        down_parts[i][:ROWS, :width] = second_low
        down_parts[i][:ROWS, 2 * width : 3 * width] = branch_low
        down_parts[i][ROWS:, :width] = sums_ref[...].astype(BF16)
    strip = width // 8
    for i, c in enumerate(contexts):
        for g in range(GROUPS):
            @pl.when((group ^ i) == g)
            def _():
                for part in range(2):
                    core, owner = divmod((g * WIDTH + part * strip) // strip, 4)
                    for turn in range(4):
                        @pl.when((quarter ^ turn) == owner)
                        def _():
                            to = 3 * width + core * strip
                            down_parts[turn][:ROWS, to : to + strip] = c[:, part * strip : (part + 1) * strip]


def dense(spot, contexts, inputs, grad, vectors, up_offset, out_matrix, up_matrix, down_matrix):
    width, hidden = up_matrix.shape
    outs = (
        (shaped((ROWS, width)), shaped((ROWS, width), F32))
        + (shaped((ROWS, WIDTH)),) * GROUPS
        + (shaped((ROWS, width + hidden // 4)),) * 4
        + (shaped((ROWS + 16, 3 * width + 256)),) * 4
    )
    scratch = (
        pltpu.VMEM(out_matrix.shape, BF16),
        pltpu.VMEM(up_matrix.shape, BF16),
        pltpu.VMEM(down_matrix.shape, BF16),
        pltpu.VMEM((ROWS, hidden), F32),
        pltpu.VMEM((ROWS, hidden), BF16),
        pltpu.VMEM((ROWS, hidden), BF16),
        pltpu.VMEM((16, width), F32),
        pltpu.SemaphoreType.DMA((3,)),
    )
    args = (spot, *contexts, inputs, grad, vectors, up_offset, out_matrix, up_matrix, down_matrix)
    found = kernel_call(
        functools.partial(dense_kernel, width), "dense", outs, args, 40, 18, 1, (9, 10, 11), scratch
    )
    return found[0], found[1], found[2:6], found[6:10], found[10:14]


def up_grad_kernel(spot, p0, p1, p2, p3, other_ref, own_ref, turned, inner):
    width = turned.shape[0]
    for i, part in enumerate((p0, p1, p2, p3)):
        turned[:, i * ROWS : (i + 1) * ROWS] = part[:, :width].T
        inner[i * ROWS : (i + 1) * ROWS, :] = part[:, width:]
    half = width // 2
    for ref, core in ((other_ref, 1 - spot[2]), (own_ref, spot[2])):
        value = dot(turned[pl.ds(pl.multiple_of(core * half, half), half), :], inner[...]).astype(BF16)
        for g in range(GROUPS):
            ref[g] = value[g * TALL : (g + 1) * TALL]


def up_grad_parts(spot, parts, width):
    tokens, columns = 4 * ROWS, parts[0].shape[1] - width
    out = shaped((GROUPS, TALL, columns))
    scratch = (pltpu.VMEM((width, tokens), BF16), pltpu.VMEM((tokens, columns), BF16))
    return kernel_call(up_grad_kernel, "up_grad", (out, out), (spot, *parts), 16, 4, 1, (), scratch)


def down_grad_kernel(spot, p0, p1, p2, p3, other_ref, own_ref, turned, second, branch, sums):
    parts = (p0, p1, p2, p3)
    width = second.shape[1]
    tall, strip = GROUPS * TALL, GROUPS * SHORT
    for i, part in enumerate(parts):
        rows = slice(i * ROWS, (i + 1) * ROWS)
        turned[: 2 * tall, rows] = part[:ROWS, width : 2 * width].T
        turned[2 * tall : 2 * tall + 256, rows] = part[:ROWS, 3 * width :].T
        second[rows, :] = part[:ROWS, :width]
        branch[rows, :] = part[:ROWS, 2 * width : 3 * width]
    total = sum(part[ROWS:, :width].astype(F32) for part in parts)
    for core in range(2):
        start = core * (width // 2)
        sums[core] = jnp.concatenate(
            [total[:EXTRA, start : start + width // 2], total[EXTRA:, start : start + width // 2]], axis=1
        )
    for ref, core in ((other_ref, 1 - spot[2]), (own_ref, spot[2])):
        down = dot(turned[pl.ds(pl.multiple_of(core * tall, tall), tall), :], second[...])
        out = dot(turned[pl.ds(pl.multiple_of(2 * tall + core * strip, 32), strip), :], branch[...])
        for g in range(GROUPS):
            ref[g] = jnp.concatenate(
                [down[g * TALL : (g + 1) * TALL], out[g * SHORT : (g + 1) * SHORT], sums[core]], axis=0
            ).astype(BF16)


def down_grad_parts(spot, parts, width):
    tokens = 4 * ROWS
    out = shaped((GROUPS, TALL + SHORT + EXTRA, width))
    scratch = (
        pltpu.VMEM((2 * GROUPS * TALL + 256, tokens), BF16),
        pltpu.VMEM((tokens, width), BF16),
        pltpu.VMEM((tokens, width), BF16),
        pltpu.VMEM((2, EXTRA, width), F32),
    )
    return kernel_call(down_grad_kernel, "down_grad", (out, out), (spot, *parts), 24, 5, 1, (), scratch)


def core_sum_kernel(which, spot, own, received, *outs):
    at = spot[which]
    for i, out in enumerate(outs):
        out[...] = (own[at ^ i].astype(F32) + received[at ^ i].astype(F32)).astype(BF16)


def core_sums(spot, own, received, which, name):
    outs = (shaped(own.shape[1:]),) * 4
    return kernel_call(functools.partial(core_sum_kernel, which), name, outs, (spot, own, received), 16, 2, 1)


def place_up_kernel(gathered, up_ref):
    share = gathered.shape[3] // 2
    for g in range(GROUPS):
        for quarter in range(4):
            block = gathered[g, quarter].astype(F32)
            for core in range(2):
                start = core * 4 * share + quarter * share
                up_ref[g * TALL : (g + 1) * TALL, start : start + share] = block[:, core * share : (core + 1) * share]


BIAS_ROWS = 16


def joined_grad_kernel(pieces, spot, query_grad, *rest):
    key_values = rest[:pieces]
    inputs = rest[pieces : pieces + 4]
    weight = rest[pieces + 4]
    other_ref, own_ref = rest[pieces + 5 : pieces + 7]
    input_grads = rest[pieces + 7 : pieces + 11]
    joined, turned = rest[pieces + 11 :]
    total = sum(k[...].astype(F32) for k in key_values)
    joined[:, :WIDTH] = query_grad[...]
    joined[:, WIDTH:] = total.T.astype(BF16)
    for i, ref in enumerate(input_grads):
        ref[...] = dot(joined[i * ROWS : (i + 1) * ROWS, :], weight[...], TURNED).astype(BF16)
    for i, x in enumerate(inputs):
        turned[:, i * ROWS : (i + 1) * ROWS] = x[...].T
    sums = jnp.concatenate(
        [column_sum(joined[...].astype(F32)), jnp.zeros((BIAS_ROWS - 1, 3 * WIDTH), F32)], axis=0
    ).astype(BF16)
    half = turned.shape[0] // 2
    for ref, core in ((other_ref, 1 - spot[2]), (own_ref, spot[2])):
        value = dot(turned[pl.ds(pl.multiple_of(core * half, half), half), :], joined[...]).astype(BF16)
        for quarter in range(4):
            ref[quarter, : half // 4, :] = value[quarter * (half // 4) : (quarter + 1) * (half // 4)]
            ref[quarter, half // 4 :, :] = sums


def joined_grads(spot, query_grad, key_values, inputs, weight):
    width = weight.shape[0]
    part = shaped((4, width // 8 + BIAS_ROWS, 3 * WIDTH))
    outs = (part, part) + (shaped((ROWS, width)),) * GROUPS
    scratch = (pltpu.VMEM((GROUPS * ROWS, 3 * WIDTH), BF16), pltpu.VMEM((width, GROUPS * ROWS), BF16))
    args = (spot, query_grad, *key_values, *inputs, weight)
    kernel = functools.partial(joined_grad_kernel, len(key_values))
    found = kernel_call(kernel, "joined_grad", outs, args, 24, 6, 1, (), scratch)
    return found[0], found[1], found[2:]


def place_down_kernel(spot, p0, p1, p2, p3, down_ref, out_ref):
    group, quarter = spot[0], spot[1]
    for i, piece in enumerate((p0, p1, p2, p3)):
        for g in range(GROUPS):
            block = piece[group ^ g]
            tall = (quarter ^ i) * (GROUPS * TALL) + g * TALL
            down_ref[pl.ds(pl.multiple_of(tall, 8), TALL), :] = block[:TALL].astype(F32)
            short = (quarter ^ i) * (GROUPS * SHORT) + g * SHORT
            out_ref[pl.ds(pl.multiple_of(short, 8), SHORT), :] = block[TALL : TALL + SHORT].astype(F32)


def place_joined_kernel(spot, p0, p1, p2, p3, weight_ref, bias_ref):
    group, quarter, core = spot[0], spot[1], spot[2]
    width = weight_ref.shape[1] // 3
    rows = p0.shape[1] - BIAS_ROWS
    for i, piece in enumerate((p0, p1, p2, p3)):
        blocks = [piece[group ^ g].astype(F32) for g in range(GROUPS)]
        for part in range(3):
            value = jnp.concatenate([b[:, part * WIDTH : (part + 1) * WIDTH] for b in blocks], axis=1)
            at = pl.ds(pl.multiple_of((quarter ^ i) * rows, 16), rows)
            weight_ref[at, part * width : (part + 1) * width] = value[:rows]
            if i == 0:
                line = value[rows : rows + 1]
                bias_ref[part : part + 1, :] = jnp.where(core == 0, line[:, : width // 2], line[:, width // 2 :])


def body(
    tokens,
    cotangent,
    lengths,
    qkv_weight,
    query_bias,
    value_bias,
    out_weight,
    out_bias,
    first_gain,
    first_shift,
    up_weight,
    up_bias,
    down_weight,
    down_bias,
    second_gain,
    second_shift,
):
    row_count, model_width = tokens.shape[1], tokens.shape[2]
    hidden_width = up_weight.shape[1]
    places = Places(lax.axis_size("seq"))
    plane_size, rest = places.plane_size, places.rest
    rank = lax.axis_index("seq")
    core = lax.axis_index("shard")
    group, position = rank // plane_size, rank % plane_size
    quarter = position // rest
    spot = jnp.stack([group, quarter, core]).astype(jnp.int32)
    length = lengths[core]
    inputs = tokens[0]
    column_rows = GROUPS * row_count
    half = model_width // 2
    turns = range(1, GROUPS)

    column_inputs = (inputs, *(places.column_swap(inputs, i) for i in turns))

    def both(block):
        return lax.all_gather(block, "shard", axis=0, tiled=True)

    def own_columns(w):
        at = group * WIDTH
        parts = [lax.dynamic_slice_in_dim(w, at + i * model_width, WIDTH, w.ndim - 1) for i in range(3)]
        return jnp.concatenate(parts, axis=-1)

    group_weight = both(own_columns(qkv_weight))
    vectors = [query_bias, value_bias, out_bias, first_gain, first_shift, down_bias, second_gain, second_shift]
    stacked = jnp.concatenate([jnp.stack(vectors), up_bias.reshape(-1, half)])
    stacked = lax.all_gather(stacked, "shard", axis=0).astype(F32)
    whole = jnp.transpose(stacked[:, : len(vectors)], (1, 0, 2)).reshape(len(vectors), model_width)
    up_offset = stacked[:, len(vectors) :].reshape(1, hidden_width)
    out_matrix = both(out_weight)
    up_matrix = both(up_weight)
    down_matrix = both(down_weight)

    offset = own_columns(jnp.concatenate([whole[0], jnp.zeros_like(whole[0]), whole[1]])).reshape(1, -1)
    query, key_value = kernel_call(
        project_kernel,
        "project",
        (shaped((column_rows, WIDTH)), shaped((column_rows, 2 * WIDTH))),
        (*column_inputs, group_weight, offset),
        16,
        2,
    )

    def masks(who):
        groups = group ^ jnp.arange(GROUPS)
        starts = (groups[None, :] * plane_size + who[:, None]) * row_count
        tokens_at = starts[:, :, None] + jnp.arange(row_count)
        return jnp.where(tokens_at.reshape(1, -1) < length, 0.0, MASKED).astype(F32)

    if plane_size == 4:
        chunks = 1
        key_values = (key_value, *(places.swap(key_value, i) for i in turns))
        bias = tuple(masks((position ^ i)[None]) for i in range(4))
    else:
        chunks = plane_size // 4
        gathered = lax.all_gather(key_value, "seq", axis=0, axis_index_groups=places.planes)
        key_values = (gathered.reshape(-1, 2 * WIDTH),)
        bias = (masks(jnp.arange(plane_size)),)
    context, log_total, context_lows = attend(query, key_values, bias, chunks)
    contexts = (context_lows[0], *(places.column_swap(context_lows[i], i) for i in turns))

    layer_out, one_grad, context_grads, up_parts, down_parts = dense(
        spot, contexts, inputs, cotangent[0], whole, up_offset, out_matrix, up_matrix, down_matrix
    )
    context_grads = (context_grads[0], *(places.column_swap(context_grads[i], i) for i in turns))
    up_parts = (up_parts[0], *(places.four_swap(up_parts[i], i) for i in turns))
    down_parts = (down_parts[0], *(places.four_swap(down_parts[i], i) for i in turns))

    def to_other(block):
        return lax.ppermute(block, "shard", [(0, 1), (1, 0)])

    def total_of(pieces, swap):
        received = [swap(pieces[i], i) for i in turns]
        total = pieces[0].astype(F32) + sum(r.astype(F32) for r in received)
        return lax.psum(total, "seq", axis_index_groups=places.rests) if rest > 1 else total

    def gather_all(part):
        column = jnp.stack([part, *(places.column_swap(part, i) for i in turns)])
        return (column, *(places.four_swap(column, i) for i in turns))

    other, own = up_grad_parts(spot, up_parts, model_width)
    up_pieces = core_sums(spot, own, to_other(other), 0, "up_sum")
    up_part = total_of(up_pieces, places.column_swap).astype(BF16)
    other, own = down_grad_parts(spot, down_parts, model_width)
    down_pieces = core_sums(spot, own, to_other(other), 0, "down_sum")
    down_part = total_of(down_pieces, places.column_swap)
    extra = down_part[TALL + SHORT :]
    up_bias_grad = jnp.concatenate([extra[6, :half], extra[7, :half], extra[0, half:], extra[1, half:]])

    query_grad, parts = attend_grad(query, context, context_grads, log_total, key_values, bias, chunks)
    if plane_size == 4:
        key_value_grads = (parts[0], *(places.swap(parts[i], i) for i in turns))
    else:
        blocks = parts[0].reshape(2 * WIDTH, plane_size, column_rows)
        blocks = places.exchange(jnp.transpose(blocks, (1, 0, 2)), places.planes)
        key_value_grads = (jnp.sum(blocks.astype(F32), axis=0),)
    other, own, input_parts = joined_grads(spot, query_grad, key_value_grads, column_inputs, group_weight)
    input_parts = (input_parts[0], *(places.column_swap(input_parts[i], i) for i in turns))
    input_grad = one_grad + sum(p.astype(F32) for p in input_parts)
    joined_pieces = core_sums(spot, own, to_other(other), 1, "joined_sum")
    joined_part = total_of(joined_pieces, places.four_swap).astype(BF16)
    up_all = lax.all_gather(up_part, "seq", axis=0, axis_index_groups=places.sixteens)
    down_all = gather_all(down_part.astype(BF16))
    joined_all = gather_all(joined_part)
    down_grad, out_grad = kernel_call(
        place_down_kernel,
        "place_down",
        (shaped((hidden_width // 2, model_width), F32), shaped((half, model_width), F32)),
        (spot, *down_all),
        24,
        5,
        1,
    )
    qkv_grad, bias_grad = kernel_call(
        place_joined_kernel,
        "place_joined",
        (shaped((half, 3 * model_width), F32), shaped((8, half), F32)),
        (spot, *joined_all),
        24,
        5,
        1,
    )
    up_grad = kernel_call(
        place_up_kernel,
        "place_up",
        shaped((half, hidden_width), F32),
        (up_all.reshape(GROUPS, 4, TALL, hidden_width // 4),),
        24,
        4,
    )

    shape = (1, row_count, model_width)
    return (
        layer_out.reshape(shape),
        input_grad.reshape(shape),
        qkv_grad,
        bias_grad[0],
        bias_grad[2],
        out_grad,
        extra[0, :half],
        extra[1, :half],
        extra[2, :half],
        up_grad,
        up_bias_grad,
        down_grad,
        extra[3, :half],
        extra[4, :half],
        extra[5, :half],
    )


def solution(mesh):
    rows, halves, whole = P("shard", "seq", None), P("shard", None), P("shard")
    in_specs = (rows, rows, P(), halves, whole, whole, halves, whole, whole, whole, halves, whole, halves, whole, whole, whole)
    out_specs = (rows, rows, halves, whole, whole, halves, whole, whole, whole, halves, whole, halves, whole, whole, whole)
    return jax.shard_map(body, mesh=mesh, in_specs=in_specs, out_specs=out_specs, check_vma=False)
```

```python
import functools

import jax
import jax.numpy as jnp
from jax import lax
from jax.experimental import pallas as pl
from jax.experimental.pallas import tpu as pltpu
from jax.sharding import PartitionSpec as P

HEADS = 12
HEAD_DIM = 64
GROUPS = 4
GROUP_HEADS = HEADS // GROUPS
WIDTH = GROUP_HEADS * HEAD_DIM
EPSILON = 1e-12
MASKED = -1e30
F32 = jnp.float32
BF16 = jnp.bfloat16
MIB = 2**20
ROWS = 128
TURNED = ((1,), (1,))
FIRST = ((1,), (0,))


def dot(left, right, dims=FIRST):
    return lax.dot_general(left, right, (dims, ((), ())), preferred_element_type=F32)


def kernel_call(kernel, name, outs, args, vmem, micros, smem=0, left=(), scratch=(), after=()):
    spaces = [
        pl.BlockSpec(memory_space=pltpu.SMEM if i < smem else pltpu.HBM if i in left else pltpu.VMEM)
        for i in range(len(args))
    ]
    count = len(args)

    def run(*refs):
        kernel(*refs[:count], *refs[count + len(after) :])

    return pl.pallas_call(
        run if after else kernel,
        out_shape=outs,
        in_specs=spaces + [pl.BlockSpec(memory_space=pl.ANY)] * len(after),
        scratch_shapes=list(scratch),
        compiler_params=pltpu.CompilerParams(vmem_limit_bytes=vmem * MIB),
        cost_estimate=pl.CostEstimate(flops=0, bytes_accessed=int(micros * 3_500_000), transcendentals=0),
        name=name,
    )(*args, *after)


def shaped(shape, dtype=BF16):
    return jax.ShapeDtypeStruct(shape, dtype)


class Places:
    def __init__(self, size):
        self.size = size
        self.plane_size = size // GROUPS
        self.rest = self.plane_size // 4
        index = lambda g, q, m: (g * 4 + q) * self.rest + m
        groups, quarters, members = range(GROUPS), range(4), range(self.rest)
        self.columns = [[index(g, q, m) for g in groups] for q in quarters for m in members]
        self.planes = [[index(g, q, m) for q in quarters for m in members] for g in groups]
        self.fours = [[index(g, q, m) for q in quarters] for g in groups for m in members]
        self.sixteens = [[index(g, q, m) for g in groups for q in quarters] for m in members]
        self.rests = [[index(g, q, m) for m in members] for g in groups for q in quarters]

    def swap(self, block, bits):
        return lax.ppermute(block, "seq", [(i, i ^ bits) for i in range(self.size)])

    def column_swap(self, block, turn):
        return self.swap(block, turn * self.plane_size)

    def four_swap(self, block, turn):
        return self.swap(block, turn * self.rest)

    def exchange(self, blocks, groups):
        return lax.all_to_all(blocks, "seq", 0, 0, axis_index_groups=groups, tiled=True)


def project_kernel(x0, x1, x2, x3, weight, offset, query_ref, key_value_ref):
    for i, x in enumerate((x0, x1, x2, x3)):
        at = slice(i * ROWS, (i + 1) * ROWS)
        joined = (dot(x[...], weight[...]) + offset[...]).astype(BF16)
        query_ref[at, :] = joined[:, :WIDTH] * jnp.asarray(0.125, BF16)
        key_value_ref[at, :] = joined[:, WIDTH:]


def attend_kernel(pieces, chunks, *refs):
    q_ref = refs[0]
    key_value_refs, bias_refs = refs[1 : 1 + pieces], refs[1 + pieces : 1 + 2 * pieces]
    context_ref, log_ref = refs[1 + 2 * pieces : 3 + 2 * pieces]
    low_refs = refs[3 + 2 * pieces :]
    rows = q_ref.shape[0]
    chunk = key_value_refs[0].shape[0] // chunks
    for block in range(rows // ROWS):
        at = slice(block * ROWS, (block + 1) * ROWS)
        for head in range(GROUP_HEADS):
            columns = slice(head * HEAD_DIM, (head + 1) * HEAD_DIM)
            value_columns = slice(WIDTH + head * HEAD_DIM, WIDTH + (head + 1) * HEAD_DIM)
            query = q_ref[at, columns]

            def step(index, state):
                highest, total, mix = state
                here = pl.ds(pl.multiple_of(index * chunk, chunk), chunk)
                scores = [dot(query, k[here, columns], TURNED) + b[:, here] for k, b in zip(key_value_refs, bias_refs)]
                peak = functools.reduce(jnp.maximum, [jnp.max(s, axis=1, keepdims=True) for s in scores])
                raised = jnp.maximum(highest, peak)
                weights = [jnp.exp(s - raised) for s in scores]
                factor = jnp.exp(highest - raised)
                total = total * factor + sum(jnp.sum(w, axis=1, keepdims=True) for w in weights)
                mix = mix * factor + sum(
                    dot(w.astype(BF16), v[here, value_columns]) for w, v in zip(weights, key_value_refs)
                )
                return raised, total, mix

            state = (
                jnp.full((ROWS, 1), MASKED, F32),
                jnp.zeros((ROWS, 1), F32),
                jnp.zeros((ROWS, HEAD_DIM), F32),
            )
            highest, total, mix = step(0, state) if chunks == 1 else lax.fori_loop(0, chunks, step, state)
            context = mix / total
            context_ref[at, columns] = context
            low_refs[block][:, columns] = context.astype(BF16)
            log_ref[at, head : head + 1] = highest + jnp.log(total)


def attend(query, key_values, bias, chunks):
    rows = query.shape[0]
    outs = (shaped((rows, WIDTH), F32), shaped((rows, 128), F32)) + (shaped((ROWS, WIDTH)),) * GROUPS
    kernel = functools.partial(attend_kernel, len(key_values), chunks)
    found = kernel_call(kernel, "attend", outs, (query, *key_values, *bias), 24 if chunks == 1 else 60, 9)
    return found[0], found[1], found[2:]


def attend_grad_kernel(pieces, chunks, *refs):
    q_ref, context_ref, log_ref = refs[:3]
    grad_refs = refs[3:7]
    key_value_refs, bias_refs = refs[7 : 7 + pieces], refs[7 + pieces : 7 + 2 * pieces]
    query_grad_ref = refs[7 + 2 * pieces]
    out_refs = refs[8 + 2 * pieces :]
    rows = q_ref.shape[0]
    chunk = key_value_refs[0].shape[0] // chunks
    for head in range(GROUP_HEADS):
        columns = slice(head * HEAD_DIM, (head + 1) * HEAD_DIM)
        value_columns = slice(WIDTH + head * HEAD_DIM, WIDTH + (head + 1) * HEAD_DIM)
        query = q_ref[:, columns]
        grad = jnp.concatenate([g[:, columns] for g in grad_refs], axis=0)
        correction = jnp.sum(grad.astype(F32) * context_ref[:, columns], axis=1, keepdims=True)
        log_total = log_ref[:, head : head + 1]
        query_turned = query.T
        grad_turned = grad.T

        def step(index, query_grad):
            here = pl.ds(pl.multiple_of(index * chunk, chunk), chunk)
            for both, b, out in zip(key_value_refs, bias_refs, out_refs):
                key = both[here, columns]
                probs = jnp.exp(dot(query, key, TURNED) + b[:, here] - log_total)
                probs_grad = dot(grad, both[here, value_columns], TURNED)
                score_grad = (probs * (probs_grad - correction)).astype(BF16)
                query_grad = query_grad + dot(score_grad, key)
                out[columns, here] = dot(query_turned, score_grad).astype(BF16)
                out[value_columns, here] = dot(grad_turned, probs.astype(BF16)).astype(BF16)
            return query_grad

        total = jnp.zeros((rows, HEAD_DIM), F32)
        total = step(0, total) if chunks == 1 else lax.fori_loop(0, chunks, step, total)
        query_grad_ref[:, columns] = (total * 0.125).astype(BF16)


def attend_grad(query, context, grads, log_total, key_values, bias, chunks):
    rows = query.shape[0]
    outs = (shaped((rows, WIDTH)),) + tuple(shaped((2 * WIDTH, k.shape[0])) for k in key_values)
    kernel = functools.partial(attend_grad_kernel, len(key_values), chunks)
    args = (query, context, log_total, *grads, *key_values, *bias)
    found = kernel_call(kernel, "attend_grad", outs, args, 32 if chunks == 1 else 60, 11)
    return found[0], found[1:]


def normalize(hidden):
    center = hidden - jnp.mean(hidden, axis=1, keepdims=True)
    scale = lax.rsqrt(jnp.mean(center * center, axis=1, keepdims=True) + EPSILON)
    return center * scale, scale


def normalize_grad(grad, normal, scale):
    return scale * (
        grad
        - jnp.mean(grad, axis=1, keepdims=True)
        - normal * jnp.mean(grad * normal, axis=1, keepdims=True)
    )


def column_sum(values):
    return jnp.sum(values, axis=0, keepdims=True)


TALL, SHORT, EXTRA = 96, 24, 8


def dense_kernel(width, spot, c0, c1, c2, c3, x_ref, grad_ref, vectors, up_offset, out_hbm, up_hbm, down_hbm, *rest):
    layer_ref, one_grad_ref = rest[:2]
    context_grads, up_parts, down_parts = rest[2:6], rest[6:10], rest[10:14]
    out_w, up_w, down_w, slope, active_ref, inner_ref, sums_ref, sems = rest[14:]
    copies = [
        pltpu.make_async_copy(source, target, sems.at[i])
        for i, (source, target) in enumerate(((out_hbm, out_w), (up_hbm, up_w), (down_hbm, down_w)))
    ]
    for copy in copies:
        copy.start()
    hidden = up_w.shape[1]
    half = width // 2
    out_offset, gain_one, shift_one, down_offset, gain_two, shift_two = (vectors[i : i + 1, :] for i in range(2, 8))
    group, quarter = spot[0], spot[1]
    contexts = (c0, c1, c2, c3)

    def turned(i):
        return pl.ds(pl.multiple_of((group ^ i) * WIDTH, WIDTH), WIDTH)

    copies[0].wait()
    branch = sum(dot(c[...], out_w[turned(i), :]) for i, c in enumerate(contexts)) + out_offset
    normal_one, scale_one = normalize(x_ref[...].astype(F32) + branch)
    normed_low = (normal_one * gain_one + shift_one).astype(BF16)
    for ref in up_parts:
        ref[:, :width] = normed_low
    copies[1].wait()
    copies[2].wait()
    step = 768
    second = jnp.zeros((ROWS, width), F32) + down_offset
    for start in range(0, hidden, step):
        at = slice(start, start + step)
        inner = dot(normed_low, up_w[:, at]) + up_offset[:, at]
        share = 0.5 + 0.5 * lax.erf(inner * 0.7071067811865476)
        density = 0.3989422804014327 * jnp.exp(-0.5 * inner * inner)
        slope[:, at] = share + inner * density
        active = (inner * share).astype(BF16)
        active_ref[:, at] = active
        second = second + dot(active, down_w[at, :])
    normal_two, scale_two = normalize(normed_low.astype(F32) + second)
    layer_ref[...] = (normal_two * gain_two + shift_two).astype(BF16)
    grad = grad_ref[...].astype(F32)
    gain_two_grad, shift_two_grad = column_sum(grad * normal_two), column_sum(grad)
    two_grad = normalize_grad(grad * gain_two, normal_two, scale_two)
    second_low = two_grad.astype(BF16)
    down_bias_grad = column_sum(second_low.astype(F32))
    normed_grad = two_grad
    for start in range(0, hidden, step):
        at = slice(start, start + step)
        inner_low = (dot(second_low, down_w[at, :], TURNED) * slope[:, at]).astype(BF16)
        inner_ref[:, at] = inner_low
        up_sum = column_sum(inner_low.astype(F32))
        for piece in range(step // half):
            place = start // half + piece
            per_core = hidden // 2 // half
            row, core = 6 + place % per_core, place // per_core
            sums_ref[row : row + 1, core * half : (core + 1) * half] = up_sum[:, piece * half : (piece + 1) * half]
        normed_grad = normed_grad + dot(inner_low, up_w[:, at], TURNED)
    gain_one_grad, shift_one_grad = column_sum(normed_grad * normal_one), column_sum(normed_grad)
    one_grad = normalize_grad(normed_grad * gain_one, normal_one, scale_one)
    one_grad_ref[...] = one_grad
    branch_low = one_grad.astype(BF16)
    for i, ref in enumerate(context_grads):
        ref[...] = dot(branch_low, out_w[turned(i), :], TURNED).astype(BF16)
    out_bias_grad = column_sum(branch_low.astype(F32))
    sums = (out_bias_grad, gain_one_grad, shift_one_grad, down_bias_grad, gain_two_grad, shift_two_grad)
    for i, total in enumerate(sums):
        sums_ref[i : i + 1, :] = total
    sums_ref[10:16, :] = jnp.zeros((6, width), F32)
    share = hidden // 8
    for i in range(4):
        for core in range(2):
            at = pl.ds(pl.multiple_of(core * (hidden // 2) + (quarter ^ i) * share, share), share)
            to = slice(width + core * share, width + (core + 1) * share)
            up_parts[i][:, to] = inner_ref[:, at]
            down_parts[i][:ROWS, to] = active_ref[:, at]
        down_parts[i][:ROWS, :width] = second_low
        down_parts[i][:ROWS, 2 * width : 3 * width] = branch_low
        down_parts[i][ROWS:, :width] = sums_ref[...].astype(BF16)
    strip = width // 8
    for i, c in enumerate(contexts):
        for g in range(GROUPS):
            @pl.when((group ^ i) == g)
            def _():
                for part in range(2):
                    core, owner = divmod((g * WIDTH + part * strip) // strip, 4)
                    for turn in range(4):
                        @pl.when((quarter ^ turn) == owner)
                        def _():
                            to = 3 * width + core * strip
                            down_parts[turn][:ROWS, to : to + strip] = c[:, part * strip : (part + 1) * strip]


def dense(spot, contexts, inputs, grad, vectors, up_offset, out_matrix, up_matrix, down_matrix):
    width, hidden = up_matrix.shape
    outs = (
        (shaped((ROWS, width)), shaped((ROWS, width), F32))
        + (shaped((ROWS, WIDTH)),) * GROUPS
        + (shaped((ROWS, width + hidden // 4)),) * 4
        + (shaped((ROWS + 16, 3 * width + 256)),) * 4
    )
    scratch = (
        pltpu.VMEM(out_matrix.shape, BF16),
        pltpu.VMEM(up_matrix.shape, BF16),
        pltpu.VMEM(down_matrix.shape, BF16),
        pltpu.VMEM((ROWS, hidden), F32),
        pltpu.VMEM((ROWS, hidden), BF16),
        pltpu.VMEM((ROWS, hidden), BF16),
        pltpu.VMEM((16, width), F32),
        pltpu.SemaphoreType.DMA((3,)),
    )
    args = (spot, *contexts, inputs, grad, vectors, up_offset, out_matrix, up_matrix, down_matrix)
    found = kernel_call(
        functools.partial(dense_kernel, width), "dense", outs, args, 22, 10, 1, (9, 10, 11), scratch
    )
    return found[0], found[1], found[2:6], found[6:10], found[10:14]


def up_grad_kernel(spot, p0, p1, p2, p3, other_ref, own_ref, turned, inner):
    width = turned.shape[0]
    for i, part in enumerate((p0, p1, p2, p3)):
        turned[:, i * ROWS : (i + 1) * ROWS] = part[:, :width].T
        inner[i * ROWS : (i + 1) * ROWS, :] = part[:, width:]
    half = width // 2
    for ref, core in ((other_ref, 1 - spot[2]), (own_ref, spot[2])):
        value = dot(turned[pl.ds(pl.multiple_of(core * half, half), half), :], inner[...]).astype(BF16)
        for g in range(GROUPS):
            ref[g] = value[g * TALL : (g + 1) * TALL]


def up_grad_parts(spot, parts, width, after):
    tokens, columns = 4 * ROWS, parts[0].shape[1] - width
    out = shaped((GROUPS, TALL, columns))
    scratch = (pltpu.VMEM((width, tokens), BF16), pltpu.VMEM((tokens, columns), BF16))
    return kernel_call(up_grad_kernel, "up_grad", (out, out), (spot, *parts), 16, 4, 1, (), scratch, after)


def down_grad_kernel(spot, p0, p1, p2, p3, other_ref, own_ref, turned, second, branch, sums):
    parts = (p0, p1, p2, p3)
    width = second.shape[1]
    tall, strip = GROUPS * TALL, GROUPS * SHORT
    for i, part in enumerate(parts):
        rows = slice(i * ROWS, (i + 1) * ROWS)
        turned[: 2 * tall, rows] = part[:ROWS, width : 2 * width].T
        turned[2 * tall : 2 * tall + 256, rows] = part[:ROWS, 3 * width :].T
        second[rows, :] = part[:ROWS, :width]
        branch[rows, :] = part[:ROWS, 2 * width : 3 * width]
    total = sum(part[ROWS:, :width].astype(F32) for part in parts)
    for core in range(2):
        start = core * (width // 2)
        sums[core] = jnp.concatenate(
            [total[:EXTRA, start : start + width // 2], total[EXTRA:, start : start + width // 2]], axis=1
        )
    for ref, core in ((other_ref, 1 - spot[2]), (own_ref, spot[2])):
        down = dot(turned[pl.ds(pl.multiple_of(core * tall, tall), tall), :], second[...])
        out = dot(turned[pl.ds(pl.multiple_of(2 * tall + core * strip, 32), strip), :], branch[...])
        for g in range(GROUPS):
            ref[g] = jnp.concatenate(
                [down[g * TALL : (g + 1) * TALL], out[g * SHORT : (g + 1) * SHORT], sums[core]], axis=0
            ).astype(BF16)


def down_grad_parts(spot, parts, width, after):
    tokens = 4 * ROWS
    out = shaped((GROUPS, TALL + SHORT + EXTRA, width))
    scratch = (
        pltpu.VMEM((2 * GROUPS * TALL + 256, tokens), BF16),
        pltpu.VMEM((tokens, width), BF16),
        pltpu.VMEM((tokens, width), BF16),
        pltpu.VMEM((2, EXTRA, width), F32),
    )
    return kernel_call(down_grad_kernel, "down_grad", (out, out), (spot, *parts), 16, 5, 1, (), scratch, after)


def core_sum_kernel(which, spot, own, received, *outs):
    at = spot[which]
    for i, out in enumerate(outs):
        out[...] = (own[at ^ i].astype(F32) + received[at ^ i].astype(F32)).astype(BF16)


def core_sums(spot, own, received, which, name):
    outs = (shaped(own.shape[1:]),) * 4
    return kernel_call(functools.partial(core_sum_kernel, which), name, outs, (spot, own, received), 16, 2, 1)


def place_up_kernel(spot, p0, p1, p2, p3, up_ref):
    group, quarter = spot[0], spot[1]
    share = p0.shape[2] // 2
    for i, piece in enumerate((p0, p1, p2, p3)):
        for g in range(GROUPS):
            block = piece[group ^ g].astype(F32)
            for core in range(2):
                start = core * 4 * share + (quarter ^ i) * share
                at = pl.ds(pl.multiple_of(start, 128), share)
                up_ref[g * TALL : (g + 1) * TALL, at] = block[:, core * share : (core + 1) * share]


BIAS_ROWS = 16


def joined_grad_kernel(pieces, spot, query_grad, *rest):
    key_values = rest[:pieces]
    inputs = rest[pieces : pieces + 4]
    weight = rest[pieces + 4]
    other_ref, own_ref = rest[pieces + 5 : pieces + 7]
    input_grads = rest[pieces + 7 : pieces + 11]
    joined, turned = rest[pieces + 11 :]
    total = sum(k[...].astype(F32) for k in key_values)
    joined[:, :WIDTH] = query_grad[...]
    joined[:, WIDTH:] = total.T.astype(BF16)
    for i, ref in enumerate(input_grads):
        ref[...] = dot(joined[i * ROWS : (i + 1) * ROWS, :], weight[...], TURNED).astype(BF16)
    for i, x in enumerate(inputs):
        turned[:, i * ROWS : (i + 1) * ROWS] = x[...].T
    sums = jnp.concatenate(
        [column_sum(joined[...].astype(F32)), jnp.zeros((BIAS_ROWS - 1, 3 * WIDTH), F32)], axis=0
    ).astype(BF16)
    half = turned.shape[0] // 2
    for ref, core in ((other_ref, 1 - spot[2]), (own_ref, spot[2])):
        value = dot(turned[pl.ds(pl.multiple_of(core * half, half), half), :], joined[...]).astype(BF16)
        for quarter in range(4):
            ref[quarter, : half // 4, :] = value[quarter * (half // 4) : (quarter + 1) * (half // 4)]
            ref[quarter, half // 4 :, :] = sums


def joined_grads(spot, query_grad, key_values, inputs, weight, after):
    width = weight.shape[0]
    part = shaped((4, width // 8 + BIAS_ROWS, 3 * WIDTH))
    outs = (part, part) + (shaped((ROWS, width)),) * GROUPS
    scratch = (pltpu.VMEM((GROUPS * ROWS, 3 * WIDTH), BF16), pltpu.VMEM((width, GROUPS * ROWS), BF16))
    args = (spot, query_grad, *key_values, *inputs, weight)
    kernel = functools.partial(joined_grad_kernel, len(key_values))
    found = kernel_call(kernel, "joined_grad", outs, args, 16, 6, 1, (), scratch, after)
    return found[0], found[1], found[2:]


def place_down_kernel(spot, p0, p1, p2, p3, down_ref, out_ref):
    group, quarter = spot[0], spot[1]
    for i, piece in enumerate((p0, p1, p2, p3)):
        for g in range(GROUPS):
            block = piece[group ^ g].astype(F32)
            place = (quarter ^ i) * GROUPS + g
            down_ref[pl.ds(pl.multiple_of(place * TALL, 8), TALL), :] = block[:TALL]
            out_ref[pl.ds(pl.multiple_of(place * SHORT, 8), SHORT), :] = block[TALL:]


def place_joined_kernel(spot, p0, p1, p2, p3, weight_ref, bias_ref):
    group, quarter, core = spot[0], spot[1], spot[2]
    width = weight_ref.shape[1] // 3
    rows = p0.shape[1] - BIAS_ROWS
    for i, piece in enumerate((p0, p1, p2, p3)):
        blocks = [piece[group ^ g].astype(F32) for g in range(GROUPS)]
        for part in range(3):
            value = jnp.concatenate([b[:, part * WIDTH : (part + 1) * WIDTH] for b in blocks], axis=1)
            at = pl.ds(pl.multiple_of((quarter ^ i) * rows, 16), rows)
            weight_ref[at, part * width : (part + 1) * width] = value[:rows]
            if i == 0:
                line = value[rows : rows + 1]
                bias_ref[part : part + 1, :] = jnp.where(core == 0, line[:, : width // 2], line[:, width // 2 :])


def body(
    tokens,
    cotangent,
    lengths,
    qkv_weight,
    query_bias,
    value_bias,
    out_weight,
    out_bias,
    first_gain,
    first_shift,
    up_weight,
    up_bias,
    down_weight,
    down_bias,
    second_gain,
    second_shift,
):
    row_count, model_width = tokens.shape[1], tokens.shape[2]
    hidden_width = up_weight.shape[1]
    places = Places(lax.axis_size("seq"))
    plane_size, rest = places.plane_size, places.rest
    rank = lax.axis_index("seq")
    core = lax.axis_index("shard")
    group, position = rank // plane_size, rank % plane_size
    quarter = position // rest
    spot = jnp.stack([group, quarter, core]).astype(jnp.int32)
    length = lengths[core]
    inputs = tokens[0]
    column_rows = GROUPS * row_count
    half = model_width // 2
    turns = range(1, GROUPS)

    column_inputs = (inputs, *(places.column_swap(inputs, i) for i in turns))

    def both(block):
        return lax.all_gather(block, "shard", axis=0, tiled=True)

    def own_columns(w):
        at = group * WIDTH
        parts = [lax.dynamic_slice_in_dim(w, at + i * model_width, WIDTH, w.ndim - 1) for i in range(3)]
        return jnp.concatenate(parts, axis=-1)

    group_weight = both(own_columns(qkv_weight))
    vectors = [query_bias, value_bias, out_bias, first_gain, first_shift, down_bias, second_gain, second_shift]
    stacked = jnp.concatenate([jnp.stack(vectors), up_bias.reshape(-1, half)])
    stacked = lax.all_gather(stacked, "shard", axis=0).astype(F32)
    whole = jnp.transpose(stacked[:, : len(vectors)], (1, 0, 2)).reshape(len(vectors), model_width)
    up_offset = stacked[:, len(vectors) :].reshape(1, hidden_width)
    out_matrix = both(out_weight)
    up_matrix = both(up_weight)
    down_matrix = both(down_weight)

    offset = own_columns(jnp.concatenate([whole[0], jnp.zeros_like(whole[0]), whole[1]])).reshape(1, -1)
    query, key_value = kernel_call(
        project_kernel,
        "project",
        (shaped((column_rows, WIDTH)), shaped((column_rows, 2 * WIDTH))),
        (*column_inputs, group_weight, offset),
        16,
        2,
    )

    def masks(who):
        groups = group ^ jnp.arange(GROUPS)
        starts = (groups[None, :] * plane_size + who[:, None]) * row_count
        tokens_at = starts[:, :, None] + jnp.arange(row_count)
        return jnp.where(tokens_at.reshape(1, -1) < length, 0.0, MASKED).astype(F32)

    if plane_size == 4:
        chunks = 1
        key_values = (key_value, *(places.swap(key_value, i) for i in turns))
        bias = tuple(masks((position ^ i)[None]) for i in range(4))
    else:
        chunks = plane_size // 4
        gathered = lax.all_gather(key_value, "seq", axis=0, axis_index_groups=places.planes)
        key_values = (gathered.reshape(-1, 2 * WIDTH),)
        bias = (masks(jnp.arange(plane_size)),)
    context, log_total, context_lows = attend(query, key_values, bias, chunks)
    contexts = (context_lows[0], *(places.column_swap(context_lows[i], i) for i in turns))

    layer_out, one_grad, context_grads, up_parts, down_parts = dense(
        spot, contexts, inputs, cotangent[0], whole, up_offset, out_matrix, up_matrix, down_matrix
    )
    context_grads = (context_grads[0], *(places.column_swap(context_grads[i], i) for i in turns))
    up_parts = (up_parts[0], *(places.four_swap(up_parts[i], i) for i in turns))
    down_parts = (down_parts[0], *(places.four_swap(down_parts[i], i) for i in turns))

    def to_other(block):
        return lax.ppermute(block, "shard", [(0, 1), (1, 0)])

    def total_of(pieces, swap):
        received = [swap(pieces[i], i) for i in turns]
        total = pieces[0].astype(F32) + sum(r.astype(F32) for r in received)
        return lax.psum(total, "seq", axis_index_groups=places.rests) if rest > 1 else total

    def gather_all(part):
        column = jnp.stack([part, *(places.column_swap(part, i) for i in turns)])
        return (column, *(places.four_swap(column, i) for i in turns))

    query_grad, parts = attend_grad(query, context, context_grads, log_total, key_values, bias, chunks)
    other, own = down_grad_parts(spot, down_parts, model_width, (query_grad,))
    down_pieces = core_sums(spot, own, to_other(other), 0, "down_sum")
    down_part = total_of(down_pieces, places.column_swap)
    extra = down_part[TALL + SHORT :]
    up_bias_grad = jnp.concatenate([extra[6, :half], extra[7, :half], extra[0, half:], extra[1, half:]])
    if plane_size == 4:
        key_value_grads = (parts[0], *(places.swap(parts[i], i) for i in turns))
    else:
        blocks = parts[0].reshape(2 * WIDTH, plane_size, column_rows)
        blocks = places.exchange(jnp.transpose(blocks, (1, 0, 2)), places.planes)
        key_value_grads = (jnp.sum(blocks.astype(F32), axis=0),)
    other, own, input_parts = joined_grads(
        spot, query_grad, key_value_grads, column_inputs, group_weight, (down_pieces[0],)
    )
    up_other, up_own = up_grad_parts(spot, up_parts, model_width, (input_parts[0],))
    up_pieces = core_sums(spot, up_own, to_other(up_other), 0, "up_sum")
    up_part = total_of(up_pieces, places.column_swap).astype(BF16)
    input_parts = (input_parts[0], *(places.column_swap(input_parts[i], i) for i in turns))
    input_grad = one_grad + sum(p.astype(F32) for p in input_parts)
    joined_pieces = core_sums(spot, own, to_other(other), 1, "joined_sum")
    joined_part = total_of(joined_pieces, places.four_swap).astype(BF16)
    low = down_part[: TALL + SHORT].astype(BF16)
    down_all = gather_all(low)
    up_all = gather_all(up_part)
    joined_all = gather_all(joined_part)
    down_grad, out_grad = kernel_call(
        place_down_kernel,
        "place_down",
        (shaped((hidden_width // 2, model_width), F32), shaped((half, model_width), F32)),
        (spot, *down_all),
        16,
        5,
        1,
    )
    qkv_grad, bias_grad = kernel_call(
        place_joined_kernel,
        "place_joined",
        (shaped((half, 3 * model_width), F32), shaped((8, half), F32)),
        (spot, *joined_all),
        24,
        5,
        1,
    )
    up_grad = kernel_call(
        place_up_kernel,
        "place_up",
        shaped((half, hidden_width), F32),
        (spot, *up_all),
        16,
        4,
        1,
    )

    shape = (1, row_count, model_width)
    return (
        layer_out.reshape(shape),
        input_grad.reshape(shape),
        qkv_grad,
        bias_grad[0],
        bias_grad[2],
        out_grad,
        extra[0, :half],
        extra[1, :half],
        extra[2, :half],
        up_grad,
        up_bias_grad,
        down_grad,
        extra[3, :half],
        extra[4, :half],
        extra[5, :half],
    )


def solution(mesh):
    rows, halves, whole = P("shard", "seq", None), P("shard", None), P("shard")
    in_specs = (rows, rows, P(), halves, whole, whole, halves, whole, whole, whole, halves, whole, halves, whole, whole, whole)
    out_specs = (rows, rows, halves, whole, whole, halves, whole, whole, whole, halves, whole, halves, whole, whole, whole)
    return jax.shard_map(body, mesh=mesh, in_specs=in_specs, out_specs=out_specs, check_vma=False)
```

```python
import functools

import jax
import jax.numpy as jnp
from jax import lax
from jax.experimental import pallas as pl
from jax.experimental.pallas import tpu as pltpu
from jax.sharding import PartitionSpec as P

HEADS = 12
HEAD_DIM = 64
GROUPS = 4
GROUP_HEADS = HEADS // GROUPS
WIDTH = GROUP_HEADS * HEAD_DIM
EPSILON = 1e-12
MASKED = -1e30
F32 = jnp.float32
BF16 = jnp.bfloat16
MIB = 2**20
ROWS = 128
TURNED = ((1,), (1,))
FIRST = ((1,), (0,))


def dot(left, right, dims=FIRST):
    return lax.dot_general(left, right, (dims, ((), ())), preferred_element_type=F32)


def kernel_call(kernel, name, outs, args, vmem, micros, smem=0, left=(), scratch=(), after=()):
    spaces = [
        pl.BlockSpec(memory_space=pltpu.SMEM if i < smem else pltpu.HBM if i in left else pltpu.VMEM)
        for i in range(len(args))
    ]
    count = len(args)

    def run(*refs):
        kernel(*refs[:count], *refs[count + len(after) :])

    return pl.pallas_call(
        run if after else kernel,
        out_shape=outs,
        in_specs=spaces + [pl.BlockSpec(memory_space=pl.ANY)] * len(after),
        scratch_shapes=list(scratch),
        compiler_params=pltpu.CompilerParams(vmem_limit_bytes=vmem * MIB),
        cost_estimate=pl.CostEstimate(flops=0, bytes_accessed=int(micros * 3_500_000), transcendentals=0),
        name=name,
    )(*args, *after)


def shaped(shape, dtype=BF16):
    return jax.ShapeDtypeStruct(shape, dtype)


class Places:
    def __init__(self, size):
        self.size = size
        self.plane_size = size // GROUPS
        self.rest = self.plane_size // 4
        index = lambda g, q, m: (g * 4 + q) * self.rest + m
        groups, quarters, members = range(GROUPS), range(4), range(self.rest)
        self.columns = [[index(g, q, m) for g in groups] for q in quarters for m in members]
        self.planes = [[index(g, q, m) for q in quarters for m in members] for g in groups]
        self.fours = [[index(g, q, m) for q in quarters] for g in groups for m in members]
        self.sixteens = [[index(g, q, m) for g in groups for q in quarters] for m in members]
        self.rests = [[index(g, q, m) for m in members] for g in groups for q in quarters]

    def swap(self, block, bits):
        return lax.ppermute(block, "seq", [(i, i ^ bits) for i in range(self.size)])

    def column_swap(self, block, turn):
        return self.swap(block, turn * self.plane_size)

    def four_swap(self, block, turn):
        return self.swap(block, turn * self.rest)

    def exchange(self, blocks, groups):
        return lax.all_to_all(blocks, "seq", 0, 0, axis_index_groups=groups, tiled=True)


def project_kernel(x0, x1, x2, x3, weight, offset, query_ref, key_value_ref):
    for i, x in enumerate((x0, x1, x2, x3)):
        at = slice(i * ROWS, (i + 1) * ROWS)
        joined = (dot(x[...], weight[...]) + offset[...]).astype(BF16)
        query_ref[at, :] = joined[:, :WIDTH] * jnp.asarray(0.125, BF16)
        key_value_ref[at, :] = joined[:, WIDTH:]


def attend_kernel(pieces, chunks, *refs):
    q_ref = refs[0]
    key_value_refs, bias_refs = refs[1 : 1 + pieces], refs[1 + pieces : 1 + 2 * pieces]
    context_ref, log_ref = refs[1 + 2 * pieces : 3 + 2 * pieces]
    low_refs = refs[3 + 2 * pieces :]
    rows = q_ref.shape[0]
    chunk = key_value_refs[0].shape[0] // chunks
    for block in range(rows // ROWS):
        at = slice(block * ROWS, (block + 1) * ROWS)
        for head in range(GROUP_HEADS):
            columns = slice(head * HEAD_DIM, (head + 1) * HEAD_DIM)
            value_columns = slice(WIDTH + head * HEAD_DIM, WIDTH + (head + 1) * HEAD_DIM)
            query = q_ref[at, columns]

            def step(index, state):
                highest, total, mix = state
                here = pl.ds(pl.multiple_of(index * chunk, chunk), chunk)
                scores = [dot(query, k[here, columns], TURNED) + b[:, here] for k, b in zip(key_value_refs, bias_refs)]
                peak = functools.reduce(jnp.maximum, [jnp.max(s, axis=1, keepdims=True) for s in scores])
                raised = jnp.maximum(highest, peak)
                weights = [jnp.exp(s - raised) for s in scores]
                factor = jnp.exp(highest - raised)
                total = total * factor + sum(jnp.sum(w, axis=1, keepdims=True) for w in weights)
                mix = mix * factor + sum(
                    dot(w.astype(BF16), v[here, value_columns]) for w, v in zip(weights, key_value_refs)
                )
                return raised, total, mix

            state = (
                jnp.full((ROWS, 1), MASKED, F32),
                jnp.zeros((ROWS, 1), F32),
                jnp.zeros((ROWS, HEAD_DIM), F32),
            )
            highest, total, mix = step(0, state) if chunks == 1 else lax.fori_loop(0, chunks, step, state)
            context = mix / total
            context_ref[at, columns] = context
            low_refs[block][:, columns] = context.astype(BF16)
            log_ref[at, head : head + 1] = highest + jnp.log(total)


def attend(query, key_values, bias, chunks):
    rows = query.shape[0]
    outs = (shaped((rows, WIDTH), F32), shaped((rows, 128), F32)) + (shaped((ROWS, WIDTH)),) * GROUPS
    kernel = functools.partial(attend_kernel, len(key_values), chunks)
    found = kernel_call(kernel, "attend", outs, (query, *key_values, *bias), 24 if chunks == 1 else 60, 9)
    return found[0], found[1], found[2:]


def attend_grad_kernel(pieces, chunks, *refs):
    q_ref, context_ref, log_ref = refs[:3]
    grad_refs = refs[3:7]
    key_value_refs, bias_refs = refs[7 : 7 + pieces], refs[7 + pieces : 7 + 2 * pieces]
    query_grad_ref = refs[7 + 2 * pieces]
    outs = refs[8 + 2 * pieces :]
    if pieces == 4:
        own_key, own_value, turned_key, turned_value, key_x, value_y = outs
        key_outs = (own_key, key_x.at[0], turned_key, key_x.at[1])
        value_outs = (own_value, turned_value, value_y.at[0], value_y.at[1])
    else:
        key_outs, value_outs = outs[:1], outs[1:]
    rows = q_ref.shape[0]
    chunk = key_value_refs[0].shape[0] // chunks
    for head in range(GROUP_HEADS):
        columns = slice(head * HEAD_DIM, (head + 1) * HEAD_DIM)
        value_columns = slice(WIDTH + head * HEAD_DIM, WIDTH + (head + 1) * HEAD_DIM)
        query = q_ref[:, columns]
        grad = jnp.concatenate([g[:, columns] for g in grad_refs], axis=0)
        correction = jnp.sum(grad.astype(F32) * context_ref[:, columns], axis=1, keepdims=True)
        log_total = log_ref[:, head : head + 1]
        query_turned = query.T
        grad_turned = grad.T

        def step(index, query_grad):
            here = pl.ds(pl.multiple_of(index * chunk, chunk), chunk)
            for both, b, key_out, value_out in zip(key_value_refs, bias_refs, key_outs, value_outs):
                key = both[here, columns]
                probs = jnp.exp(dot(query, key, TURNED) + b[:, here] - log_total)
                probs_grad = dot(grad, both[here, value_columns], TURNED)
                score_grad = (probs * (probs_grad - correction)).astype(BF16)
                query_grad = query_grad + dot(score_grad, key)
                key_out[columns, here] = dot(query_turned, score_grad).astype(BF16)
                value_out[columns, here] = dot(grad_turned, probs.astype(BF16)).astype(BF16)
            return query_grad

        total = jnp.zeros((rows, HEAD_DIM), F32)
        total = step(0, total) if chunks == 1 else lax.fori_loop(0, chunks, step, total)
        query_grad_ref[:, columns] = (total * 0.125).astype(BF16)


def attend_grad(query, context, grads, log_total, key_values, bias, chunks):
    rows, keys = query.shape[0], key_values[0].shape[0]
    one, two = shaped((WIDTH, keys)), shaped((2, WIDTH, keys))
    outs = (shaped((rows, WIDTH)),) + ((one, one, one, one, two, two) if len(key_values) == 4 else (one, one))
    kernel = functools.partial(attend_grad_kernel, len(key_values), chunks)
    args = (query, context, log_total, *grads, *key_values, *bias)
    found = kernel_call(kernel, "attend_grad", outs, args, 32 if chunks == 1 else 60, 11)
    return found[0], found[1:]


def normalize(hidden):
    center = hidden - jnp.mean(hidden, axis=1, keepdims=True)
    scale = lax.rsqrt(jnp.mean(center * center, axis=1, keepdims=True) + EPSILON)
    return center * scale, scale


def normalize_grad(grad, normal, scale):
    return scale * (
        grad
        - jnp.mean(grad, axis=1, keepdims=True)
        - normal * jnp.mean(grad * normal, axis=1, keepdims=True)
    )


def column_sum(values):
    return jnp.sum(values, axis=0, keepdims=True)


TALL, SHORT, EXTRA = 96, 24, 8


def dense_kernel(width, spot, c0, c1, c2, c3, x_ref, grad_ref, vectors, up_offset, out_hbm, up_hbm, down_hbm, *rest):
    layer_ref, one_grad_ref = rest[:2]
    context_grads, up_parts, down_parts = rest[2:6], rest[6:10], rest[10:14]
    out_w, up_w, down_w, slope, active_ref, inner_ref, sums_ref, sems = rest[14:]
    copies = [
        pltpu.make_async_copy(source, target, sems.at[i])
        for i, (source, target) in enumerate(((out_hbm, out_w), (up_hbm, up_w), (down_hbm, down_w)))
    ]
    for copy in copies:
        copy.start()
    hidden = up_w.shape[1]
    half = width // 2
    out_offset, gain_one, shift_one, down_offset, gain_two, shift_two = (vectors[i : i + 1, :] for i in range(2, 8))
    group, quarter = spot[0], spot[1]
    contexts = (c0, c1, c2, c3)

    def turned(i):
        return pl.ds(pl.multiple_of((group ^ i) * WIDTH, WIDTH), WIDTH)

    copies[0].wait()
    branch = sum(dot(c[...], out_w[turned(i), :]) for i, c in enumerate(contexts)) + out_offset
    normal_one, scale_one = normalize(x_ref[...].astype(F32) + branch)
    normed_low = (normal_one * gain_one + shift_one).astype(BF16)
    for ref in up_parts:
        ref[:, :width] = normed_low
    copies[1].wait()
    copies[2].wait()
    step = 768
    second = jnp.zeros((ROWS, width), F32) + down_offset
    for start in range(0, hidden, step):
        at = slice(start, start + step)
        inner = dot(normed_low, up_w[:, at]) + up_offset[:, at]
        share = 0.5 + 0.5 * lax.erf(inner * 0.7071067811865476)
        density = 0.3989422804014327 * jnp.exp(-0.5 * inner * inner)
        slope[:, at] = share + inner * density
        active = (inner * share).astype(BF16)
        active_ref[:, at] = active
        second = second + dot(active, down_w[at, :])
    normal_two, scale_two = normalize(normed_low.astype(F32) + second)
    layer_ref[...] = (normal_two * gain_two + shift_two).astype(BF16)
    grad = grad_ref[...].astype(F32)
    gain_two_grad, shift_two_grad = column_sum(grad * normal_two), column_sum(grad)
    two_grad = normalize_grad(grad * gain_two, normal_two, scale_two)
    second_low = two_grad.astype(BF16)
    down_bias_grad = column_sum(second_low.astype(F32))
    normed_grad = two_grad
    for start in range(0, hidden, step):
        at = slice(start, start + step)
        inner_low = (dot(second_low, down_w[at, :], TURNED) * slope[:, at]).astype(BF16)
        inner_ref[:, at] = inner_low
        up_sum = column_sum(inner_low.astype(F32))
        for piece in range(step // half):
            place = start // half + piece
            per_core = hidden // 2 // half
            row, core = 6 + place % per_core, place // per_core
            sums_ref[row : row + 1, core * half : (core + 1) * half] = up_sum[:, piece * half : (piece + 1) * half]
        normed_grad = normed_grad + dot(inner_low, up_w[:, at], TURNED)
    gain_one_grad, shift_one_grad = column_sum(normed_grad * normal_one), column_sum(normed_grad)
    one_grad = normalize_grad(normed_grad * gain_one, normal_one, scale_one)
    one_grad_ref[...] = one_grad
    branch_low = one_grad.astype(BF16)
    for i, ref in enumerate(context_grads):
        ref[...] = dot(branch_low, out_w[turned(i), :], TURNED).astype(BF16)
    out_bias_grad = column_sum(branch_low.astype(F32))
    sums = (out_bias_grad, gain_one_grad, shift_one_grad, down_bias_grad, gain_two_grad, shift_two_grad)
    for i, total in enumerate(sums):
        sums_ref[i : i + 1, :] = total
    sums_ref[10:16, :] = jnp.zeros((6, width), F32)
    share = hidden // 8
    for i in range(4):
        for core in range(2):
            at = pl.ds(pl.multiple_of(core * (hidden // 2) + (quarter ^ i) * share, share), share)
            to = slice(width + core * share, width + (core + 1) * share)
            up_parts[i][:, to] = inner_ref[:, at]
            down_parts[i][:ROWS, to] = active_ref[:, at]
        down_parts[i][:ROWS, :width] = second_low
        down_parts[i][:ROWS, 2 * width : 3 * width] = branch_low
        down_parts[i][ROWS:, :width] = sums_ref[...].astype(BF16)
    strip = width // 8
    for i, c in enumerate(contexts):
        for g in range(GROUPS):
            @pl.when((group ^ i) == g)
            def _():
                for part in range(2):
                    core, owner = divmod((g * WIDTH + part * strip) // strip, 4)
                    for turn in range(4):
                        @pl.when((quarter ^ turn) == owner)
                        def _():
                            to = 3 * width + core * strip
                            down_parts[turn][:ROWS, to : to + strip] = c[:, part * strip : (part + 1) * strip]


def dense(spot, contexts, inputs, grad, vectors, up_offset, out_matrix, up_matrix, down_matrix):
    width, hidden = up_matrix.shape
    outs = (
        (shaped((ROWS, width)), shaped((ROWS, width), F32))
        + (shaped((ROWS, WIDTH)),) * GROUPS
        + (shaped((ROWS, width + hidden // 4)),) * 4
        + (shaped((ROWS + 16, 3 * width + 256)),) * 4
    )
    scratch = (
        pltpu.VMEM(out_matrix.shape, BF16),
        pltpu.VMEM(up_matrix.shape, BF16),
        pltpu.VMEM(down_matrix.shape, BF16),
        pltpu.VMEM((ROWS, hidden), F32),
        pltpu.VMEM((ROWS, hidden), BF16),
        pltpu.VMEM((ROWS, hidden), BF16),
        pltpu.VMEM((16, width), F32),
        pltpu.SemaphoreType.DMA((3,)),
    )
    args = (spot, *contexts, inputs, grad, vectors, up_offset, out_matrix, up_matrix, down_matrix)
    found = kernel_call(
        functools.partial(dense_kernel, width), "dense", outs, args, 22, 10, 1, (9, 10, 11), scratch
    )
    return found[0], found[1], found[2:6], found[6:10], found[10:14]


def halves_of(spot, first, second):
    return ((first, 1 - spot[2]), (second, spot[2]))


def up_grad_kernel(spot, p0, p1, p2, p3, other_ref, own_ref, turned, inner):
    width = turned.shape[0]
    for i, part in enumerate((p0, p1, p2, p3)):
        turned[:, i * ROWS : (i + 1) * ROWS] = part[:, :width].T
        inner[i * ROWS : (i + 1) * ROWS, :] = part[:, width:]
    half = width // 2
    for ref, core in halves_of(spot, other_ref, own_ref):
        value = dot(turned[pl.ds(pl.multiple_of(core * half, half), half), :], inner[...]).astype(BF16)
        for g in range(GROUPS):
            ref[g] = value[g * TALL : (g + 1) * TALL]


def up_grad_parts(spot, parts, width):
    tokens, columns = 4 * ROWS, parts[0].shape[1] - width
    out = shaped((GROUPS, TALL, columns))
    scratch = (pltpu.VMEM((width, tokens), BF16), pltpu.VMEM((tokens, columns), BF16))
    return kernel_call(up_grad_kernel, "up_grad", (out, out), (spot, *parts), 16, 4, 1, (), scratch)


def down_grad_kernel(spot, p0, p1, p2, p3, other_ref, own_ref, turned, second, branch, sums):
    parts = (p0, p1, p2, p3)
    width = second.shape[1]
    tall, strip = GROUPS * TALL, GROUPS * SHORT
    for i, part in enumerate(parts):
        rows = slice(i * ROWS, (i + 1) * ROWS)
        turned[: 2 * tall, rows] = part[:ROWS, width : 2 * width].T
        turned[2 * tall : 2 * tall + 256, rows] = part[:ROWS, 3 * width :].T
        second[rows, :] = part[:ROWS, :width]
        branch[rows, :] = part[:ROWS, 2 * width : 3 * width]
    total = sum(part[ROWS:, :width].astype(F32) for part in parts)
    for core in range(2):
        start = core * (width // 2)
        sums[core] = jnp.concatenate(
            [total[:EXTRA, start : start + width // 2], total[EXTRA:, start : start + width // 2]], axis=1
        )
    for ref, core in halves_of(spot, other_ref, own_ref):
        down = dot(turned[pl.ds(pl.multiple_of(core * tall, tall), tall), :], second[...])
        out = dot(turned[pl.ds(pl.multiple_of(2 * tall + core * strip, 32), strip), :], branch[...])
        for g in range(GROUPS):
            ref[g] = jnp.concatenate(
                [down[g * TALL : (g + 1) * TALL], out[g * SHORT : (g + 1) * SHORT], sums[core]], axis=0
            ).astype(BF16)


def down_grad_parts(spot, parts, width):
    tokens = 4 * ROWS
    out = shaped((GROUPS, TALL + SHORT + EXTRA, width))
    scratch = (
        pltpu.VMEM((2 * GROUPS * TALL + 256, tokens), BF16),
        pltpu.VMEM((tokens, width), BF16),
        pltpu.VMEM((tokens, width), BF16),
        pltpu.VMEM((2, EXTRA, width), F32),
    )
    return kernel_call(down_grad_kernel, "down_grad", (out, out), (spot, *parts), 16, 5, 1, (), scratch)


def core_sum_kernel(which, spot, own, received, *outs):
    at = spot[which]
    for i, out in enumerate(outs):
        out[...] = (own[at ^ i].astype(F32) + received[at ^ i].astype(F32)).astype(BF16)


def core_sums(spot, own, received, which, name):
    outs = (shaped(own.shape[1:]),) * 4
    return kernel_call(functools.partial(core_sum_kernel, which), name, outs, (spot, own, received), 16, 2, 1)


def pair_sum_kernel(spot, own, received, kept, sent):
    for i, out in ((1, sent.at[0]), (2, sent.at[1]), (3, kept.at[1]), (0, kept.at[0])):
        at = spot[0] ^ i
        out[...] = (own[at].astype(F32) + received[at].astype(F32)).astype(BF16)


def pair_sums(spot, own, received, name):
    pair = shaped((2, *own.shape[1:]))
    return kernel_call(pair_sum_kernel, name, (pair, pair), (spot, own, received), 16, 2, 1)


def placed(spot, pieces, turned):
    group, quarter = spot[0], spot[1]
    for i in range(4):
        for g in range(GROUPS):
            turn = group ^ g
            at = ((turn & 1) << 1) ^ ((turn >> 1) * 3) if turned[1] else g
            if turned[0]:
                yield quarter ^ i, g, pieces[i][at]
            else:
                yield i, g, pieces[0][i, at]


def place_up_kernel(turned, spot, *refs):
    up_ref = refs[-1]
    for quarter, g, block in placed(spot, refs[:-1], turned):
        share = block.shape[1] // 2
        block = block.astype(F32)
        for core in range(2):
            at = pl.ds(pl.multiple_of(core * 4 * share + quarter * share, 128), share)
            up_ref[g * TALL : (g + 1) * TALL, at] = block[:, core * share : (core + 1) * share]


BIAS_ROWS = 16


def joined_grad_kernel(pieces, spot, query_grad, *rest):
    keys, values = rest[:pieces], rest[pieces : 2 * pieces]
    inputs = rest[2 * pieces : 2 * pieces + 4]
    weight, other_ref, own_ref, kept_ref, sent_ref, joined, turned = rest[2 * pieces + 4 :]

    def total(parts):
        blocks = [p[0] if len(p.shape) == 3 else p[...] for p in parts]
        return sum(b.astype(F32) for b in blocks).T.astype(BF16)

    joined[:, :WIDTH] = query_grad[...]
    joined[:, WIDTH : 2 * WIDTH] = total(keys)
    joined[:, 2 * WIDTH :] = total(values)
    for i, ref in ((1, sent_ref.at[0]), (2, sent_ref.at[1]), (3, kept_ref.at[1]), (0, kept_ref.at[0])):
        ref[...] = dot(joined[i * ROWS : (i + 1) * ROWS, :], weight[...], TURNED).astype(BF16)
    for i, x in enumerate(inputs):
        turned[:, i * ROWS : (i + 1) * ROWS] = x[...].T
    sums = jnp.concatenate(
        [column_sum(joined[...].astype(F32)), jnp.zeros((BIAS_ROWS - 1, 3 * WIDTH), F32)], axis=0
    ).astype(BF16)
    half = turned.shape[0] // 2
    for ref, core in halves_of(spot, other_ref, own_ref):
        value = dot(turned[pl.ds(pl.multiple_of(core * half, half), half), :], joined[...]).astype(BF16)
        for quarter in range(4):
            ref[quarter, : half // 4, :] = value[quarter * (half // 4) : (quarter + 1) * (half // 4)]
            ref[quarter, half // 4 :, :] = sums


def joined_grads(spot, query_grad, keys, values, inputs, weight):
    width = weight.shape[0]
    part, pair = shaped((4, width // 8 + BIAS_ROWS, 3 * WIDTH)), shaped((2, ROWS, width))
    scratch = (pltpu.VMEM((GROUPS * ROWS, 3 * WIDTH), BF16), pltpu.VMEM((width, GROUPS * ROWS), BF16))
    args = (spot, query_grad, *keys, *values, *inputs, weight)
    kernel = functools.partial(joined_grad_kernel, len(keys))
    return kernel_call(kernel, "joined_grad", (part, part, pair, pair), args, 16, 6, 1, (), scratch)


def place_down_kernel(turned, spot, *refs):
    down_ref, out_ref = refs[-2:]
    for quarter, g, block in placed(spot, refs[:-2], turned):
        block = block.astype(F32)
        place = quarter * GROUPS + g
        down_ref[pl.ds(pl.multiple_of(place * TALL, 8), TALL), :] = block[:TALL]
        out_ref[pl.ds(pl.multiple_of(place * SHORT, 8), SHORT), :] = block[TALL : TALL + SHORT]


def place_joined_kernel(turned, spot, *refs):
    weight_ref, bias_ref = refs[-2:]
    core = spot[2]
    width = weight_ref.shape[1] // 3
    found = list(placed(spot, refs[:-2], turned))
    for i in range(4):
        quarter = found[i * GROUPS][0]
        blocks = [block.astype(F32) for _, _, block in found[i * GROUPS : (i + 1) * GROUPS]]
        rows = blocks[0].shape[0] - BIAS_ROWS
        at = pl.ds(pl.multiple_of(quarter * rows, 16), rows)
        for part in range(3):
            value = jnp.concatenate([b[:, part * WIDTH : (part + 1) * WIDTH] for b in blocks], axis=1)
            weight_ref[at, part * width : (part + 1) * width] = value[:rows]
            if i == 0:
                line = value[rows : rows + 1]
                bias_ref[part : part + 1, :] = jnp.where(core == 0, line[:, : width // 2], line[:, width // 2 :])


def body(
    tokens,
    cotangent,
    lengths,
    qkv_weight,
    query_bias,
    value_bias,
    out_weight,
    out_bias,
    first_gain,
    first_shift,
    up_weight,
    up_bias,
    down_weight,
    down_bias,
    second_gain,
    second_shift,
):
    row_count, model_width = tokens.shape[1], tokens.shape[2]
    hidden_width = up_weight.shape[1]
    places = Places(lax.axis_size("seq"))
    plane_size, rest = places.plane_size, places.rest
    rank = lax.axis_index("seq")
    core = lax.axis_index("shard")
    group, position = rank // plane_size, rank % plane_size
    quarter = position // rest
    spot = jnp.stack([group, quarter, core]).astype(jnp.int32)
    length = lengths[core]
    inputs = tokens[0]
    column_rows = GROUPS * row_count
    half = model_width // 2
    turns = range(1, GROUPS)

    column_inputs = (inputs, *(places.column_swap(inputs, i) for i in turns))

    def both(block):
        return lax.all_gather(block, "shard", axis=0, tiled=True)

    def own_columns(w):
        at = group * WIDTH
        parts = [lax.dynamic_slice_in_dim(w, at + i * model_width, WIDTH, w.ndim - 1) for i in range(3)]
        return jnp.concatenate(parts, axis=-1)

    group_weight = both(own_columns(qkv_weight))
    vectors = [query_bias, value_bias, out_bias, first_gain, first_shift, down_bias, second_gain, second_shift]
    stacked = jnp.concatenate([jnp.stack(vectors), up_bias.reshape(-1, half)])
    stacked = lax.all_gather(stacked, "shard", axis=0).astype(F32)
    whole = jnp.transpose(stacked[:, : len(vectors)], (1, 0, 2)).reshape(len(vectors), model_width)
    up_offset = stacked[:, len(vectors) :].reshape(1, hidden_width)
    out_matrix = both(out_weight)
    up_matrix = both(up_weight)
    down_matrix = both(down_weight)

    offset = own_columns(jnp.concatenate([whole[0], jnp.zeros_like(whole[0]), whole[1]])).reshape(1, -1)
    query, key_value = kernel_call(
        project_kernel,
        "project",
        (shaped((column_rows, WIDTH)), shaped((column_rows, 2 * WIDTH))),
        (*column_inputs, group_weight, offset),
        16,
        2,
    )

    def masks(who):
        groups = group ^ jnp.arange(GROUPS)
        starts = (groups[None, :] * plane_size + who[:, None]) * row_count
        tokens_at = starts[:, :, None] + jnp.arange(row_count)
        return jnp.where(tokens_at.reshape(1, -1) < length, 0.0, MASKED).astype(F32)

    if plane_size == 4:
        chunks = 1
        key_values = (key_value, *(places.swap(key_value, i) for i in turns))
        bias = tuple(masks((position ^ i)[None]) for i in range(4))
    else:
        chunks = plane_size // 4
        gathered = lax.all_gather(key_value, "seq", axis=0, axis_index_groups=places.planes)
        key_values = (gathered.reshape(-1, 2 * WIDTH),)
        bias = (masks(jnp.arange(plane_size)),)
    context, log_total, context_lows = attend(query, key_values, bias, chunks)
    contexts = (context_lows[0], *(places.column_swap(context_lows[i], i) for i in turns))

    layer_out, one_grad, context_grads, up_parts, down_parts = dense(
        spot, contexts, inputs, cotangent[0], whole, up_offset, out_matrix, up_matrix, down_matrix
    )
    def after(value, *others):
        return lax.optimization_barrier((value, *others))[0]

    def to_other(block):
        return lax.ppermute(block, "shard", [(0, 1), (1, 0)])

    def rest_sum(total):
        return lax.psum(total, "seq", axis_index_groups=places.rests) if rest > 1 else total

    def add(left, right):
        return (left.astype(F32) + right.astype(F32)).astype(BF16)

    def column_total(kept, sent):
        near = places.column_swap(sent, 1)
        far = places.column_swap(add(kept[1], near[1]), 3)
        return kept[0].astype(F32) + near[0].astype(F32) + far.astype(F32)

    def column_gather(part):
        pair = jnp.stack([part, places.column_swap(part, 3)])
        return jnp.concatenate([pair, places.column_swap(pair, 1)])

    def plane_gather(column):
        return (column, *(places.four_swap(column, i) for i in turns))

    context_grads = (context_grads[0], *(places.column_swap(context_grads[i], i) for i in turns))
    down_parts = (down_parts[0], *(places.four_swap(down_parts[i], i) for i in turns))
    query_grad, parts = attend_grad(query, context, context_grads, log_total, key_values, bias, chunks)
    if plane_size == 4:
        own_key, own_value, turned_key, turned_value, key_x, value_y = parts
        key_x, value_y = places.swap(key_x, 1), places.swap(value_y, 2)
        keys = (own_key, key_x, places.swap(add(turned_key, key_x[1]), 2))
        values = (own_value, value_y, places.swap(add(turned_value, value_y[1]), 1))
    else:
        blocks = jnp.stack(parts).reshape(2 * WIDTH, plane_size, column_rows)
        blocks = places.exchange(jnp.transpose(blocks, (1, 0, 2)), places.planes)
        blocks = jnp.sum(blocks.astype(F32), axis=0)
        keys, values = (blocks[:WIDTH],), (blocks[WIDTH:],)
    down_parts = after(down_parts, query_grad)
    other, own = down_grad_parts(spot, down_parts, model_width)
    down_part = rest_sum(column_total(*pair_sums(spot, own, to_other(other), "down_sum")))
    keys, values = after((keys, values), down_part)
    other, own, kept, sent = joined_grads(spot, query_grad, keys, values, column_inputs, group_weight)
    input_grad = one_grad + column_total(kept, sent)
    joined_pieces = core_sums(spot, own, to_other(other), 1, "joined_sum")
    received = [places.four_swap(joined_pieces[i], i) for i in turns]
    joined_part = rest_sum(joined_pieces[0].astype(F32) + sum(r.astype(F32) for r in received)).astype(BF16)
    up_parts = after(up_parts, down_parts)
    up_parts = (up_parts[0], *(places.four_swap(up_parts[i], i) for i in turns))
    up_parts = after(up_parts, kept)
    other, own = up_grad_parts(spot, up_parts, model_width)
    up_part = rest_sum(column_total(*pair_sums(spot, own, to_other(other), "up_sum"))).astype(BF16)
    down_all = plane_gather(column_gather(down_part[: TALL + SHORT].astype(BF16)))
    up_all = plane_gather(column_gather(up_part))
    joined_all = plane_gather(column_gather(joined_part))
    extra = down_part[TALL + SHORT :]
    up_bias_grad = jnp.concatenate([extra[6, :half], extra[7, :half], extra[0, half:], extra[1, half:]])
    turned = (True, True)
    down_grad, out_grad = kernel_call(
        functools.partial(place_down_kernel, turned),
        "place_down",
        (shaped((hidden_width // 2, model_width), F32), shaped((half, model_width), F32)),
        (spot, *down_all),
        16,
        5,
        1,
    )
    qkv_grad, bias_grad = kernel_call(
        functools.partial(place_joined_kernel, turned),
        "place_joined",
        (shaped((half, 3 * model_width), F32), shaped((8, half), F32)),
        (spot, *joined_all),
        16,
        5,
        1,
    )
    up_grad = kernel_call(
        functools.partial(place_up_kernel, turned),
        "place_up",
        shaped((half, hidden_width), F32),
        (spot, *up_all),
        16,
        4,
        1,
    )

    shape = (1, row_count, model_width)
    return (
        layer_out.reshape(shape),
        input_grad.reshape(shape),
        qkv_grad,
        bias_grad[0],
        bias_grad[2],
        out_grad,
        extra[0, :half],
        extra[1, :half],
        extra[2, :half],
        up_grad,
        up_bias_grad,
        down_grad,
        extra[3, :half],
        extra[4, :half],
        extra[5, :half],
    )


def solution(mesh):
    rows, halves, whole = P("shard", "seq", None), P("shard", None), P("shard")
    in_specs = (rows, rows, P(), halves, whole, whole, halves, whole, whole, whole, halves, whole, halves, whole, whole, whole)
    out_specs = (rows, rows, halves, whole, whole, halves, whole, whole, whole, halves, whole, halves, whole, whole, whole)
    return jax.shard_map(body, mesh=mesh, in_specs=in_specs, out_specs=out_specs, check_vma=False)
```

```python
import functools

import jax
import jax.numpy as jnp
from jax import lax
from jax.experimental import pallas as pl
from jax.experimental.pallas import tpu as pltpu
from jax.sharding import PartitionSpec as P

HEADS = 12
HEAD_DIM = 64
GROUPS = 4
GROUP_HEADS = HEADS // GROUPS
WIDTH = GROUP_HEADS * HEAD_DIM
EPSILON = 1e-12
MASKED = -1e30
F32 = jnp.float32
BF16 = jnp.bfloat16
MIB = 2**20
ROWS = 128
TURNED = ((1,), (1,))
FIRST = ((1,), (0,))


def dot(left, right, dims=FIRST):
    return lax.dot_general(left, right, (dims, ((), ())), preferred_element_type=F32)


def kernel_call(kernel, name, outs, args, vmem, micros, smem=0, left=(), scratch=(), after=()):
    spaces = [
        pl.BlockSpec(memory_space=pltpu.SMEM if i < smem else pltpu.HBM if i in left else pltpu.VMEM)
        for i in range(len(args))
    ]
    count = len(args)

    def run(*refs):
        kernel(*refs[:count], *refs[count + len(after) :])

    return pl.pallas_call(
        run if after else kernel,
        out_shape=outs,
        in_specs=spaces + [pl.BlockSpec(memory_space=pl.ANY)] * len(after),
        scratch_shapes=list(scratch),
        compiler_params=pltpu.CompilerParams(vmem_limit_bytes=vmem * MIB),
        cost_estimate=pl.CostEstimate(flops=0, bytes_accessed=int(micros * 3_500_000), transcendentals=0),
        name=name,
    )(*args, *after)


def in_hbm(array):
    return pltpu.with_memory_space_constraint(array, pltpu.HBM)


def shaped(shape, dtype=BF16):
    return jax.ShapeDtypeStruct(shape, dtype)


class Places:
    def __init__(self, size):
        self.size = size
        self.plane_size = size // GROUPS
        self.rest = self.plane_size // 4
        index = lambda g, q, m: (g * 4 + q) * self.rest + m
        groups, quarters, members = range(GROUPS), range(4), range(self.rest)
        self.columns = [[index(g, q, m) for g in groups] for q in quarters for m in members]
        self.planes = [[index(g, q, m) for q in quarters for m in members] for g in groups]
        self.fours = [[index(g, q, m) for q in quarters] for g in groups for m in members]
        self.sixteens = [[index(g, q, m) for g in groups for q in quarters] for m in members]
        self.rests = [[index(g, q, m) for m in members] for g in groups for q in quarters]

    def swap(self, block, bits):
        return lax.ppermute(block, "seq", [(i, i ^ bits) for i in range(self.size)])

    def column_swap(self, block, turn):
        return self.swap(block, turn * self.plane_size)

    def four_swap(self, block, turn):
        return self.swap(block, turn * self.rest)

    def exchange(self, blocks, groups):
        return lax.all_to_all(blocks, "seq", 0, 0, axis_index_groups=groups, tiled=True)


def project_kernel(x0, x1, x2, x3, weight, offset, query_ref, key_value_ref):
    for i, x in enumerate((x0, x1, x2, x3)):
        at = slice(i * ROWS, (i + 1) * ROWS)
        joined = (dot(x[...], weight[...]) + offset[...]).astype(BF16)
        query_ref[at, :] = joined[:, :WIDTH] * jnp.asarray(0.125, BF16)
        key_value_ref[at, :] = joined[:, WIDTH:]


def attend_kernel(pieces, chunks, *refs):
    q_ref = refs[0]
    key_value_refs, bias_refs = refs[1 : 1 + pieces], refs[1 + pieces : 1 + 2 * pieces]
    context_ref, log_ref = refs[1 + 2 * pieces : 3 + 2 * pieces]
    low_refs = refs[3 + 2 * pieces :]
    rows = q_ref.shape[0]
    chunk = key_value_refs[0].shape[0] // chunks
    for block in range(rows // ROWS):
        at = slice(block * ROWS, (block + 1) * ROWS)
        for head in range(GROUP_HEADS):
            columns = slice(head * HEAD_DIM, (head + 1) * HEAD_DIM)
            value_columns = slice(WIDTH + head * HEAD_DIM, WIDTH + (head + 1) * HEAD_DIM)
            query = q_ref[at, columns]

            def step(index, state):
                highest, total, mix = state
                here = pl.ds(pl.multiple_of(index * chunk, chunk), chunk)
                scores = [dot(query, k[here, columns], TURNED) + b[:, here] for k, b in zip(key_value_refs, bias_refs)]
                peak = functools.reduce(jnp.maximum, [jnp.max(s, axis=1, keepdims=True) for s in scores])
                raised = jnp.maximum(highest, peak)
                weights = [jnp.exp(s - raised) for s in scores]
                factor = jnp.exp(highest - raised)
                total = total * factor + sum(jnp.sum(w, axis=1, keepdims=True) for w in weights)
                mix = mix * factor + sum(
                    dot(w.astype(BF16), v[here, value_columns]) for w, v in zip(weights, key_value_refs)
                )
                return raised, total, mix

            state = (
                jnp.full((ROWS, 1), MASKED, F32),
                jnp.zeros((ROWS, 1), F32),
                jnp.zeros((ROWS, HEAD_DIM), F32),
            )
            highest, total, mix = step(0, state) if chunks == 1 else lax.fori_loop(0, chunks, step, state)
            context = mix / total
            context_ref[at, columns] = context
            low_refs[block][:, columns] = context.astype(BF16)
            log_ref[at, head : head + 1] = highest + jnp.log(total)


def attend(query, key_values, bias, chunks):
    rows = query.shape[0]
    outs = (shaped((rows, WIDTH), F32), shaped((rows, 128), F32)) + (shaped((ROWS, WIDTH)),) * GROUPS
    kernel = functools.partial(attend_kernel, len(key_values), chunks)
    found = kernel_call(kernel, "attend", outs, (query, *key_values, *bias), 24 if chunks == 1 else 60, 9)
    return found[0], found[1], found[2:]


def attend_grad_kernel(pieces, chunks, *refs):
    q_ref, context_ref, log_ref = refs[:3]
    grad_refs = refs[3:7]
    key_value_refs, bias_refs = refs[7 : 7 + pieces], refs[7 + pieces : 7 + 2 * pieces]
    query_grad_ref = refs[7 + 2 * pieces]
    outs = refs[8 + 2 * pieces :]
    if pieces == 4:
        own_key, own_value, turned_key, turned_value, key_x, value_y = outs
        key_outs = (own_key, key_x.at[0], turned_key, key_x.at[1])
        value_outs = (own_value, turned_value, value_y.at[0], value_y.at[1])
    else:
        key_outs, value_outs = outs[:1], outs[1:]
    rows = q_ref.shape[0]
    chunk = key_value_refs[0].shape[0] // chunks
    for head in range(GROUP_HEADS):
        columns = slice(head * HEAD_DIM, (head + 1) * HEAD_DIM)
        value_columns = slice(WIDTH + head * HEAD_DIM, WIDTH + (head + 1) * HEAD_DIM)
        query = q_ref[:, columns]
        grad = jnp.concatenate([g[:, columns] for g in grad_refs], axis=0)
        correction = jnp.sum(grad.astype(F32) * context_ref[:, columns], axis=1, keepdims=True)
        log_total = log_ref[:, head : head + 1]
        query_turned = query.T
        grad_turned = grad.T

        def step(index, query_grad):
            here = pl.ds(pl.multiple_of(index * chunk, chunk), chunk)
            for both, b, key_out, value_out in zip(key_value_refs, bias_refs, key_outs, value_outs):
                key = both[here, columns]
                probs = jnp.exp(dot(query, key, TURNED) + b[:, here] - log_total)
                probs_grad = dot(grad, both[here, value_columns], TURNED)
                score_grad = (probs * (probs_grad - correction)).astype(BF16)
                query_grad = query_grad + dot(score_grad, key)
                key_out[columns, here] = dot(query_turned, score_grad).astype(BF16)
                value_out[columns, here] = dot(grad_turned, probs.astype(BF16)).astype(BF16)
            return query_grad

        total = jnp.zeros((rows, HEAD_DIM), F32)
        total = step(0, total) if chunks == 1 else lax.fori_loop(0, chunks, step, total)
        query_grad_ref[:, columns] = (total * 0.125).astype(BF16)


def attend_grad(query, context, grads, log_total, key_values, bias, chunks):
    rows, keys = query.shape[0], key_values[0].shape[0]
    one, two = shaped((WIDTH, keys)), shaped((2, WIDTH, keys))
    outs = (shaped((rows, WIDTH)),) + ((one, one, one, one, two, two) if len(key_values) == 4 else (one, one))
    kernel = functools.partial(attend_grad_kernel, len(key_values), chunks)
    args = (query, context, log_total, *grads, *key_values, *bias)
    found = kernel_call(kernel, "attend_grad", outs, args, 32 if chunks == 1 else 60, 11)
    return found[0], found[1:]


def normalize(hidden):
    center = hidden - jnp.mean(hidden, axis=1, keepdims=True)
    scale = lax.rsqrt(jnp.mean(center * center, axis=1, keepdims=True) + EPSILON)
    return center * scale, scale


def normalize_grad(grad, normal, scale):
    return scale * (
        grad
        - jnp.mean(grad, axis=1, keepdims=True)
        - normal * jnp.mean(grad * normal, axis=1, keepdims=True)
    )


def column_sum(values):
    return jnp.sum(values, axis=0, keepdims=True)


TALL, SHORT, EXTRA = 96, 24, 8


def dense_kernel(width, spot, c0, c1, c2, c3, x_ref, grad_ref, vectors, up_offset, out_hbm, up_hbm, down_hbm, *rest):
    layer_ref, one_grad_ref = rest[:2]
    context_grads, up_parts, down_parts = rest[2:6], rest[6:10], rest[10:14]
    out_w, up_w, down_w, slope, active_ref, inner_ref, sums_ref, sems = rest[14:]
    copies = [
        pltpu.make_async_copy(source, target, sems.at[i])
        for i, (source, target) in enumerate(((out_hbm, out_w), (up_hbm, up_w), (down_hbm, down_w)))
    ]
    for copy in copies:
        copy.start()
    hidden = up_w.shape[1]
    half = width // 2
    out_offset, gain_one, shift_one, down_offset, gain_two, shift_two = (vectors[i : i + 1, :] for i in range(2, 8))
    group, quarter = spot[0], spot[1]
    contexts = (c0, c1, c2, c3)

    def turned(i):
        return pl.ds(pl.multiple_of((group ^ i) * WIDTH, WIDTH), WIDTH)

    copies[0].wait()
    branch = sum(dot(c[...], out_w[turned(i), :]) for i, c in enumerate(contexts)) + out_offset
    normal_one, scale_one = normalize(x_ref[...].astype(F32) + branch)
    normed_low = (normal_one * gain_one + shift_one).astype(BF16)
    for ref in up_parts:
        ref[:, :width] = normed_low
    copies[1].wait()
    copies[2].wait()
    step = 768
    second = jnp.zeros((ROWS, width), F32) + down_offset
    for start in range(0, hidden, step):
        at = slice(start, start + step)
        inner = dot(normed_low, up_w[:, at]) + up_offset[:, at]
        share = 0.5 + 0.5 * lax.erf(inner * 0.7071067811865476)
        density = 0.3989422804014327 * jnp.exp(-0.5 * inner * inner)
        slope[:, at] = share + inner * density
        active = (inner * share).astype(BF16)
        active_ref[:, at] = active
        second = second + dot(active, down_w[at, :])
    normal_two, scale_two = normalize(normed_low.astype(F32) + second)
    layer_ref[...] = (normal_two * gain_two + shift_two).astype(BF16)
    grad = grad_ref[...].astype(F32)
    gain_two_grad, shift_two_grad = column_sum(grad * normal_two), column_sum(grad)
    two_grad = normalize_grad(grad * gain_two, normal_two, scale_two)
    second_low = two_grad.astype(BF16)
    down_bias_grad = column_sum(second_low.astype(F32))
    normed_grad = two_grad
    for start in range(0, hidden, step):
        at = slice(start, start + step)
        inner_low = (dot(second_low, down_w[at, :], TURNED) * slope[:, at]).astype(BF16)
        inner_ref[:, at] = inner_low
        up_sum = column_sum(inner_low.astype(F32))
        for piece in range(step // half):
            place = start // half + piece
            per_core = hidden // 2 // half
            row, core = 6 + place % per_core, place // per_core
            sums_ref[row : row + 1, core * half : (core + 1) * half] = up_sum[:, piece * half : (piece + 1) * half]
        normed_grad = normed_grad + dot(inner_low, up_w[:, at], TURNED)
    gain_one_grad, shift_one_grad = column_sum(normed_grad * normal_one), column_sum(normed_grad)
    one_grad = normalize_grad(normed_grad * gain_one, normal_one, scale_one)
    one_grad_ref[...] = one_grad
    branch_low = one_grad.astype(BF16)
    for i, ref in enumerate(context_grads):
        ref[...] = dot(branch_low, out_w[turned(i), :], TURNED).astype(BF16)
    out_bias_grad = column_sum(branch_low.astype(F32))
    sums = (out_bias_grad, gain_one_grad, shift_one_grad, down_bias_grad, gain_two_grad, shift_two_grad)
    for i, total in enumerate(sums):
        sums_ref[i : i + 1, :] = total
    sums_ref[10:16, :] = jnp.zeros((6, width), F32)
    share = hidden // 8
    for i in range(4):
        for core in range(2):
            at = pl.ds(pl.multiple_of(core * (hidden // 2) + (quarter ^ i) * share, share), share)
            to = slice(width + core * share, width + (core + 1) * share)
            up_parts[i][:, to] = inner_ref[:, at]
            down_parts[i][:ROWS, to] = active_ref[:, at]
        down_parts[i][:ROWS, :width] = second_low
        down_parts[i][:ROWS, 2 * width : 3 * width] = branch_low
        down_parts[i][ROWS:, :width] = sums_ref[...].astype(BF16)
    strip = width // 8
    for i, c in enumerate(contexts):
        for g in range(GROUPS):
            @pl.when((group ^ i) == g)
            def _():
                for part in range(2):
                    core, owner = divmod((g * WIDTH + part * strip) // strip, 4)
                    for turn in range(4):
                        @pl.when((quarter ^ turn) == owner)
                        def _():
                            to = 3 * width + core * strip
                            down_parts[turn][:ROWS, to : to + strip] = c[:, part * strip : (part + 1) * strip]


def dense(spot, contexts, inputs, grad, vectors, up_offset, out_matrix, up_matrix, down_matrix):
    width, hidden = up_matrix.shape
    outs = (
        (shaped((ROWS, width)), shaped((ROWS, width), F32))
        + (shaped((ROWS, WIDTH)),) * GROUPS
        + (shaped((ROWS, width + hidden // 4)),) * 4
        + (shaped((ROWS + 16, 3 * width + 256)),) * 4
    )
    scratch = (
        pltpu.VMEM(out_matrix.shape, BF16),
        pltpu.VMEM(up_matrix.shape, BF16),
        pltpu.VMEM(down_matrix.shape, BF16),
        pltpu.VMEM((ROWS, hidden), F32),
        pltpu.VMEM((ROWS, hidden), BF16),
        pltpu.VMEM((ROWS, hidden), BF16),
        pltpu.VMEM((16, width), F32),
        pltpu.SemaphoreType.DMA((3,)),
    )
    args = (spot, *contexts, inputs, grad, vectors, up_offset, out_matrix, up_matrix, down_matrix)
    found = kernel_call(
        functools.partial(dense_kernel, width), "dense", outs, args, 22, 10, 1, (9, 10, 11), scratch
    )
    return found[0], found[1], found[2:6], found[6:10], found[10:14]


def halves_of(spot, first, second):
    return ((first, 1 - spot[2]), (second, spot[2]))


def up_grad_kernel(spot, p0, p1, p2, p3, other_ref, own_ref, turned, inner):
    width = turned.shape[0]
    for i, part in enumerate((p0, p1, p2, p3)):
        turned[:, i * ROWS : (i + 1) * ROWS] = part[:, :width].T
        inner[i * ROWS : (i + 1) * ROWS, :] = part[:, width:]
    half = width // 2
    for ref, core in halves_of(spot, other_ref, own_ref):
        value = dot(turned[pl.ds(pl.multiple_of(core * half, half), half), :], inner[...]).astype(BF16)
        for g in range(GROUPS):
            ref[g] = value[g * TALL : (g + 1) * TALL]


def up_grad_parts(spot, parts, width):
    tokens, columns = 4 * ROWS, parts[0].shape[1] - width
    out = shaped((GROUPS, TALL, columns))
    scratch = (pltpu.VMEM((width, tokens), BF16), pltpu.VMEM((tokens, columns), BF16))
    return kernel_call(up_grad_kernel, "up_grad", (out, out), (spot, *parts), 16, 4, 1, (), scratch)


def down_grad_kernel(spot, p0, p1, p2, p3, other_ref, own_ref, turned, second, branch, sums):
    parts = (p0, p1, p2, p3)
    width = second.shape[1]
    tall, strip = GROUPS * TALL, GROUPS * SHORT
    for i, part in enumerate(parts):
        rows = slice(i * ROWS, (i + 1) * ROWS)
        turned[: 2 * tall, rows] = part[:ROWS, width : 2 * width].T
        turned[2 * tall : 2 * tall + 256, rows] = part[:ROWS, 3 * width :].T
        second[rows, :] = part[:ROWS, :width]
        branch[rows, :] = part[:ROWS, 2 * width : 3 * width]
    total = sum(part[ROWS:, :width].astype(F32) for part in parts)
    for core in range(2):
        start = core * (width // 2)
        sums[core] = jnp.concatenate(
            [total[:EXTRA, start : start + width // 2], total[EXTRA:, start : start + width // 2]], axis=1
        )
    for ref, core in halves_of(spot, other_ref, own_ref):
        down = dot(turned[pl.ds(pl.multiple_of(core * tall, tall), tall), :], second[...])
        out = dot(turned[pl.ds(pl.multiple_of(2 * tall + core * strip, 32), strip), :], branch[...])
        for g in range(GROUPS):
            ref[g] = jnp.concatenate(
                [down[g * TALL : (g + 1) * TALL], out[g * SHORT : (g + 1) * SHORT], sums[core]], axis=0
            ).astype(BF16)


def down_grad_parts(spot, parts, width):
    tokens = 4 * ROWS
    out = shaped((GROUPS, TALL + SHORT + EXTRA, width))
    scratch = (
        pltpu.VMEM((2 * GROUPS * TALL + 256, tokens), BF16),
        pltpu.VMEM((tokens, width), BF16),
        pltpu.VMEM((tokens, width), BF16),
        pltpu.VMEM((2, EXTRA, width), F32),
    )
    return kernel_call(down_grad_kernel, "down_grad", (out, out), (spot, *parts), 16, 5, 1, (), scratch)


def pair_sum_kernel(which, turns, spot, own, received, kept, sent):
    for i, out in zip(turns, (sent.at[0], sent.at[1], kept.at[1], kept.at[0])):
        at = spot[which] ^ i
        out[...] = (own[at].astype(F32) + received[at].astype(F32)).astype(BF16)


def pair_sums(spot, own, received, name, which=0, turns=(1, 2, 3, 0)):
    pair = shaped((2, *own.shape[1:]))
    kernel = functools.partial(pair_sum_kernel, which, turns)
    return kernel_call(kernel, name, (pair, pair), (spot, own, received), 16, 2, 1)


def placed(spot, pieces):
    group, quarter = spot[0], spot[1]
    for i in range(4):
        for g in range(GROUPS):
            turn = group ^ g
            at = ((turn & 1) << 1) ^ ((turn >> 1) * 3)
            if i < 3:
                block = pieces[i][at]
            else:
                block = jnp.where(at < 2, pieces[3][at & 1], pieces[4][at & 1])
            yield quarter ^ i, g, block


def place_up_kernel(spot, *refs):
    up_ref = refs[-1]
    for quarter, g, block in placed(spot, refs[:-1]):
        share = block.shape[1] // 2
        block = block.astype(F32)
        for core in range(2):
            at = pl.ds(pl.multiple_of(core * 4 * share + quarter * share, 128), share)
            up_ref[g * TALL : (g + 1) * TALL, at] = block[:, core * share : (core + 1) * share]


BIAS_ROWS = 16


def joined_grad_kernel(pieces, spot, query_grad, *rest):
    keys, values = rest[:pieces], rest[pieces : 2 * pieces]
    inputs = rest[2 * pieces : 2 * pieces + 4]
    weight, other_ref, own_ref, kept_ref, sent_ref, joined, turned = rest[2 * pieces + 4 :]

    def total(parts):
        blocks = [p[0] if len(p.shape) == 3 else p[...] for p in parts]
        return sum(b.astype(F32) for b in blocks).T.astype(BF16)

    joined[:, :WIDTH] = query_grad[...]
    joined[:, WIDTH : 2 * WIDTH] = total(keys)
    joined[:, 2 * WIDTH :] = total(values)
    for i, ref in ((1, sent_ref.at[0]), (2, sent_ref.at[1]), (3, kept_ref.at[1]), (0, kept_ref.at[0])):
        ref[...] = dot(joined[i * ROWS : (i + 1) * ROWS, :], weight[...], TURNED).astype(BF16)
    for i, x in enumerate(inputs):
        turned[:, i * ROWS : (i + 1) * ROWS] = x[...].T
    sums = jnp.concatenate(
        [column_sum(joined[...].astype(F32)), jnp.zeros((BIAS_ROWS - 1, 3 * WIDTH), F32)], axis=0
    ).astype(BF16)
    half = turned.shape[0] // 2
    for ref, core in halves_of(spot, other_ref, own_ref):
        value = dot(turned[pl.ds(pl.multiple_of(core * half, half), half), :], joined[...]).astype(BF16)
        for quarter in range(4):
            ref[quarter, : half // 4, :] = value[quarter * (half // 4) : (quarter + 1) * (half // 4)]
            ref[quarter, half // 4 :, :] = sums


def joined_grads(spot, query_grad, keys, values, inputs, weight):
    width = weight.shape[0]
    part, pair = shaped((4, width // 8 + BIAS_ROWS, 3 * WIDTH)), shaped((2, ROWS, width))
    scratch = (pltpu.VMEM((GROUPS * ROWS, 3 * WIDTH), BF16), pltpu.VMEM((width, GROUPS * ROWS), BF16))
    args = (spot, query_grad, *keys, *values, *inputs, weight)
    kernel = functools.partial(joined_grad_kernel, len(keys))
    return kernel_call(kernel, "joined_grad", (part, part, pair, pair), args, 16, 6, 1, (), scratch)


def place_down_kernel(spot, *refs):
    down_ref, out_ref = refs[-2:]
    for quarter, g, block in placed(spot, refs[:-2]):
        block = block.astype(F32)
        place = quarter * GROUPS + g
        down_ref[pl.ds(pl.multiple_of(place * TALL, 8), TALL), :] = block[:TALL]
        out_ref[pl.ds(pl.multiple_of(place * SHORT, 8), SHORT), :] = block[TALL : TALL + SHORT]


def place_joined_kernel(spot, *refs):
    weight_ref, bias_ref = refs[-2:]
    core = spot[2]
    width = weight_ref.shape[1] // 3
    found = list(placed(spot, refs[:-2]))
    for i in range(4):
        quarter = found[i * GROUPS][0]
        blocks = [block.astype(F32) for _, _, block in found[i * GROUPS : (i + 1) * GROUPS]]
        rows = blocks[0].shape[0] - BIAS_ROWS
        at = pl.ds(pl.multiple_of(quarter * rows, 16), rows)
        for part in range(3):
            value = jnp.concatenate([b[:, part * WIDTH : (part + 1) * WIDTH] for b in blocks], axis=1)
            weight_ref[at, part * width : (part + 1) * width] = value[:rows]
            if i == 0:
                line = value[rows : rows + 1]
                bias_ref[part : part + 1, :] = jnp.where(core == 0, line[:, : width // 2], line[:, width // 2 :])


def body(
    tokens,
    cotangent,
    lengths,
    qkv_weight,
    query_bias,
    value_bias,
    out_weight,
    out_bias,
    first_gain,
    first_shift,
    up_weight,
    up_bias,
    down_weight,
    down_bias,
    second_gain,
    second_shift,
):
    row_count, model_width = tokens.shape[1], tokens.shape[2]
    hidden_width = up_weight.shape[1]
    places = Places(lax.axis_size("seq"))
    plane_size, rest = places.plane_size, places.rest
    rank = lax.axis_index("seq")
    core = lax.axis_index("shard")
    group, position = rank // plane_size, rank % plane_size
    quarter = position // rest
    spot = jnp.stack([group, quarter, core]).astype(jnp.int32)
    length = lengths[core]
    inputs = tokens[0]
    column_rows = GROUPS * row_count
    half = model_width // 2
    turns = range(1, GROUPS)

    column_inputs = (inputs, *(places.column_swap(inputs, i) for i in turns))

    def both(block):
        return lax.all_gather(block, "shard", axis=0, tiled=True)

    def own_columns(w):
        at = group * WIDTH
        parts = [lax.dynamic_slice_in_dim(w, at + i * model_width, WIDTH, w.ndim - 1) for i in range(3)]
        return jnp.concatenate(parts, axis=-1)

    group_weight = both(own_columns(qkv_weight))
    vectors = [query_bias, value_bias, out_bias, first_gain, first_shift, down_bias, second_gain, second_shift]
    stacked = jnp.concatenate([jnp.stack(vectors), up_bias.reshape(-1, half)])
    stacked = lax.all_gather(stacked, "shard", axis=0).astype(F32)
    whole = jnp.transpose(stacked[:, : len(vectors)], (1, 0, 2)).reshape(len(vectors), model_width)
    up_offset = stacked[:, len(vectors) :].reshape(1, hidden_width)
    out_matrix = in_hbm(both(out_weight))
    up_matrix = in_hbm(both(up_weight))
    down_matrix = in_hbm(both(down_weight))

    offset = own_columns(jnp.concatenate([whole[0], jnp.zeros_like(whole[0]), whole[1]])).reshape(1, -1)
    query, key_value = kernel_call(
        project_kernel,
        "project",
        (shaped((column_rows, WIDTH)), shaped((column_rows, 2 * WIDTH))),
        (*column_inputs, group_weight, offset),
        16,
        2,
    )

    def masks(who):
        groups = group ^ jnp.arange(GROUPS)
        starts = (groups[None, :] * plane_size + who[:, None]) * row_count
        tokens_at = starts[:, :, None] + jnp.arange(row_count)
        return jnp.where(tokens_at.reshape(1, -1) < length, 0.0, MASKED).astype(F32)

    if plane_size == 4:
        chunks = 1
        key_values = (key_value, *(places.swap(key_value, i) for i in turns))
        bias = tuple(masks((position ^ i)[None]) for i in range(4))
    else:
        chunks = plane_size // 4
        gathered = lax.all_gather(key_value, "seq", axis=0, axis_index_groups=places.planes)
        key_values = (gathered.reshape(-1, 2 * WIDTH),)
        bias = (masks(jnp.arange(plane_size)),)
    context, log_total, context_lows = attend(query, key_values, bias, chunks)
    contexts = (context_lows[0], *(places.column_swap(context_lows[i], i) for i in turns))

    layer_out, one_grad, context_grads, up_parts, down_parts = dense(
        spot, contexts, inputs, cotangent[0], whole, up_offset, out_matrix, up_matrix, down_matrix
    )
    def after(value, *others):
        return lax.optimization_barrier((value, *others))[0]

    def to_other(block):
        return lax.ppermute(block, "shard", [(0, 1), (1, 0)])

    def rest_sum(total):
        return lax.psum(total, "seq", axis_index_groups=places.rests) if rest > 1 else total

    def add(left, right):
        return (left.astype(F32) + right.astype(F32)).astype(BF16)

    def column_total(kept, sent):
        near = places.column_swap(sent, 1)
        far = places.column_swap(add(kept[1], near[1]), 3)
        return kept[0].astype(F32) + near[0].astype(F32) + far.astype(F32)

    def four_total(kept, sent):
        near = places.four_swap(sent, 1)
        far = places.four_swap(add(kept[1], near[1]), 2)
        return kept[0].astype(F32) + near[0].astype(F32) + far.astype(F32)

    def column_gather(part):
        pair = jnp.stack([part, places.column_swap(part, 3)])
        return jnp.concatenate([pair, places.column_swap(pair, 1)])

    def plane_gather(column):
        first, second = places.four_swap(column, 1), places.four_swap(column, 2)
        return column, first, second, places.four_swap(first[:2], 2), places.four_swap(second[2:], 1)

    context_grads = (context_grads[0], *(places.column_swap(context_grads[i], i) for i in turns))
    down_parts = (down_parts[0], *(places.four_swap(down_parts[i], i) for i in turns))
    query_grad, parts = attend_grad(query, context, context_grads, log_total, key_values, bias, chunks)
    if plane_size == 4:
        own_key, own_value, turned_key, turned_value, key_x, value_y = parts
        key_x, value_y = places.swap(key_x, 1), places.swap(value_y, 2)
        keys = (own_key, key_x, places.swap(add(turned_key, key_x[1]), 2))
        values = (own_value, value_y, places.swap(add(turned_value, value_y[1]), 1))
    else:
        blocks = jnp.stack(parts).reshape(2 * WIDTH, plane_size, column_rows)
        blocks = places.exchange(jnp.transpose(blocks, (1, 0, 2)), places.planes)
        blocks = jnp.sum(blocks.astype(F32), axis=0)
        keys, values = (blocks[:WIDTH],), (blocks[WIDTH:],)
    down_parts = after(down_parts, query_grad)
    other, own = down_grad_parts(spot, down_parts, model_width)
    down_part = rest_sum(column_total(*pair_sums(spot, own, to_other(other), "down_sum")))
    keys, values = after((keys, values), down_part)
    down_column = column_gather(down_part[: TALL + SHORT].astype(BF16))
    other, own, kept, sent = joined_grads(spot, query_grad, keys, values, column_inputs, group_weight)
    input_grad = one_grad + column_total(kept, sent)
    joined_pieces = pair_sums(spot, own, to_other(other), "joined_sum", 1, (1, 3, 2, 0))
    joined_part = rest_sum(four_total(*joined_pieces)).astype(BF16)
    up_parts = after(up_parts, down_parts)
    up_parts = (up_parts[0], *(places.four_swap(up_parts[i], i) for i in turns))
    up_parts = after(up_parts, kept, down_column)
    other, own = up_grad_parts(spot, up_parts, model_width)
    up_part = rest_sum(column_total(*pair_sums(spot, own, to_other(other), "up_sum"))).astype(BF16)
    down_all = plane_gather(down_column)
    up_all = plane_gather(after(column_gather(up_part), down_all))
    joined_all = plane_gather(after(column_gather(joined_part), down_all))
    extra = down_part[TALL + SHORT :]
    up_bias_grad = jnp.concatenate([extra[6, :half], extra[7, :half], extra[0, half:], extra[1, half:]])
    down_grad, out_grad = kernel_call(
        place_down_kernel,
        "place_down",
        (shaped((hidden_width // 2, model_width), F32), shaped((half, model_width), F32)),
        (spot, *down_all),
        16,
        5,
        1,
    )
    qkv_grad, bias_grad = kernel_call(
        place_joined_kernel,
        "place_joined",
        (shaped((half, 3 * model_width), F32), shaped((8, half), F32)),
        (spot, *joined_all),
        16,
        5,
        1,
    )
    up_grad = kernel_call(
        place_up_kernel,
        "place_up",
        shaped((half, hidden_width), F32),
        (spot, *up_all),
        16,
        4,
        1,
    )

    shape = (1, row_count, model_width)
    return (
        layer_out.reshape(shape),
        input_grad.reshape(shape),
        qkv_grad,
        bias_grad[0],
        bias_grad[2],
        out_grad,
        extra[0, :half],
        extra[1, :half],
        extra[2, :half],
        up_grad,
        up_bias_grad,
        down_grad,
        extra[3, :half],
        extra[4, :half],
        extra[5, :half],
    )


def solution(mesh):
    rows, halves, whole = P("shard", "seq", None), P("shard", None), P("shard")
    in_specs = (rows, rows, P(), halves, whole, whole, halves, whole, whole, whole, halves, whole, halves, whole, whole, whole)
    out_specs = (rows, rows, halves, whole, whole, halves, whole, whole, whole, halves, whole, halves, whole, whole, whole)
    return jax.shard_map(body, mesh=mesh, in_specs=in_specs, out_specs=out_specs, check_vma=False)
```

```python
import functools

import jax
import jax.numpy as jnp
from jax import lax
from jax.experimental import pallas as pl
from jax.experimental.pallas import tpu as pltpu
from jax.sharding import PartitionSpec as P

HEADS = 12
HEAD_DIM = 64
GROUPS = 4
GROUP_HEADS = HEADS // GROUPS
WIDTH = GROUP_HEADS * HEAD_DIM
EPSILON = 1e-12
MASKED = -1e30
F32 = jnp.float32
BF16 = jnp.bfloat16
MIB = 2**20
ROWS = 128
TURNED = ((1,), (1,))
FIRST = ((1,), (0,))


def dot(left, right, dims=FIRST):
    return lax.dot_general(left, right, (dims, ((), ())), preferred_element_type=F32)


def kernel_call(kernel, name, outs, args, vmem, micros, smem=0, left=(), scratch=(), after=()):
    spaces = [
        pl.BlockSpec(memory_space=pltpu.SMEM if i < smem else pltpu.HBM if i in left else pltpu.VMEM)
        for i in range(len(args))
    ]
    count = len(args)

    def run(*refs):
        kernel(*refs[:count], *refs[count + len(after) :])

    return pl.pallas_call(
        run if after else kernel,
        out_shape=outs,
        in_specs=spaces + [pl.BlockSpec(memory_space=pl.ANY)] * len(after),
        scratch_shapes=list(scratch),
        compiler_params=pltpu.CompilerParams(vmem_limit_bytes=vmem * MIB),
        cost_estimate=pl.CostEstimate(flops=0, bytes_accessed=int(micros * 3_500_000), transcendentals=0),
        name=name,
    )(*args, *after)


def in_hbm(array):
    return pltpu.with_memory_space_constraint(array, pltpu.HBM)


def shaped(shape, dtype=BF16):
    return jax.ShapeDtypeStruct(shape, dtype)


class Places:
    def __init__(self, size):
        self.size = size
        self.plane_size = size // GROUPS
        self.rest = self.plane_size // 4
        index = lambda g, q, m: (g * 4 + q) * self.rest + m
        groups, quarters, members = range(GROUPS), range(4), range(self.rest)
        self.columns = [[index(g, q, m) for g in groups] for q in quarters for m in members]
        self.planes = [[index(g, q, m) for q in quarters for m in members] for g in groups]
        self.fours = [[index(g, q, m) for q in quarters] for g in groups for m in members]
        self.sixteens = [[index(g, q, m) for g in groups for q in quarters] for m in members]
        self.rests = [[index(g, q, m) for m in members] for g in groups for q in quarters]

    def swap(self, block, bits):
        return lax.ppermute(block, "seq", [(i, i ^ bits) for i in range(self.size)])

    def column_swap(self, block, turn):
        return self.swap(block, turn * self.plane_size)

    def four_swap(self, block, turn):
        return self.swap(block, turn * self.rest)

    def exchange(self, blocks, groups):
        return lax.all_to_all(blocks, "seq", 0, 0, axis_index_groups=groups, tiled=True)


def project_kernel(x0, x1, x2, x3, weight, offset, query_ref, key_value_ref):
    for i, x in enumerate((x0, x1, x2, x3)):
        at = slice(i * ROWS, (i + 1) * ROWS)
        joined = (dot(x[...], weight[...]) + offset[...]).astype(BF16)
        query_ref[at, :] = joined[:, :WIDTH] * jnp.asarray(0.125, BF16)
        key_value_ref[at, :] = joined[:, WIDTH:]


def attend_kernel(pieces, chunks, *refs):
    q_ref = refs[0]
    key_value_refs, bias_refs = refs[1 : 1 + pieces], refs[1 + pieces : 1 + 2 * pieces]
    context_ref, log_ref = refs[1 + 2 * pieces : 3 + 2 * pieces]
    low_refs = refs[3 + 2 * pieces :]
    rows = q_ref.shape[0]
    chunk = key_value_refs[0].shape[0] // chunks
    for block in range(rows // ROWS):
        at = slice(block * ROWS, (block + 1) * ROWS)
        for head in range(GROUP_HEADS):
            columns = slice(head * HEAD_DIM, (head + 1) * HEAD_DIM)
            value_columns = slice(WIDTH + head * HEAD_DIM, WIDTH + (head + 1) * HEAD_DIM)
            query = q_ref[at, columns]

            def step(index, state):
                highest, total, mix = state
                here = pl.ds(pl.multiple_of(index * chunk, chunk), chunk)
                scores = [dot(query, k[here, columns], TURNED) + b[:, here] for k, b in zip(key_value_refs, bias_refs)]
                peak = functools.reduce(jnp.maximum, [jnp.max(s, axis=1, keepdims=True) for s in scores])
                raised = jnp.maximum(highest, peak)
                weights = [jnp.exp(s - raised) for s in scores]
                factor = jnp.exp(highest - raised)
                total = total * factor + sum(jnp.sum(w, axis=1, keepdims=True) for w in weights)
                mix = mix * factor + sum(
                    dot(w.astype(BF16), v[here, value_columns]) for w, v in zip(weights, key_value_refs)
                )
                return raised, total, mix

            state = (
                jnp.full((ROWS, 1), MASKED, F32),
                jnp.zeros((ROWS, 1), F32),
                jnp.zeros((ROWS, HEAD_DIM), F32),
            )
            highest, total, mix = step(0, state) if chunks == 1 else lax.fori_loop(0, chunks, step, state)
            context = mix / total
            context_ref[at, columns] = context
            low_refs[block][:, columns] = context.astype(BF16)
            log_ref[at, head : head + 1] = highest + jnp.log(total)


def attend(query, key_values, bias, chunks):
    rows = query.shape[0]
    outs = (shaped((rows, WIDTH), F32), shaped((rows, 128), F32)) + (shaped((ROWS, WIDTH)),) * GROUPS
    kernel = functools.partial(attend_kernel, len(key_values), chunks)
    found = kernel_call(kernel, "attend", outs, (query, *key_values, *bias), 24 if chunks == 1 else 60, 9)
    return found[0], found[1], found[2:]


def attend_grad_kernel(pieces, chunks, *refs):
    q_ref, context_ref, log_ref = refs[:3]
    grad_refs = refs[3:7]
    key_value_refs, bias_refs = refs[7 : 7 + pieces], refs[7 + pieces : 7 + 2 * pieces]
    query_grad_ref = refs[7 + 2 * pieces]
    outs = refs[8 + 2 * pieces :]
    if pieces == 4:
        own_key, own_value, turned_key, turned_value, key_x, value_y = outs
        key_outs = (own_key, key_x.at[0], turned_key, key_x.at[1])
        value_outs = (own_value, turned_value, value_y.at[0], value_y.at[1])
    else:
        key_outs, value_outs = outs[:1], outs[1:]
    rows = q_ref.shape[0]
    chunk = key_value_refs[0].shape[0] // chunks
    for head in range(GROUP_HEADS):
        columns = slice(head * HEAD_DIM, (head + 1) * HEAD_DIM)
        value_columns = slice(WIDTH + head * HEAD_DIM, WIDTH + (head + 1) * HEAD_DIM)
        query = q_ref[:, columns]
        grad = jnp.concatenate([g[:, columns] for g in grad_refs], axis=0)
        correction = jnp.sum(grad.astype(F32) * context_ref[:, columns], axis=1, keepdims=True)
        log_total = log_ref[:, head : head + 1]
        query_turned = query.T
        grad_turned = grad.T

        def step(index, query_grad):
            here = pl.ds(pl.multiple_of(index * chunk, chunk), chunk)
            for both, b, key_out, value_out in zip(key_value_refs, bias_refs, key_outs, value_outs):
                key = both[here, columns]
                probs = jnp.exp(dot(query, key, TURNED) + b[:, here] - log_total)
                probs_grad = dot(grad, both[here, value_columns], TURNED)
                score_grad = (probs * (probs_grad - correction)).astype(BF16)
                query_grad = query_grad + dot(score_grad, key)
                key_out[columns, here] = dot(query_turned, score_grad).astype(BF16)
                value_out[columns, here] = dot(grad_turned, probs.astype(BF16)).astype(BF16)
            return query_grad

        total = jnp.zeros((rows, HEAD_DIM), F32)
        total = step(0, total) if chunks == 1 else lax.fori_loop(0, chunks, step, total)
        query_grad_ref[:, columns] = (total * 0.125).astype(BF16)


def attend_grad(query, context, grads, log_total, key_values, bias, chunks):
    rows, keys = query.shape[0], key_values[0].shape[0]
    one, two = shaped((WIDTH, keys)), shaped((2, WIDTH, keys))
    outs = (shaped((rows, WIDTH)),) + ((one, one, one, one, two, two) if len(key_values) == 4 else (one, one))
    kernel = functools.partial(attend_grad_kernel, len(key_values), chunks)
    args = (query, context, log_total, *grads, *key_values, *bias)
    found = kernel_call(kernel, "attend_grad", outs, args, 32 if chunks == 1 else 60, 11)
    return found[0], found[1:]


def normalize(hidden):
    center = hidden - jnp.mean(hidden, axis=1, keepdims=True)
    scale = lax.rsqrt(jnp.mean(center * center, axis=1, keepdims=True) + EPSILON)
    return center * scale, scale


def normalize_grad(grad, normal, scale):
    return scale * (
        grad
        - jnp.mean(grad, axis=1, keepdims=True)
        - normal * jnp.mean(grad * normal, axis=1, keepdims=True)
    )


def column_sum(values):
    return jnp.sum(values, axis=0, keepdims=True)


TALL, SHORT, EXTRA = 96, 24, 8
PACKED = 32


def dense_kernel(width, spot, c0, c1, c2, c3, x_ref, grad_ref, vectors, up_offset, out_hbm, up_hbm, down_hbm, *rest):
    layer_ref, one_grad_ref = rest[:2]
    branch_ref = rest[2]
    context_grads, up_parts, down_parts = rest[3:7], rest[7:11], rest[11:15]
    out_w, up_w, down_w, slope, active_ref, inner_ref, sums_ref, sems = rest[15:]
    copies = [
        pltpu.make_async_copy(source, target, sems.at[i])
        for i, (source, target) in enumerate(((out_hbm, out_w), (up_hbm, up_w), (down_hbm, down_w)))
    ]
    for copy in copies:
        copy.start()
    hidden = up_w.shape[1]
    half = width // 2
    out_offset, gain_one, shift_one, down_offset, gain_two, shift_two = (vectors[i : i + 1, :] for i in range(2, 8))
    group, quarter = spot[0], spot[1]
    contexts = (c0, c1, c2, c3)

    def turned(i):
        return pl.ds(pl.multiple_of((group ^ i) * WIDTH, WIDTH), WIDTH)

    copies[0].wait()
    branch = sum(dot(c[...], out_w[turned(i), :]) for i, c in enumerate(contexts)) + out_offset
    normal_one, scale_one = normalize(x_ref[...].astype(F32) + branch)
    normed_low = (normal_one * gain_one + shift_one).astype(BF16)
    for ref in up_parts:
        ref[:, :width] = normed_low
    copies[1].wait()
    step = 768
    for start in range(0, hidden, step):
        at = slice(start, start + step)
        inner = dot(normed_low, up_w[:, at]) + up_offset[:, at]
        share = 0.5 + 0.5 * lax.erf(inner * 0.7071067811865476)
        density = 0.3989422804014327 * jnp.exp(-0.5 * inner * inner)
        slope[:, at] = share + inner * density
        active_ref[:, at] = (inner * share).astype(BF16)
    copies[2].wait()
    second = dot(active_ref[...], down_w[...]) + down_offset
    normal_two, scale_two = normalize(normed_low.astype(F32) + second)
    layer_ref[...] = (normal_two * gain_two + shift_two).astype(BF16)
    grad = grad_ref[...].astype(F32)
    gain_two_grad, shift_two_grad = column_sum(grad * normal_two), column_sum(grad)
    two_grad = normalize_grad(grad * gain_two, normal_two, scale_two)
    second_low = two_grad.astype(BF16)
    down_bias_grad = column_sum(second_low.astype(F32))
    normed_grad = two_grad
    for start in range(0, hidden, step):
        at = slice(start, start + step)
        inner_low = (dot(second_low, down_w[at, :], TURNED) * slope[:, at]).astype(BF16)
        inner_ref[:, at] = inner_low
        up_sum = column_sum(inner_low.astype(F32))
        for piece in range(step // half):
            place = start // half + piece
            per_core = hidden // 2 // half
            row, core = 6 + place % per_core, place // per_core
            sums_ref[row : row + 1, core * half : (core + 1) * half] = up_sum[:, piece * half : (piece + 1) * half]
        normed_grad = normed_grad + dot(inner_low, up_w[:, at], TURNED)
    gain_one_grad, shift_one_grad = column_sum(normed_grad * normal_one), column_sum(normed_grad)
    one_grad = normalize_grad(normed_grad * gain_one, normal_one, scale_one)
    one_grad_ref[...] = one_grad
    branch_low = one_grad.astype(BF16)
    branch_ref[...] = branch_low
    for i, ref in enumerate(context_grads):
        ref[...] = dot(branch_low, out_w[turned(i), :], TURNED).astype(BF16)
    out_bias_grad = column_sum(branch_low.astype(F32))
    sums = (out_bias_grad, gain_one_grad, shift_one_grad, down_bias_grad, gain_two_grad, shift_two_grad)
    for i, total in enumerate(sums):
        sums_ref[i : i + 1, :] = total
    sums_ref[10:16, :] = jnp.zeros((6, width), F32)
    share = hidden // 8
    for i in range(4):
        for core in range(2):
            at = pl.ds(pl.multiple_of(core * (hidden // 2) + (quarter ^ i) * share, share), share)
            to = slice(width + core * share, width + (core + 1) * share)
            up_parts[i][:, to] = inner_ref[:, at]
            down_parts[i][:ROWS, to] = active_ref[:, at]
        down_parts[i][:ROWS, :width] = second_low
        down_parts[i][ROWS:, :width] = sums_ref[...].astype(BF16)


def dense(spot, contexts, inputs, grad, vectors, up_offset, out_matrix, up_matrix, down_matrix):
    width, hidden = up_matrix.shape
    outs = (
        (shaped((ROWS, width)), shaped((ROWS, width), F32), shaped((ROWS, width)))
        + (shaped((ROWS, WIDTH)),) * GROUPS
        + (shaped((ROWS, width + hidden // 4)),) * 4
        + (shaped((ROWS + 16, width + hidden // 4)),) * 4
    )
    scratch = (
        pltpu.VMEM(out_matrix.shape, BF16),
        pltpu.VMEM(up_matrix.shape, BF16),
        pltpu.VMEM(down_matrix.shape, BF16),
        pltpu.VMEM((ROWS, hidden), F32),
        pltpu.VMEM((ROWS, hidden), BF16),
        pltpu.VMEM((ROWS, hidden), BF16),
        pltpu.VMEM((16, width), F32),
        pltpu.SemaphoreType.DMA((3,)),
    )
    args = (spot, *contexts, inputs, grad, vectors, up_offset, out_matrix, up_matrix, down_matrix)
    found = kernel_call(
        functools.partial(dense_kernel, width), "dense", outs, args, 22, 10, 1, (9, 10, 11), scratch
    )
    return found[:3], found[3:7], found[7:11], found[11:15]


def halves_of(spot, first, second):
    return ((first, 1 - spot[2]), (second, spot[2]))


def up_grad_kernel(spot, p0, p1, p2, p3, other_ref, own_ref, turned, inner):
    width = turned.shape[0]
    for i, part in enumerate((p0, p1, p2, p3)):
        turned[:, i * ROWS : (i + 1) * ROWS] = part[:, :width].T
        inner[i * ROWS : (i + 1) * ROWS, :] = part[:, width:]
    half = width // 2
    for ref, core in halves_of(spot, other_ref, own_ref):
        value = dot(turned[pl.ds(pl.multiple_of(core * half, half), half), :], inner[...]).astype(BF16)
        for g in range(GROUPS):
            ref[g] = value[g * TALL : (g + 1) * TALL]


def up_grad_parts(spot, parts, width):
    tokens, columns = 4 * ROWS, parts[0].shape[1] - width
    out = shaped((GROUPS, TALL, columns))
    scratch = (pltpu.VMEM((width, tokens), BF16), pltpu.VMEM((tokens, columns), BF16))
    return kernel_call(up_grad_kernel, "up_grad", (out, out), (spot, *parts), 16, 4, 1, (), scratch)


def down_grad_kernel(spot, p0, p1, p2, p3, other_ref, own_ref, turned, second, sums):
    parts = (p0, p1, p2, p3)
    width = second.shape[1]
    tall = GROUPS * TALL
    for i, part in enumerate(parts):
        rows = slice(i * ROWS, (i + 1) * ROWS)
        turned[:, rows] = part[:ROWS, width:].T
        second[rows, :] = part[:ROWS, :width]
    total = sum(part[ROWS:, :width].astype(F32) for part in parts)
    for core in range(2):
        start = core * (width // 2)
        sums[core] = jnp.concatenate(
            [total[:EXTRA, start : start + width // 2], total[EXTRA:, start : start + width // 2]], axis=1
        )
    for ref, core in halves_of(spot, other_ref, own_ref):
        down = dot(turned[pl.ds(pl.multiple_of(core * tall, tall), tall), :], second[...])
        for g in range(GROUPS):
            ref[g] = jnp.concatenate([down[g * TALL : (g + 1) * TALL], sums[core]], axis=0).astype(BF16)


def down_grad_parts(spot, parts, width):
    tokens = 4 * ROWS
    out = shaped((GROUPS, TALL + EXTRA, width))
    scratch = (
        pltpu.VMEM((2 * GROUPS * TALL, tokens), BF16),
        pltpu.VMEM((tokens, width), BF16),
        pltpu.VMEM((2, EXTRA, width), F32),
    )
    return kernel_call(down_grad_kernel, "down_grad", (out, out), (spot, *parts), 16, 5, 1, (), scratch)


def pair_sum_kernel(which, turns, spot, own, received, kept, sent):
    for i, out in zip(turns, (sent.at[0], sent.at[1], kept.at[1], kept.at[0])):
        at = spot[which] ^ i
        out[...] = (own[at].astype(F32) + received[at].astype(F32)).astype(BF16)


def pair_sums(spot, own, received, name, which=0, turns=(1, 2, 3, 0)):
    pair = shaped((2, *own.shape[1:]))
    kernel = functools.partial(pair_sum_kernel, which, turns)
    return kernel_call(kernel, name, (pair, pair), (spot, own, received), 16, 2, 1)


def placed(spot, pieces):
    group, quarter = spot[0], spot[1]
    for i in range(4):
        for g in range(GROUPS):
            turn = group ^ g
            at = ((turn & 1) << 1) ^ ((turn >> 1) * 3)
            if i < 3:
                block = pieces[i][at]
            else:
                block = jnp.where(at < 2, pieces[3][at & 1], pieces[4][at & 1])
            yield quarter ^ i, g, block


def place_up_kernel(spot, *refs):
    up_ref = refs[-1]
    for quarter, g, block in placed(spot, refs[:-1]):
        share = block.shape[1] // 2
        block = block.astype(F32)
        for core in range(2):
            at = pl.ds(pl.multiple_of(core * 4 * share + quarter * share, 128), share)
            up_ref[g * TALL : (g + 1) * TALL, at] = block[:, core * share : (core + 1) * share]


BIAS_ROWS = 16


def joined_grad_kernel(pieces, spot, query_grad, *rest):
    keys, values = rest[:pieces], rest[pieces : 2 * pieces]
    inputs = rest[2 * pieces : 2 * pieces + 4]
    contexts = rest[2 * pieces + 4 : 2 * pieces + 8]
    branches = rest[2 * pieces + 8 : 2 * pieces + 12]
    weight, other_ref, own_ref, kept_ref, sent_ref, joined, turned, context_turned, branch = rest[2 * pieces + 12 :]

    def total(parts):
        blocks = [p[0] if len(p.shape) == 3 else p[...] for p in parts]
        return sum(b.astype(F32) for b in blocks).T.astype(BF16)

    joined[:, :WIDTH] = query_grad[...]
    joined[:, WIDTH : 2 * WIDTH] = total(keys)
    joined[:, 2 * WIDTH :] = total(values)
    for i, ref in ((1, sent_ref.at[0]), (2, sent_ref.at[1]), (3, kept_ref.at[1]), (0, kept_ref.at[0])):
        ref[...] = dot(joined[i * ROWS : (i + 1) * ROWS, :], weight[...], TURNED).astype(BF16)
    for i, x in enumerate(inputs):
        at = slice(i * ROWS, (i + 1) * ROWS)
        turned[:, at] = x[...].T
        context_turned[:, at] = contexts[i][...].T
        branch[at, :] = branches[i][...]
    sums = jnp.concatenate(
        [column_sum(joined[...].astype(F32)), jnp.zeros((BIAS_ROWS - 1, 3 * WIDTH), F32)], axis=0
    ).astype(BF16)
    half = turned.shape[0] // 2
    for ref, core in halves_of(spot, other_ref, own_ref):
        value = dot(turned[pl.ds(pl.multiple_of(core * half, half), half), :], joined[...]).astype(BF16)
        strip = WIDTH // 2
        out = dot(context_turned[pl.ds(pl.multiple_of(core * strip, 32), strip), :], branch[...])
        for quarter in range(4):
            ref[quarter, :TALL, :] = value[quarter * TALL : (quarter + 1) * TALL]
            block = out[quarter * SHORT : (quarter + 1) * SHORT]
            last = jnp.concatenate([block[k * 8 : k * 8 + 8, 3 * WIDTH :] for k in range(3)], axis=1)
            packed = jnp.concatenate([block[:, : 3 * WIDTH], last], axis=0)
            ref[quarter, TALL : TALL + PACKED, :] = packed.astype(BF16)
            ref[quarter, TALL + PACKED :, :] = sums


def joined_grads(spot, query_grad, keys, values, inputs, contexts, branches, weight):
    width = weight.shape[0]
    part, pair = shaped((4, TALL + PACKED + BIAS_ROWS, 3 * WIDTH)), shaped((2, ROWS, width))
    tokens = GROUPS * ROWS
    scratch = (
        pltpu.VMEM((tokens, 3 * WIDTH), BF16),
        pltpu.VMEM((width, tokens), BF16),
        pltpu.VMEM((WIDTH, tokens), BF16),
        pltpu.VMEM((tokens, width), BF16),
    )
    args = (spot, query_grad, *keys, *values, *inputs, *contexts, *branches, weight)
    kernel = functools.partial(joined_grad_kernel, len(keys))
    return kernel_call(kernel, "joined_grad", (part, part, pair, pair), args, 16, 6, 1, (), scratch)


def place_down_kernel(spot, *refs):
    down_ref = refs[-1]
    for quarter, g, block in placed(spot, refs[:-1]):
        place = quarter * GROUPS + g
        down_ref[pl.ds(pl.multiple_of(place * TALL, 8), TALL), :] = block.astype(F32)


def place_joined_kernel(spot, *refs):
    weight_ref, bias_ref, kept_ref, sent_ref = refs[-4:]
    core = spot[2]
    width = weight_ref.shape[1] // 3
    found = list(placed(spot, refs[:-4]))
    rows = TALL
    for i in range(4):
        quarter = found[i * GROUPS][0]
        blocks = [block.astype(F32) for _, _, block in found[i * GROUPS : (i + 1) * GROUPS]]
        at = pl.ds(pl.multiple_of(quarter * rows, 16), rows)
        for part in range(3):
            value = jnp.concatenate([b[:, part * WIDTH : (part + 1) * WIDTH] for b in blocks], axis=1)
            weight_ref[at, part * width : (part + 1) * width] = value[:rows]
            if i == 0:
                line = value[rows + PACKED : rows + PACKED + 1]
                bias_ref[part : part + 1, :] = jnp.where(core == 0, line[:, : width // 2], line[:, width // 2 :])
        for g, block in enumerate(blocks):
            last = block[rows + SHORT : rows + PACKED]
            last = jnp.concatenate([last[:, k * WIDTH : (k + 1) * WIDTH] for k in range(3)], axis=0)
            strip = jnp.concatenate([block[rows : rows + SHORT], last], axis=1).astype(BF16)
            target = g // 2

            @pl.when(core == target)
            def _():
                kept_ref[g % 2, quarter] = strip

            @pl.when(core != target)
            def _():
                sent_ref[g % 2, quarter] = strip


def place_out_kernel(spot, kept, received, out_ref):
    core = spot[2]
    for g in range(2):
        for ref, side in ((kept, core), (received, 1 - core)):
            for quarter in range(4):
                start = g * WIDTH + side * (WIDTH // 2) + quarter * SHORT
                out_ref[pl.ds(pl.multiple_of(start, 8), SHORT), :] = ref[g, quarter].astype(F32)


def body(
    tokens,
    cotangent,
    lengths,
    qkv_weight,
    query_bias,
    value_bias,
    out_weight,
    out_bias,
    first_gain,
    first_shift,
    up_weight,
    up_bias,
    down_weight,
    down_bias,
    second_gain,
    second_shift,
):
    row_count, model_width = tokens.shape[1], tokens.shape[2]
    hidden_width = up_weight.shape[1]
    places = Places(lax.axis_size("seq"))
    plane_size, rest = places.plane_size, places.rest
    rank = lax.axis_index("seq")
    core = lax.axis_index("shard")
    group, position = rank // plane_size, rank % plane_size
    quarter = position // rest
    spot = jnp.stack([group, quarter, core]).astype(jnp.int32)
    length = lengths[core]
    inputs = tokens[0]
    column_rows = GROUPS * row_count
    half = model_width // 2
    turns = range(1, GROUPS)

    column_inputs = (inputs, *(places.column_swap(inputs, i) for i in turns))

    def both(block):
        return lax.all_gather(block, "shard", axis=0, tiled=True)

    def own_columns(w):
        at = group * WIDTH
        parts = [lax.dynamic_slice_in_dim(w, at + i * model_width, WIDTH, w.ndim - 1) for i in range(3)]
        return jnp.concatenate(parts, axis=-1)

    group_weight = both(own_columns(qkv_weight))
    vectors = [query_bias, value_bias, out_bias, first_gain, first_shift, down_bias, second_gain, second_shift]
    stacked = jnp.concatenate([jnp.stack(vectors), up_bias.reshape(-1, half)])
    stacked = lax.all_gather(stacked, "shard", axis=0).astype(F32)
    whole = jnp.transpose(stacked[:, : len(vectors)], (1, 0, 2)).reshape(len(vectors), model_width)
    up_offset = stacked[:, len(vectors) :].reshape(1, hidden_width)
    out_matrix = in_hbm(both(out_weight))
    up_matrix = in_hbm(both(up_weight))
    down_matrix = in_hbm(both(down_weight))

    offset = own_columns(jnp.concatenate([whole[0], jnp.zeros_like(whole[0]), whole[1]])).reshape(1, -1)
    query, key_value = kernel_call(
        project_kernel,
        "project",
        (shaped((column_rows, WIDTH)), shaped((column_rows, 2 * WIDTH))),
        (*column_inputs, group_weight, offset),
        16,
        2,
    )

    def masks(who):
        groups = group ^ jnp.arange(GROUPS)
        starts = (groups[None, :] * plane_size + who[:, None]) * row_count
        tokens_at = starts[:, :, None] + jnp.arange(row_count)
        return jnp.where(tokens_at.reshape(1, -1) < length, 0.0, MASKED).astype(F32)

    if plane_size == 4:
        chunks = 1
        key_values = (key_value, *(places.swap(key_value, i) for i in turns))
        bias = tuple(masks((position ^ i)[None]) for i in range(4))
    else:
        chunks = plane_size // 4
        gathered = lax.all_gather(key_value, "seq", axis=0, axis_index_groups=places.planes)
        key_values = (gathered.reshape(-1, 2 * WIDTH),)
        bias = (masks(jnp.arange(plane_size)),)
    context, log_total, context_lows = attend(query, key_values, bias, chunks)
    contexts = (context_lows[0], *(places.column_swap(context_lows[i], i) for i in turns))

    (layer_out, one_grad, branch_low), context_grads, up_parts, down_parts = dense(
        spot, contexts, inputs, cotangent[0], whole, up_offset, out_matrix, up_matrix, down_matrix
    )
    def after(value, *others):
        return lax.optimization_barrier((value, *others))[0]

    def to_other(block):
        return lax.ppermute(block, "shard", [(0, 1), (1, 0)])

    def rest_sum(total):
        return lax.psum(total, "seq", axis_index_groups=places.rests) if rest > 1 else total

    def add(left, right):
        return (left.astype(F32) + right.astype(F32)).astype(BF16)

    def column_total(kept, sent):
        near = places.column_swap(sent, 1)
        far = places.column_swap(add(kept[1], near[1]), 3)
        return kept[0].astype(F32) + near[0].astype(F32) + far.astype(F32)

    def four_total(kept, sent):
        near = places.four_swap(sent, 1)
        far = places.four_swap(add(kept[1], near[1]), 2)
        return kept[0].astype(F32) + near[0].astype(F32) + far.astype(F32)

    def column_gather(part):
        pair = jnp.stack([part, places.column_swap(part, 3)])
        return jnp.concatenate([pair, places.column_swap(pair, 1)])

    def plane_gather(column, *others):
        first, second = places.four_swap(column, 1), places.four_swap(column, 2)
        halves = (first[:2], second[2:])
        if others:
            halves = after(halves, *others)
        return column, first, second, places.four_swap(halves[0], 2), places.four_swap(halves[1], 1)

    context_grads = (context_grads[0], *(places.column_swap(context_grads[i], i) for i in turns))
    down_parts = (down_parts[0], *(places.four_swap(down_parts[i], i) for i in turns))
    branch_low = after(branch_low, context_grads)
    far = places.column_swap(branch_low, 3)
    branches = (branch_low, places.column_swap(branch_low, 1), places.column_swap(far, 1), far)
    query_grad, parts = attend_grad(query, context, context_grads, log_total, key_values, bias, chunks)
    if plane_size == 4:
        own_key, own_value, turned_key, turned_value, key_x, value_y = parts
        key_x, value_y = first_step = places.swap(key_x, 1), places.swap(value_y, 2)
        keys = (own_key, key_x, places.swap(add(turned_key, key_x[1]), 2))
        values = (own_value, value_y, places.swap(add(turned_value, value_y[1]), 1))
    else:
        blocks = jnp.stack(parts).reshape(2 * WIDTH, plane_size, column_rows)
        blocks = places.exchange(jnp.transpose(blocks, (1, 0, 2)), places.planes)
        blocks = jnp.sum(blocks.astype(F32), axis=0)
        keys, values = first_step = (blocks[:WIDTH],), (blocks[WIDTH:],)
    down_parts = after(down_parts, query_grad, branches)
    other, own = down_grad_parts(spot, down_parts, model_width)
    down_pieces = pair_sums(spot, own, to_other(other), "down_sum")
    down_part = rest_sum(column_total(*down_pieces))
    up_parts = after(up_parts, first_step)
    up_parts = (up_parts[0], *(places.four_swap(up_parts[i], i) for i in turns))
    keys, values = after((keys, values), down_part, up_parts)
    down_column = column_gather(down_part[:TALL].astype(BF16))
    other, own, kept, sent = joined_grads(
        spot, query_grad, keys, values, column_inputs, context_lows, branches, group_weight
    )
    input_grad = one_grad + column_total(kept, sent)
    joined_pieces = pair_sums(spot, own, to_other(other), "joined_sum", 1, (1, 3, 2, 0))
    joined_part = rest_sum(four_total(*joined_pieces)).astype(BF16)
    up_parts = after(up_parts, kept)
    other, own = up_grad_parts(spot, up_parts, model_width)
    up_part = rest_sum(column_total(*pair_sums(spot, own, to_other(other), "up_sum"))).astype(BF16)
    down_all = plane_gather(down_column)
    down_grad = kernel_call(
        place_down_kernel,
        "place_down",
        shaped((hidden_width // 2, model_width), F32),
        (spot, *down_all),
        16,
        5,
        1,
    )
    up_all = plane_gather(after(column_gather(up_part), down_all), down_grad)
    joined_all = plane_gather(after(column_gather(joined_part), down_all), down_grad)
    strips = shaped((2, 4, SHORT, model_width))
    qkv_grad, bias_grad, out_kept, out_sent = kernel_call(
        place_joined_kernel,
        "place_joined",
        (shaped((half, 3 * model_width), F32), shaped((8, half), F32), strips, strips),
        (spot, *joined_all),
        16,
        5,
        1,
    )
    out_grad = kernel_call(
        place_out_kernel, "place_out", shaped((half, model_width), F32), (spot, out_kept, to_other(out_sent)), 8, 2, 1
    )
    up_grad = kernel_call(
        place_up_kernel,
        "place_up",
        shaped((half, hidden_width), F32),
        (spot, *up_all),
        16,
        4,
        1,
    )

    extra = down_part[TALL:]
    up_bias_grad = jnp.concatenate([extra[6, :half], extra[7, :half], extra[0, half:], extra[1, half:]])
    shape = (1, row_count, model_width)
    return (
        layer_out.reshape(shape),
        input_grad.reshape(shape),
        qkv_grad,
        bias_grad[0],
        bias_grad[2],
        out_grad,
        extra[0, :half],
        extra[1, :half],
        extra[2, :half],
        up_grad,
        up_bias_grad,
        down_grad,
        extra[3, :half],
        extra[4, :half],
        extra[5, :half],
    )


def solution(mesh):
    rows, halves, whole = P("shard", "seq", None), P("shard", None), P("shard")
    in_specs = (rows, rows, P(), halves, whole, whole, halves, whole, whole, whole, halves, whole, halves, whole, whole, whole)
    out_specs = (rows, rows, halves, whole, whole, halves, whole, whole, whole, halves, whole, halves, whole, whole, whole)
    return jax.shard_map(body, mesh=mesh, in_specs=in_specs, out_specs=out_specs, check_vma=False)
```

```python
import functools

import jax
import jax.numpy as jnp
from jax import lax
from jax.experimental import pallas as pl
from jax.experimental.pallas import tpu as pltpu
from jax.sharding import PartitionSpec as P

HEADS = 12
HEAD_DIM = 64
GROUPS = 4
GROUP_HEADS = HEADS // GROUPS
WIDTH = GROUP_HEADS * HEAD_DIM
EPSILON = 1e-12
MASKED = -1e30
F32 = jnp.float32
BF16 = jnp.bfloat16
MIB = 2**20
ROWS = 128
TURNED = ((1,), (1,))
FIRST = ((1,), (0,))


def dot(left, right, dims=FIRST):
    return lax.dot_general(left, right, (dims, ((), ())), preferred_element_type=F32)


def kernel_call(kernel, name, outs, args, vmem, micros, smem=0, left=(), scratch=(), after=()):
    spaces = [
        pl.BlockSpec(memory_space=pltpu.SMEM if i < smem else pltpu.HBM if i in left else pltpu.VMEM)
        for i in range(len(args))
    ]
    count = len(args)

    def run(*refs):
        kernel(*refs[:count], *refs[count + len(after) :])

    return pl.pallas_call(
        run if after else kernel,
        out_shape=outs,
        in_specs=spaces + [pl.BlockSpec(memory_space=pl.ANY)] * len(after),
        scratch_shapes=list(scratch),
        compiler_params=pltpu.CompilerParams(vmem_limit_bytes=vmem * MIB),
        cost_estimate=pl.CostEstimate(flops=0, bytes_accessed=int(micros * 3_500_000), transcendentals=0),
        name=name,
    )(*args, *after)


def in_hbm(array):
    return pltpu.with_memory_space_constraint(array, pltpu.HBM)


def shaped(shape, dtype=BF16):
    return jax.ShapeDtypeStruct(shape, dtype)


class Places:
    def __init__(self, size):
        self.size = size
        self.plane_size = size // GROUPS
        self.rest = self.plane_size // 4
        index = lambda g, q, m: (g * 4 + q) * self.rest + m
        groups, quarters, members = range(GROUPS), range(4), range(self.rest)
        self.columns = [[index(g, q, m) for g in groups] for q in quarters for m in members]
        self.planes = [[index(g, q, m) for q in quarters for m in members] for g in groups]
        self.fours = [[index(g, q, m) for q in quarters] for g in groups for m in members]
        self.sixteens = [[index(g, q, m) for g in groups for q in quarters] for m in members]
        self.rests = [[index(g, q, m) for m in members] for g in groups for q in quarters]

    def swap(self, block, bits):
        return lax.ppermute(block, "seq", [(i, i ^ bits) for i in range(self.size)])

    def column_swap(self, block, turn):
        return self.swap(block, turn * self.plane_size)

    def four_swap(self, block, turn):
        return self.swap(block, turn * self.rest)

    def exchange(self, blocks, groups):
        return lax.all_to_all(blocks, "seq", 0, 0, axis_index_groups=groups, tiled=True)


def project_kernel(x0, x1, x2, x3, weight, offset, query_ref, key_value_ref):
    for i, x in enumerate((x0, x1, x2, x3)):
        at = slice(i * ROWS, (i + 1) * ROWS)
        joined = (dot(x[...], weight[...]) + offset[...]).astype(BF16)
        query_ref[at, :] = joined[:, :WIDTH] * jnp.asarray(0.125, BF16)
        key_value_ref[at, :] = joined[:, WIDTH:]


def attend_kernel(pieces, chunks, *refs):
    q_ref = refs[0]
    key_value_refs, bias_refs = refs[1 : 1 + pieces], refs[1 + pieces : 1 + 2 * pieces]
    context_ref, log_ref = refs[1 + 2 * pieces : 3 + 2 * pieces]
    low_refs = refs[3 + 2 * pieces :]
    rows = q_ref.shape[0]
    chunk = key_value_refs[0].shape[0] // chunks
    for block in range(rows // ROWS):
        at = slice(block * ROWS, (block + 1) * ROWS)
        for head in range(GROUP_HEADS):
            columns = slice(head * HEAD_DIM, (head + 1) * HEAD_DIM)
            value_columns = slice(WIDTH + head * HEAD_DIM, WIDTH + (head + 1) * HEAD_DIM)
            query = q_ref[at, columns]

            def step(index, state):
                highest, total, mix = state
                here = pl.ds(pl.multiple_of(index * chunk, chunk), chunk)
                scores = [dot(query, k[here, columns], TURNED) + b[:, here] for k, b in zip(key_value_refs, bias_refs)]
                peak = functools.reduce(jnp.maximum, [jnp.max(s, axis=1, keepdims=True) for s in scores])
                raised = jnp.maximum(highest, peak)
                weights = [jnp.exp(s - raised) for s in scores]
                factor = jnp.exp(highest - raised)
                total = total * factor + sum(jnp.sum(w, axis=1, keepdims=True) for w in weights)
                mix = mix * factor + sum(
                    dot(w.astype(BF16), v[here, value_columns]) for w, v in zip(weights, key_value_refs)
                )
                return raised, total, mix

            state = (
                jnp.full((ROWS, 1), MASKED, F32),
                jnp.zeros((ROWS, 1), F32),
                jnp.zeros((ROWS, HEAD_DIM), F32),
            )
            highest, total, mix = step(0, state) if chunks == 1 else lax.fori_loop(0, chunks, step, state)
            context = mix / total
            context_ref[at, columns] = context
            low_refs[block][:, columns] = context.astype(BF16)
            log_ref[at, head : head + 1] = highest + jnp.log(total)


def attend(query, key_values, bias, chunks):
    rows = query.shape[0]
    outs = (shaped((rows, WIDTH), F32), shaped((rows, 128), F32)) + (shaped((ROWS, WIDTH)),) * GROUPS
    kernel = functools.partial(attend_kernel, len(key_values), chunks)
    found = kernel_call(kernel, "attend", outs, (query, *key_values, *bias), 24 if chunks == 1 else 60, 9)
    return found[0], found[1], found[2:]


def attend_grad_kernel(pieces, chunks, *refs):
    q_ref, context_ref, log_ref = refs[:3]
    grad_refs = refs[3:7]
    key_value_refs, bias_refs = refs[7 : 7 + pieces], refs[7 + pieces : 7 + 2 * pieces]
    query_grad_ref = refs[7 + 2 * pieces]
    outs = refs[8 + 2 * pieces :]
    if pieces == 4:
        own_key, own_value, turned_key, turned_value, key_x, value_y = outs
        key_outs = (own_key, key_x.at[0], turned_key, key_x.at[1])
        value_outs = (own_value, turned_value, value_y.at[0], value_y.at[1])
    else:
        key_outs, value_outs = outs[:1], outs[1:]
    rows = q_ref.shape[0]
    chunk = key_value_refs[0].shape[0] // chunks
    for head in range(GROUP_HEADS):
        columns = slice(head * HEAD_DIM, (head + 1) * HEAD_DIM)
        value_columns = slice(WIDTH + head * HEAD_DIM, WIDTH + (head + 1) * HEAD_DIM)
        query = q_ref[:, columns]
        grad = jnp.concatenate([g[:, columns] for g in grad_refs], axis=0)
        correction = jnp.sum(grad.astype(F32) * context_ref[:, columns], axis=1, keepdims=True)
        log_total = log_ref[:, head : head + 1]
        query_turned = query.T
        grad_turned = grad.T

        def step(index, query_grad):
            here = pl.ds(pl.multiple_of(index * chunk, chunk), chunk)
            for both, b, key_out, value_out in zip(key_value_refs, bias_refs, key_outs, value_outs):
                key = both[here, columns]
                probs = jnp.exp(dot(query, key, TURNED) + b[:, here] - log_total)
                probs_grad = dot(grad, both[here, value_columns], TURNED)
                score_grad = (probs * (probs_grad - correction)).astype(BF16)
                query_grad = query_grad + dot(score_grad, key)
                key_out[columns, here] = dot(query_turned, score_grad).astype(BF16)
                value_out[columns, here] = dot(grad_turned, probs.astype(BF16)).astype(BF16)
            return query_grad

        total = jnp.zeros((rows, HEAD_DIM), F32)
        total = step(0, total) if chunks == 1 else lax.fori_loop(0, chunks, step, total)
        query_grad_ref[:, columns] = (total * 0.125).astype(BF16)


def attend_grad(query, context, grads, log_total, key_values, bias, chunks):
    rows, keys = query.shape[0], key_values[0].shape[0]
    one, two = shaped((WIDTH, keys)), shaped((2, WIDTH, keys))
    outs = (shaped((rows, WIDTH)),) + ((one, one, one, one, two, two) if len(key_values) == 4 else (one, one))
    kernel = functools.partial(attend_grad_kernel, len(key_values), chunks)
    args = (query, context, log_total, *grads, *key_values, *bias)
    found = kernel_call(kernel, "attend_grad", outs, args, 32 if chunks == 1 else 60, 11)
    return found[0], found[1:]


def normalize(hidden):
    center = hidden - jnp.mean(hidden, axis=1, keepdims=True)
    scale = lax.rsqrt(jnp.mean(center * center, axis=1, keepdims=True) + EPSILON)
    return center * scale, scale


def normalize_grad(grad, normal, scale):
    return scale * (
        grad
        - jnp.mean(grad, axis=1, keepdims=True)
        - normal * jnp.mean(grad * normal, axis=1, keepdims=True)
    )


def column_sum(values):
    return jnp.sum(values, axis=0, keepdims=True)


TALL, SHORT, EXTRA = 96, 24, 8
PACKED = 32


def dense_kernel(width, spot, c0, c1, c2, c3, x_ref, grad_ref, vectors, up_offset, out_hbm, up_hbm, down_hbm, *rest):
    layer_ref, one_grad_ref = rest[:2]
    branch_ref = rest[2]
    context_grads, up_parts, down_parts = rest[3:7], rest[7:11], rest[11:15]
    out_w, up_w, down_w, slope, active_ref, inner_ref, sums_ref, sems = rest[15:]
    copies = [
        pltpu.make_async_copy(source, target, sems.at[i])
        for i, (source, target) in enumerate(((out_hbm, out_w), (up_hbm, up_w), (down_hbm, down_w)))
    ]
    for copy in copies:
        copy.start()
    hidden = up_w.shape[1]
    half = width // 2
    out_offset, gain_one, shift_one, down_offset, gain_two, shift_two = (vectors[i : i + 1, :] for i in range(2, 8))
    group, quarter = spot[0], spot[1]
    contexts = (c0, c1, c2, c3)

    def turned(i):
        return pl.ds(pl.multiple_of((group ^ i) * WIDTH, WIDTH), WIDTH)

    copies[0].wait()
    branch = sum(dot(c[...], out_w[turned(i), :]) for i, c in enumerate(contexts)) + out_offset
    normal_one, scale_one = normalize(x_ref[...].astype(F32) + branch)
    normed_low = (normal_one * gain_one + shift_one).astype(BF16)
    for ref in up_parts:
        ref[:, :width] = normed_low
    copies[1].wait()
    step = 768
    for start in range(0, hidden, step):
        at = slice(start, start + step)
        inner = dot(normed_low, up_w[:, at]) + up_offset[:, at]
        share = 0.5 + 0.5 * lax.erf(inner * 0.7071067811865476)
        density = 0.3989422804014327 * jnp.exp(-0.5 * inner * inner)
        slope[:, at] = share + inner * density
        active_ref[:, at] = (inner * share).astype(BF16)
    copies[2].wait()
    second = dot(active_ref[...], down_w[...]) + down_offset
    normal_two, scale_two = normalize(normed_low.astype(F32) + second)
    layer_ref[...] = (normal_two * gain_two + shift_two).astype(BF16)
    grad = grad_ref[...].astype(F32)
    gain_two_grad, shift_two_grad = column_sum(grad * normal_two), column_sum(grad)
    two_grad = normalize_grad(grad * gain_two, normal_two, scale_two)
    second_low = two_grad.astype(BF16)
    down_bias_grad = column_sum(second_low.astype(F32))
    normed_grad = two_grad
    for start in range(0, hidden, step):
        at = slice(start, start + step)
        inner_low = (dot(second_low, down_w[at, :], TURNED) * slope[:, at]).astype(BF16)
        inner_ref[:, at] = inner_low
        up_sum = column_sum(inner_low.astype(F32))
        for piece in range(step // half):
            place = start // half + piece
            per_core = hidden // 2 // half
            row, core = 6 + place % per_core, place // per_core
            sums_ref[row : row + 1, core * half : (core + 1) * half] = up_sum[:, piece * half : (piece + 1) * half]
        normed_grad = normed_grad + dot(inner_low, up_w[:, at], TURNED)
    gain_one_grad, shift_one_grad = column_sum(normed_grad * normal_one), column_sum(normed_grad)
    one_grad = normalize_grad(normed_grad * gain_one, normal_one, scale_one)
    one_grad_ref[...] = one_grad
    branch_low = one_grad.astype(BF16)
    branch_ref[...] = branch_low
    for i, ref in enumerate(context_grads):
        ref[...] = dot(branch_low, out_w[turned(i), :], TURNED).astype(BF16)
    out_bias_grad = column_sum(branch_low.astype(F32))
    sums = (out_bias_grad, gain_one_grad, shift_one_grad, down_bias_grad, gain_two_grad, shift_two_grad)
    for i, total in enumerate(sums):
        sums_ref[i : i + 1, :] = total
    sums_ref[10:16, :] = jnp.zeros((6, width), F32)
    share = hidden // 8
    for i in range(4):
        for core in range(2):
            at = pl.ds(pl.multiple_of(core * (hidden // 2) + (quarter ^ i) * share, share), share)
            to = slice(width + core * share, width + (core + 1) * share)
            up_parts[i][:, to] = inner_ref[:, at]
            down_parts[i][:ROWS, to] = active_ref[:, at]
        down_parts[i][:ROWS, :width] = second_low
        down_parts[i][ROWS:, :width] = sums_ref[...].astype(BF16)


def dense(spot, contexts, inputs, grad, vectors, up_offset, out_matrix, up_matrix, down_matrix):
    width, hidden = up_matrix.shape
    outs = (
        (shaped((ROWS, width)), shaped((ROWS, width), F32), shaped((ROWS, width)))
        + (shaped((ROWS, WIDTH)),) * GROUPS
        + (shaped((ROWS, width + hidden // 4)),) * 4
        + (shaped((ROWS + 16, width + hidden // 4)),) * 4
    )
    scratch = (
        pltpu.VMEM(out_matrix.shape, BF16),
        pltpu.VMEM(up_matrix.shape, BF16),
        pltpu.VMEM(down_matrix.shape, BF16),
        pltpu.VMEM((ROWS, hidden), F32),
        pltpu.VMEM((ROWS, hidden), BF16),
        pltpu.VMEM((ROWS, hidden), BF16),
        pltpu.VMEM((16, width), F32),
        pltpu.SemaphoreType.DMA((3,)),
    )
    args = (spot, *contexts, inputs, grad, vectors, up_offset, out_matrix, up_matrix, down_matrix)
    found = kernel_call(
        functools.partial(dense_kernel, width), "dense", outs, args, 22, 10, 1, (9, 10, 11), scratch
    )
    return found[:3], found[3:7], found[7:11], found[11:15]


def halves_of(spot, first, second):
    return ((first, 1 - spot[2]), (second, spot[2]))


def up_grad_kernel(spot, p0, p1, p2, p3, other_ref, own_ref, turned, inner):
    width = turned.shape[0]
    for i, part in enumerate((p0, p1, p2, p3)):
        turned[:, i * ROWS : (i + 1) * ROWS] = part[:, :width].T
        inner[i * ROWS : (i + 1) * ROWS, :] = part[:, width:]
    half = width // 2
    for ref, core in halves_of(spot, other_ref, own_ref):
        value = dot(turned[pl.ds(pl.multiple_of(core * half, half), half), :], inner[...]).astype(BF16)
        for g in range(GROUPS):
            ref[g] = value[g * TALL : (g + 1) * TALL]


def up_grad_parts(spot, parts, width):
    tokens, columns = 4 * ROWS, parts[0].shape[1] - width
    out = shaped((GROUPS, TALL, columns))
    scratch = (pltpu.VMEM((width, tokens), BF16), pltpu.VMEM((tokens, columns), BF16))
    return kernel_call(up_grad_kernel, "up_grad", (out, out), (spot, *parts), 16, 4, 1, (), scratch)


def down_grad_kernel(spot, p0, p1, p2, p3, other_ref, own_ref, turned, second, sums):
    parts = (p0, p1, p2, p3)
    width = second.shape[1]
    tall = GROUPS * TALL
    for i, part in enumerate(parts):
        rows = slice(i * ROWS, (i + 1) * ROWS)
        turned[:, rows] = part[:ROWS, width:].T
        second[rows, :] = part[:ROWS, :width]
    total = sum(part[ROWS:, :width].astype(F32) for part in parts)
    for core in range(2):
        start = core * (width // 2)
        sums[core] = jnp.concatenate(
            [total[:EXTRA, start : start + width // 2], total[EXTRA:, start : start + width // 2]], axis=1
        )
    for ref, core in halves_of(spot, other_ref, own_ref):
        down = dot(turned[pl.ds(pl.multiple_of(core * tall, tall), tall), :], second[...])
        for g in range(GROUPS):
            ref[g] = jnp.concatenate([down[g * TALL : (g + 1) * TALL], sums[core]], axis=0).astype(BF16)


def down_grad_parts(spot, parts, width):
    tokens = 4 * ROWS
    out = shaped((GROUPS, TALL + EXTRA, width))
    scratch = (
        pltpu.VMEM((2 * GROUPS * TALL, tokens), BF16),
        pltpu.VMEM((tokens, width), BF16),
        pltpu.VMEM((2, EXTRA, width), F32),
    )
    return kernel_call(down_grad_kernel, "down_grad", (out, out), (spot, *parts), 16, 5, 1, (), scratch)


def pair_sum_kernel(which, turns, spot, own, received, kept, sent):
    for i, out in zip(turns, (sent.at[0], sent.at[1], kept.at[1], kept.at[0])):
        at = spot[which] ^ i
        out[...] = (own[at].astype(F32) + received[at].astype(F32)).astype(BF16)


def pair_sums(spot, own, received, name, which=0, turns=(1, 2, 3, 0)):
    pair = shaped((2, *own.shape[1:]))
    kernel = functools.partial(pair_sum_kernel, which, turns)
    return kernel_call(kernel, name, (pair, pair), (spot, own, received), 16, 2, 1)


def placed(spot, pieces):
    group, quarter = spot[0], spot[1]
    for i in range(4):
        for g in range(GROUPS):
            turn = group ^ g
            at = ((turn & 1) << 1) ^ ((turn >> 1) * 3)
            if i < 3:
                block = pieces[i][at]
            else:
                block = jnp.where(at < 2, pieces[3][at & 1], pieces[4][at & 1])
            yield quarter ^ i, g, block


def place_up_kernel(spot, *refs):
    up_ref = refs[-1]
    for quarter, g, block in placed(spot, refs[:-1]):
        share = block.shape[1] // 2
        block = block.astype(F32)
        for core in range(2):
            at = pl.ds(pl.multiple_of(core * 4 * share + quarter * share, 128), share)
            up_ref[g * TALL : (g + 1) * TALL, at] = block[:, core * share : (core + 1) * share]


BIAS_ROWS = 16


def joined_grad_kernel(pieces, spot, query_grad, *rest):
    keys, values = rest[:pieces], rest[pieces : 2 * pieces]
    inputs = rest[2 * pieces : 2 * pieces + 4]
    contexts = rest[2 * pieces + 4 : 2 * pieces + 8]
    branches = rest[2 * pieces + 8 : 2 * pieces + 12]
    weight, other_ref, own_ref, kept_ref, sent_ref, joined, turned, context_turned, branch = rest[2 * pieces + 12 :]

    def total(parts):
        blocks = [p[0] if len(p.shape) == 3 else p[...] for p in parts]
        return sum(b.astype(F32) for b in blocks).T.astype(BF16)

    joined[:, :WIDTH] = query_grad[...]
    joined[:, WIDTH : 2 * WIDTH] = total(keys)
    joined[:, 2 * WIDTH :] = total(values)
    for i, ref in ((1, sent_ref.at[0]), (2, sent_ref.at[1]), (3, kept_ref.at[1]), (0, kept_ref.at[0])):
        ref[...] = dot(joined[i * ROWS : (i + 1) * ROWS, :], weight[...], TURNED).astype(BF16)
    for i, x in enumerate(inputs):
        at = slice(i * ROWS, (i + 1) * ROWS)
        turned[:, at] = x[...].T
        context_turned[:, at] = contexts[i][...].T
        branch[at, :] = branches[i][...]
    sums = jnp.concatenate(
        [column_sum(joined[...].astype(F32)), jnp.zeros((BIAS_ROWS - 1, 3 * WIDTH), F32)], axis=0
    ).astype(BF16)
    half = turned.shape[0] // 2
    for ref, core in halves_of(spot, other_ref, own_ref):
        value = dot(turned[pl.ds(pl.multiple_of(core * half, half), half), :], joined[...]).astype(BF16)
        strip = WIDTH // 2
        out = dot(context_turned[pl.ds(pl.multiple_of(core * strip, 32), strip), :], branch[...])
        for quarter in range(4):
            ref[quarter, :TALL, :] = value[quarter * TALL : (quarter + 1) * TALL]
            block = out[quarter * SHORT : (quarter + 1) * SHORT]
            last = jnp.concatenate([block[k * 8 : k * 8 + 8, 3 * WIDTH :] for k in range(3)], axis=1)
            packed = jnp.concatenate([block[:, : 3 * WIDTH], last], axis=0)
            ref[quarter, TALL : TALL + PACKED, :] = packed.astype(BF16)
            ref[quarter, TALL + PACKED :, :] = sums


def joined_grads(spot, query_grad, keys, values, inputs, contexts, branches, weight):
    width = weight.shape[0]
    part, pair = shaped((4, TALL + PACKED + BIAS_ROWS, 3 * WIDTH)), shaped((2, ROWS, width))
    tokens = GROUPS * ROWS
    scratch = (
        pltpu.VMEM((tokens, 3 * WIDTH), BF16),
        pltpu.VMEM((width, tokens), BF16),
        pltpu.VMEM((WIDTH, tokens), BF16),
        pltpu.VMEM((tokens, width), BF16),
    )
    args = (spot, query_grad, *keys, *values, *inputs, *contexts, *branches, weight)
    kernel = functools.partial(joined_grad_kernel, len(keys))
    return kernel_call(kernel, "joined_grad", (part, part, pair, pair), args, 16, 6, 1, (), scratch)


def place_down_kernel(spot, *refs):
    down_ref = refs[-1]
    for quarter, g, block in placed(spot, refs[:-1]):
        place = quarter * GROUPS + g
        down_ref[pl.ds(pl.multiple_of(place * TALL, 8), TALL), :] = block.astype(F32)


def place_joined_kernel(spot, *refs):
    weight_ref, bias_ref, kept_ref, sent_ref = refs[-4:]
    core = spot[2]
    width = weight_ref.shape[1] // 3
    found = list(placed(spot, refs[:-4]))
    rows = TALL
    for i in range(4):
        quarter = found[i * GROUPS][0]
        blocks = [block.astype(F32) for _, _, block in found[i * GROUPS : (i + 1) * GROUPS]]
        at = pl.ds(pl.multiple_of(quarter * rows, 16), rows)
        for part in range(3):
            value = jnp.concatenate([b[:, part * WIDTH : (part + 1) * WIDTH] for b in blocks], axis=1)
            weight_ref[at, part * width : (part + 1) * width] = value[:rows]
            if i == 0:
                line = value[rows + PACKED : rows + PACKED + 1]
                bias_ref[part : part + 1, :] = jnp.where(core == 0, line[:, : width // 2], line[:, width // 2 :])
        for g, block in enumerate(blocks):
            last = block[rows + SHORT : rows + PACKED]
            last = jnp.concatenate([last[:, k * WIDTH : (k + 1) * WIDTH] for k in range(3)], axis=0)
            strip = jnp.concatenate([block[rows : rows + SHORT], last], axis=1).astype(BF16)
            target = g // 2

            @pl.when(core == target)
            def _():
                kept_ref[g % 2, quarter] = strip

            @pl.when(core != target)
            def _():
                sent_ref[g % 2, quarter] = strip


def place_out_kernel(spot, kept, received, out_ref):
    core = spot[2]
    for g in range(2):
        for ref, side in ((kept, core), (received, 1 - core)):
            for quarter in range(4):
                start = g * WIDTH + side * (WIDTH // 2) + quarter * SHORT
                out_ref[pl.ds(pl.multiple_of(start, 8), SHORT), :] = ref[g, quarter].astype(F32)


def body(
    tokens,
    cotangent,
    lengths,
    qkv_weight,
    query_bias,
    value_bias,
    out_weight,
    out_bias,
    first_gain,
    first_shift,
    up_weight,
    up_bias,
    down_weight,
    down_bias,
    second_gain,
    second_shift,
):
    row_count, model_width = tokens.shape[1], tokens.shape[2]
    hidden_width = up_weight.shape[1]
    places = Places(lax.axis_size("seq"))
    plane_size, rest = places.plane_size, places.rest
    rank = lax.axis_index("seq")
    core = lax.axis_index("shard")
    group, position = rank // plane_size, rank % plane_size
    quarter = position // rest
    spot = jnp.stack([group, quarter, core]).astype(jnp.int32)
    length = lengths[core]
    inputs = tokens[0]
    column_rows = GROUPS * row_count
    half = model_width // 2
    turns = range(1, GROUPS)

    column_inputs = (inputs, *(places.column_swap(inputs, i) for i in turns))

    def both(block):
        return lax.all_gather(block, "shard", axis=0, tiled=True)

    def own_columns(w):
        at = group * WIDTH
        parts = [lax.dynamic_slice_in_dim(w, at + i * model_width, WIDTH, w.ndim - 1) for i in range(3)]
        return jnp.concatenate(parts, axis=-1)

    group_weight = both(own_columns(qkv_weight))
    vectors = [query_bias, value_bias, out_bias, first_gain, first_shift, down_bias, second_gain, second_shift]
    stacked = jnp.concatenate([jnp.stack(vectors), up_bias.reshape(-1, half)])
    stacked = lax.all_gather(stacked, "shard", axis=0).astype(F32)
    whole = jnp.transpose(stacked[:, : len(vectors)], (1, 0, 2)).reshape(len(vectors), model_width)
    up_offset = stacked[:, len(vectors) :].reshape(1, hidden_width)
    out_matrix = in_hbm(both(out_weight))
    up_matrix = in_hbm(both(up_weight))
    down_matrix = in_hbm(both(down_weight))

    offset = own_columns(jnp.concatenate([whole[0], jnp.zeros_like(whole[0]), whole[1]])).reshape(1, -1)
    query, key_value = kernel_call(
        project_kernel,
        "project",
        (shaped((column_rows, WIDTH)), shaped((column_rows, 2 * WIDTH))),
        (*column_inputs, group_weight, offset),
        16,
        2,
    )

    def masks(who):
        groups = group ^ jnp.arange(GROUPS)
        starts = (groups[None, :] * plane_size + who[:, None]) * row_count
        tokens_at = starts[:, :, None] + jnp.arange(row_count)
        return jnp.where(tokens_at.reshape(1, -1) < length, 0.0, MASKED).astype(F32)

    if plane_size == 4:
        chunks = 1
        key_values = (key_value, *(places.swap(key_value, i) for i in turns))
        bias = tuple(masks((position ^ i)[None]) for i in range(4))
    else:
        chunks = plane_size // 4
        gathered = lax.all_gather(key_value, "seq", axis=0, axis_index_groups=places.planes)
        key_values = (gathered.reshape(-1, 2 * WIDTH),)
        bias = (masks(jnp.arange(plane_size)),)
    context, log_total, context_lows = attend(query, key_values, bias, chunks)
    contexts = (context_lows[0], *(places.column_swap(context_lows[i], i) for i in turns))

    (layer_out, one_grad, branch_low), context_grads, up_parts, down_parts = dense(
        spot, contexts, inputs, cotangent[0], whole, up_offset, out_matrix, up_matrix, down_matrix
    )
    def after(value, *others):
        return lax.optimization_barrier((value, *others))[0]

    def to_other(block):
        return lax.ppermute(block, "shard", [(0, 1), (1, 0)])

    def rest_sum(total):
        return lax.psum(total, "seq", axis_index_groups=places.rests) if rest > 1 else total

    def add(left, right):
        return (left.astype(F32) + right.astype(F32)).astype(BF16)

    def column_total(kept, sent):
        near = places.column_swap(sent, 1)
        far = places.column_swap(add(kept[1], near[1]), 3)
        return kept[0].astype(F32) + near[0].astype(F32) + far.astype(F32)

    def four_total(kept, sent):
        near = places.four_swap(sent, 1)
        far = places.four_swap(add(kept[1], near[1]), 2)
        return kept[0].astype(F32) + near[0].astype(F32) + far.astype(F32)

    def column_gather(part):
        pair = jnp.stack([part, places.column_swap(part, 3)])
        return jnp.concatenate([pair, places.column_swap(pair, 1)])

    def plane_gather(column, *others):
        first, second = places.four_swap(column, 1), places.four_swap(column, 2)
        halves = (first[:2], second[2:])
        if others:
            halves = after(halves, *others)
        return column, first, second, places.four_swap(halves[0], 2), places.four_swap(halves[1], 1)

    context_grads = (context_grads[0], *(places.column_swap(context_grads[i], i) for i in turns))
    down_parts = (down_parts[0], *(places.four_swap(down_parts[i], i) for i in turns))
    query_grad, parts = attend_grad(query, context, context_grads, log_total, key_values, bias, chunks)
    if plane_size == 4:
        own_key, own_value, turned_key, turned_value, key_x, value_y = parts
        key_x, value_y = first_step = places.swap(key_x, 1), places.swap(value_y, 2)
        keys = (own_key, key_x, places.swap(add(turned_key, key_x[1]), 2))
        values = (own_value, value_y, places.swap(add(turned_value, value_y[1]), 1))
    else:
        blocks = jnp.stack(parts).reshape(2 * WIDTH, plane_size, column_rows)
        blocks = places.exchange(jnp.transpose(blocks, (1, 0, 2)), places.planes)
        blocks = jnp.sum(blocks.astype(F32), axis=0)
        keys, values = first_step = (blocks[:WIDTH],), (blocks[WIDTH:],)
    branch_low = after(branch_low, first_step)
    far = places.column_swap(branch_low, 3)
    branches = (branch_low, places.column_swap(branch_low, 1), places.column_swap(far, 1), far)
    down_parts = after(down_parts, query_grad)
    other, own = down_grad_parts(spot, down_parts, model_width)
    down_pieces = pair_sums(spot, own, to_other(other), "down_sum")
    down_part = rest_sum(column_total(*down_pieces))
    up_parts = after(up_parts, query_grad)
    up_parts = (up_parts[0], *(places.four_swap(up_parts[i], i) for i in turns))
    keys, values = after((keys, values), down_part, up_parts)
    down_column = column_gather(down_part[:TALL].astype(BF16))
    other, own, kept, sent = joined_grads(
        spot, query_grad, keys, values, column_inputs, context_lows, branches, group_weight
    )
    input_grad = one_grad + column_total(kept, sent)
    joined_pieces = pair_sums(spot, own, to_other(other), "joined_sum", 1, (1, 3, 2, 0))
    joined_part = rest_sum(four_total(*joined_pieces)).astype(BF16)
    up_parts = after(up_parts, kept)
    other, own = up_grad_parts(spot, up_parts, model_width)
    up_part = rest_sum(column_total(*pair_sums(spot, own, to_other(other), "up_sum"))).astype(BF16)
    down_all = plane_gather(down_column)
    down_grad = kernel_call(
        place_down_kernel,
        "place_down",
        shaped((hidden_width // 2, model_width), F32),
        (spot, *down_all),
        16,
        5,
        1,
    )
    up_all = plane_gather(after(column_gather(up_part), down_all), down_grad)
    joined_all = plane_gather(after(column_gather(joined_part), down_all), down_grad)
    strips = shaped((2, 4, SHORT, model_width))
    qkv_grad, bias_grad, out_kept, out_sent = kernel_call(
        place_joined_kernel,
        "place_joined",
        (shaped((half, 3 * model_width), F32), shaped((8, half), F32), strips, strips),
        (spot, *joined_all),
        16,
        5,
        1,
    )
    out_grad = kernel_call(
        place_out_kernel, "place_out", shaped((half, model_width), F32), (spot, out_kept, to_other(out_sent)), 8, 2, 1
    )
    up_grad = kernel_call(
        place_up_kernel,
        "place_up",
        shaped((half, hidden_width), F32),
        (spot, *up_all),
        16,
        4,
        1,
    )

    extra = down_part[TALL:]
    up_bias_grad = jnp.concatenate([extra[6, :half], extra[7, :half], extra[0, half:], extra[1, half:]])
    shape = (1, row_count, model_width)
    return (
        layer_out.reshape(shape),
        input_grad.reshape(shape),
        qkv_grad,
        bias_grad[0],
        bias_grad[2],
        out_grad,
        extra[0, :half],
        extra[1, :half],
        extra[2, :half],
        up_grad,
        up_bias_grad,
        down_grad,
        extra[3, :half],
        extra[4, :half],
        extra[5, :half],
    )


def solution(mesh):
    rows, halves, whole = P("shard", "seq", None), P("shard", None), P("shard")
    in_specs = (rows, rows, P(), halves, whole, whole, halves, whole, whole, whole, halves, whole, halves, whole, whole, whole)
    out_specs = (rows, rows, halves, whole, whole, halves, whole, whole, whole, halves, whole, halves, whole, whole, whole)
    return jax.shard_map(body, mesh=mesh, in_specs=in_specs, out_specs=out_specs, check_vma=False)
```

```python
import functools

import jax
import jax.numpy as jnp
from jax import lax
from jax.experimental import pallas as pl
from jax.experimental.pallas import tpu as pltpu
from jax.sharding import PartitionSpec as P

HEADS = 12
HEAD_DIM = 64
GROUPS = 4
GROUP_HEADS = HEADS // GROUPS
WIDTH = GROUP_HEADS * HEAD_DIM
EPSILON = 1e-12
MASKED = -1e30
F32 = jnp.float32
BF16 = jnp.bfloat16
MIB = 2**20
ROWS = 128
TURNED = ((1,), (1,))
FIRST = ((1,), (0,))


def dot(left, right, dims=FIRST):
    return lax.dot_general(left, right, (dims, ((), ())), preferred_element_type=F32)


def kernel_call(kernel, name, outs, args, vmem, micros, smem=0, left=(), scratch=(), after=()):
    spaces = [
        pl.BlockSpec(memory_space=pltpu.SMEM if i < smem else pltpu.HBM if i in left else pltpu.VMEM)
        for i in range(len(args))
    ]
    count = len(args)

    def run(*refs):
        kernel(*refs[:count], *refs[count + len(after) :])

    return pl.pallas_call(
        run if after else kernel,
        out_shape=outs,
        in_specs=spaces + [pl.BlockSpec(memory_space=pl.ANY)] * len(after),
        scratch_shapes=list(scratch),
        compiler_params=pltpu.CompilerParams(vmem_limit_bytes=vmem * MIB),
        cost_estimate=pl.CostEstimate(flops=0, bytes_accessed=int(micros * 3_500_000), transcendentals=0),
        name=name,
    )(*args, *after)


def in_hbm(array):
    return pltpu.with_memory_space_constraint(array, pltpu.HBM)


def shaped(shape, dtype=BF16):
    return jax.ShapeDtypeStruct(shape, dtype)


class Places:
    def __init__(self, size):
        self.size = size
        self.plane_size = size // GROUPS
        self.rest = self.plane_size // 4
        index = lambda g, q, m: (g * 4 + q) * self.rest + m
        groups, quarters, members = range(GROUPS), range(4), range(self.rest)
        self.columns = [[index(g, q, m) for g in groups] for q in quarters for m in members]
        self.planes = [[index(g, q, m) for q in quarters for m in members] for g in groups]
        self.fours = [[index(g, q, m) for q in quarters] for g in groups for m in members]
        self.sixteens = [[index(g, q, m) for g in groups for q in quarters] for m in members]
        self.rests = [[index(g, q, m) for m in members] for g in groups for q in quarters]

    def swap(self, block, bits):
        return lax.ppermute(block, "seq", [(i, i ^ bits) for i in range(self.size)])

    def column_swap(self, block, turn):
        return self.swap(block, turn * self.plane_size)

    def four_swap(self, block, turn):
        return self.swap(block, turn * self.rest)

    def exchange(self, blocks, groups):
        return lax.all_to_all(blocks, "seq", 0, 0, axis_index_groups=groups, tiled=True)


def project_kernel(x0, x1, x2, x3, weight, offset, query_ref, key_value_ref):
    for i, x in enumerate((x0, x1, x2, x3)):
        at = slice(i * ROWS, (i + 1) * ROWS)
        joined = (dot(x[...], weight[...]) + offset[...]).astype(BF16)
        query_ref[at, :] = joined[:, :WIDTH] * jnp.asarray(0.125, BF16)
        key_value_ref[at, :] = joined[:, WIDTH:]


SPAN = 512


def attend_kernel(pieces, chunks, *refs):
    q_ref = refs[0]
    key_value_refs, bias_refs = refs[1 : 1 + pieces], refs[1 + pieces : 1 + 2 * pieces]
    context_ref, log_ref = refs[1 + 2 * pieces : 3 + 2 * pieces]
    low_refs = refs[3 + 2 * pieces :]
    rows = q_ref.shape[0]
    chunk = key_value_refs[0].shape[0] // chunks
    for block in range(rows // SPAN):
        at = slice(block * SPAN, (block + 1) * SPAN)
        for head in range(GROUP_HEADS):
            columns = slice(head * HEAD_DIM, (head + 1) * HEAD_DIM)
            value_columns = slice(WIDTH + head * HEAD_DIM, WIDTH + (head + 1) * HEAD_DIM)
            query = q_ref[at, columns]

            def step(index, state):
                highest, total, mix = state
                here = pl.ds(pl.multiple_of(index * chunk, chunk), chunk)
                scores = [dot(query, k[here, columns], TURNED) + b[:, here] for k, b in zip(key_value_refs, bias_refs)]
                peak = functools.reduce(jnp.maximum, [jnp.max(s, axis=1, keepdims=True) for s in scores])
                raised = jnp.maximum(highest, peak)
                weights = [jnp.exp(s - raised) for s in scores]
                factor = jnp.exp(highest - raised)
                total = total * factor + sum(jnp.sum(w, axis=1, keepdims=True) for w in weights)
                mix = mix * factor + sum(
                    dot(w.astype(BF16), v[here, value_columns]) for w, v in zip(weights, key_value_refs)
                )
                return raised, total, mix

            state = (
                jnp.full((SPAN, 1), MASKED, F32),
                jnp.zeros((SPAN, 1), F32),
                jnp.zeros((SPAN, HEAD_DIM), F32),
            )
            highest, total, mix = step(0, state) if chunks == 1 else lax.fori_loop(0, chunks, step, state)
            context = mix / total
            context_ref[at, columns] = context
            for part in range(SPAN // ROWS):
                low = context[part * ROWS : (part + 1) * ROWS].astype(BF16)
                low_refs[block * (SPAN // ROWS) + part][:, columns] = low
            log_ref[at, head : head + 1] = highest + jnp.log(total)


def attend(query, key_values, bias, chunks):
    rows = query.shape[0]
    outs = (shaped((rows, WIDTH), F32), shaped((rows, 128), F32)) + (shaped((ROWS, WIDTH)),) * GROUPS
    kernel = functools.partial(attend_kernel, len(key_values), chunks)
    found = kernel_call(kernel, "attend", outs, (query, *key_values, *bias), 24 if chunks == 1 else 60, 9)
    return found[0], found[1], found[2:]


def attend_grad_kernel(pieces, chunks, *refs):
    q_ref, context_ref, log_ref = refs[:3]
    grad_refs = refs[3:7]
    key_value_refs, bias_refs = refs[7 : 7 + pieces], refs[7 + pieces : 7 + 2 * pieces]
    query_grad_ref = refs[7 + 2 * pieces]
    outs = refs[8 + 2 * pieces :]
    if pieces == 4:
        own_key, own_value, turned_key, turned_value, key_x, value_y = outs
        key_outs = (own_key, key_x.at[0], turned_key, key_x.at[1])
        value_outs = (own_value, turned_value, value_y.at[0], value_y.at[1])
    else:
        key_outs, value_outs = outs[:1], outs[1:]
    rows = q_ref.shape[0]
    chunk = key_value_refs[0].shape[0] // chunks
    for head in range(GROUP_HEADS):
        columns = slice(head * HEAD_DIM, (head + 1) * HEAD_DIM)
        value_columns = slice(WIDTH + head * HEAD_DIM, WIDTH + (head + 1) * HEAD_DIM)
        query = q_ref[:, columns]
        grad = jnp.concatenate([g[:, columns] for g in grad_refs], axis=0)
        correction = jnp.sum(grad.astype(F32) * context_ref[:, columns], axis=1, keepdims=True)
        log_total = log_ref[:, head : head + 1]
        query_turned = query.T
        grad_turned = grad.T

        def step(index, query_grad):
            here = pl.ds(pl.multiple_of(index * chunk, chunk), chunk)
            for both, b, key_out, value_out in zip(key_value_refs, bias_refs, key_outs, value_outs):
                key = both[here, columns]
                probs = jnp.exp(dot(query, key, TURNED) + b[:, here] - log_total)
                probs_grad = dot(grad, both[here, value_columns], TURNED)
                score_grad = (probs * (probs_grad - correction)).astype(BF16)
                query_grad = query_grad + dot(score_grad, key)
                key_out[columns, here] = dot(query_turned, score_grad).astype(BF16)
                value_out[columns, here] = dot(grad_turned, probs.astype(BF16)).astype(BF16)
            return query_grad

        total = jnp.zeros((rows, HEAD_DIM), F32)
        total = step(0, total) if chunks == 1 else lax.fori_loop(0, chunks, step, total)
        query_grad_ref[:, columns] = (total * 0.125).astype(BF16)


def attend_grad(query, context, grads, log_total, key_values, bias, chunks):
    rows, keys = query.shape[0], key_values[0].shape[0]
    one, two = shaped((WIDTH, keys)), shaped((2, WIDTH, keys))
    outs = (shaped((rows, WIDTH)),) + ((one, one, one, one, two, two) if len(key_values) == 4 else (one, one))
    kernel = functools.partial(attend_grad_kernel, len(key_values), chunks)
    args = (query, context, log_total, *grads, *key_values, *bias)
    found = kernel_call(kernel, "attend_grad", outs, args, 32 if chunks == 1 else 60, 11)
    return found[0], found[1:]


def normalize(hidden):
    center = hidden - jnp.mean(hidden, axis=1, keepdims=True)
    scale = lax.rsqrt(jnp.mean(center * center, axis=1, keepdims=True) + EPSILON)
    return center * scale, scale


def normalize_grad(grad, normal, scale):
    return scale * (
        grad
        - jnp.mean(grad, axis=1, keepdims=True)
        - normal * jnp.mean(grad * normal, axis=1, keepdims=True)
    )


def column_sum(values):
    return jnp.sum(values, axis=0, keepdims=True)


TALL, SHORT, EXTRA = 96, 24, 8
PACKED = 32


def dense_kernel(width, spot, c0, c1, c2, c3, x_ref, grad_ref, vectors, up_offset, out_hbm, up_hbm, down_hbm, *rest):
    layer_ref, one_grad_ref = rest[:2]
    branch_ref = rest[2]
    context_grads, up_parts, down_parts = rest[3:7], rest[7:11], rest[11:15]
    out_w, up_w, down_w, slope, active_ref, inner_ref, sums_ref, sems = rest[15:]
    copies = [
        pltpu.make_async_copy(source, target, sems.at[i])
        for i, (source, target) in enumerate(((out_hbm, out_w), (up_hbm, up_w), (down_hbm, down_w)))
    ]
    for copy in copies:
        copy.start()
    hidden = up_w.shape[1]
    half = width // 2
    out_offset, gain_one, shift_one, down_offset, gain_two, shift_two = (vectors[i : i + 1, :] for i in range(2, 8))
    group, quarter = spot[0], spot[1]
    contexts = (c0, c1, c2, c3)

    def turned(i):
        return pl.ds(pl.multiple_of((group ^ i) * WIDTH, WIDTH), WIDTH)

    copies[0].wait()
    branch = sum(dot(c[...], out_w[turned(i), :]) for i, c in enumerate(contexts)) + out_offset
    normal_one, scale_one = normalize(x_ref[...].astype(F32) + branch)
    normed_low = (normal_one * gain_one + shift_one).astype(BF16)
    for ref in up_parts:
        ref[:, :width] = normed_low
    copies[1].wait()
    step = 768
    for start in range(0, hidden, step):
        at = slice(start, start + step)
        inner = dot(normed_low, up_w[:, at]) + up_offset[:, at]
        share = 0.5 + 0.5 * lax.erf(inner * 0.7071067811865476)
        density = 0.3989422804014327 * jnp.exp(-0.5 * inner * inner)
        slope[:, at] = share + inner * density
        active_ref[:, at] = (inner * share).astype(BF16)
    copies[2].wait()
    second = dot(active_ref[...], down_w[...]) + down_offset
    normal_two, scale_two = normalize(normed_low.astype(F32) + second)
    layer_ref[...] = (normal_two * gain_two + shift_two).astype(BF16)
    grad = grad_ref[...].astype(F32)
    gain_two_grad, shift_two_grad = column_sum(grad * normal_two), column_sum(grad)
    two_grad = normalize_grad(grad * gain_two, normal_two, scale_two)
    second_low = two_grad.astype(BF16)
    down_bias_grad = column_sum(second_low.astype(F32))
    normed_grad = two_grad
    for start in range(0, hidden, step):
        at = slice(start, start + step)
        inner_low = (dot(second_low, down_w[at, :], TURNED) * slope[:, at]).astype(BF16)
        inner_ref[:, at] = inner_low
        up_sum = column_sum(inner_low.astype(F32))
        for piece in range(step // half):
            place = start // half + piece
            per_core = hidden // 2 // half
            row, core = 6 + place % per_core, place // per_core
            sums_ref[row : row + 1, core * half : (core + 1) * half] = up_sum[:, piece * half : (piece + 1) * half]
        normed_grad = normed_grad + dot(inner_low, up_w[:, at], TURNED)
    gain_one_grad, shift_one_grad = column_sum(normed_grad * normal_one), column_sum(normed_grad)
    one_grad = normalize_grad(normed_grad * gain_one, normal_one, scale_one)
    one_grad_ref[...] = one_grad
    branch_low = one_grad.astype(BF16)
    branch_ref[...] = branch_low
    for i, ref in enumerate(context_grads):
        ref[...] = dot(branch_low, out_w[turned(i), :], TURNED).astype(BF16)
    out_bias_grad = column_sum(branch_low.astype(F32))
    sums = (out_bias_grad, gain_one_grad, shift_one_grad, down_bias_grad, gain_two_grad, shift_two_grad)
    for i, total in enumerate(sums):
        sums_ref[i : i + 1, :] = total
    sums_ref[10:16, :] = jnp.zeros((6, width), F32)
    share = hidden // 8
    for i in range(4):
        for core in range(2):
            at = pl.ds(pl.multiple_of(core * (hidden // 2) + (quarter ^ i) * share, share), share)
            to = slice(width + core * share, width + (core + 1) * share)
            up_parts[i][:, to] = inner_ref[:, at]
            down_parts[i][:ROWS, to] = active_ref[:, at]
        down_parts[i][:ROWS, :width] = second_low
        down_parts[i][ROWS:, :width] = sums_ref[...].astype(BF16)


def dense(spot, contexts, inputs, grad, vectors, up_offset, out_matrix, up_matrix, down_matrix):
    width, hidden = up_matrix.shape
    outs = (
        (shaped((ROWS, width)), shaped((ROWS, width), F32), shaped((ROWS, width)))
        + (shaped((ROWS, WIDTH)),) * GROUPS
        + (shaped((ROWS, width + hidden // 4)),) * 4
        + (shaped((ROWS + 16, width + hidden // 4)),) * 4
    )
    scratch = (
        pltpu.VMEM(out_matrix.shape, BF16),
        pltpu.VMEM(up_matrix.shape, BF16),
        pltpu.VMEM(down_matrix.shape, BF16),
        pltpu.VMEM((ROWS, hidden), F32),
        pltpu.VMEM((ROWS, hidden), BF16),
        pltpu.VMEM((ROWS, hidden), BF16),
        pltpu.VMEM((16, width), F32),
        pltpu.SemaphoreType.DMA((3,)),
    )
    args = (spot, *contexts, inputs, grad, vectors, up_offset, out_matrix, up_matrix, down_matrix)
    found = kernel_call(
        functools.partial(dense_kernel, width), "dense", outs, args, 22, 10, 1, (9, 10, 11), scratch
    )
    return found[:3], found[3:7], found[7:11], found[11:15]


def halves_of(spot, first, second):
    return ((first, 1 - spot[2]), (second, spot[2]))


def up_grad_kernel(spot, p0, p1, p2, p3, other_ref, own_ref, turned, inner):
    width = turned.shape[0]
    for i, part in enumerate((p0, p1, p2, p3)):
        turned[:, i * ROWS : (i + 1) * ROWS] = part[:, :width].T
        inner[i * ROWS : (i + 1) * ROWS, :] = part[:, width:]
    half = width // 2
    for ref, core in halves_of(spot, other_ref, own_ref):
        value = dot(turned[pl.ds(pl.multiple_of(core * half, half), half), :], inner[...]).astype(BF16)
        for g in range(GROUPS):
            ref[g] = value[g * TALL : (g + 1) * TALL]


def up_grad_parts(spot, parts, width):
    tokens, columns = 4 * ROWS, parts[0].shape[1] - width
    out = shaped((GROUPS, TALL, columns))
    scratch = (pltpu.VMEM((width, tokens), BF16), pltpu.VMEM((tokens, columns), BF16))
    return kernel_call(up_grad_kernel, "up_grad", (out, out), (spot, *parts), 16, 4, 1, (), scratch)


def down_grad_kernel(spot, p0, p1, p2, p3, other_ref, own_ref, turned, second, sums):
    parts = (p0, p1, p2, p3)
    width = second.shape[1]
    tall = GROUPS * TALL
    for i, part in enumerate(parts):
        rows = slice(i * ROWS, (i + 1) * ROWS)
        turned[:, rows] = part[:ROWS, width:].T
        second[rows, :] = part[:ROWS, :width]
    total = sum(part[ROWS:, :width].astype(F32) for part in parts)
    for core in range(2):
        start = core * (width // 2)
        sums[core] = jnp.concatenate(
            [total[:EXTRA, start : start + width // 2], total[EXTRA:, start : start + width // 2]], axis=1
        )
    for ref, core in halves_of(spot, other_ref, own_ref):
        down = dot(turned[pl.ds(pl.multiple_of(core * tall, tall), tall), :], second[...])
        for g in range(GROUPS):
            ref[g] = jnp.concatenate([down[g * TALL : (g + 1) * TALL], sums[core]], axis=0).astype(BF16)


def down_grad_parts(spot, parts, width):
    tokens = 4 * ROWS
    out = shaped((GROUPS, TALL + EXTRA, width))
    scratch = (
        pltpu.VMEM((2 * GROUPS * TALL, tokens), BF16),
        pltpu.VMEM((tokens, width), BF16),
        pltpu.VMEM((2, EXTRA, width), F32),
    )
    return kernel_call(down_grad_kernel, "down_grad", (out, out), (spot, *parts), 16, 5, 1, (), scratch)


def pair_sum_kernel(which, turns, spot, own, received, kept, sent):
    for i, out in zip(turns, (sent.at[0], sent.at[1], kept.at[1], kept.at[0])):
        at = spot[which] ^ i
        out[...] = (own[at].astype(F32) + received[at].astype(F32)).astype(BF16)


def pair_sums(spot, own, received, name, which=0, turns=(1, 2, 3, 0)):
    pair = shaped((2, *own.shape[1:]))
    kernel = functools.partial(pair_sum_kernel, which, turns)
    return kernel_call(kernel, name, (pair, pair), (spot, own, received), 16, 2, 1)


def placed(spot, pieces):
    group, quarter = spot[0], spot[1]
    for i in range(4):
        for g in range(GROUPS):
            turn = group ^ g
            at = ((turn & 1) << 1) ^ ((turn >> 1) * 3)
            if i < 3:
                block = pieces[i][at]
            else:
                block = jnp.where(at < 2, pieces[3][at & 1], pieces[4][at & 1])
            yield quarter ^ i, g, block


def place_up_kernel(spot, *refs):
    up_ref = refs[-1]
    for quarter, g, block in placed(spot, refs[:-1]):
        share = block.shape[1] // 2
        block = block.astype(F32)
        for core in range(2):
            at = pl.ds(pl.multiple_of(core * 4 * share + quarter * share, 128), share)
            up_ref[g * TALL : (g + 1) * TALL, at] = block[:, core * share : (core + 1) * share]


BIAS_ROWS = 16


def joined_grad_kernel(pieces, spot, query_grad, *rest):
    keys, values = rest[:pieces], rest[pieces : 2 * pieces]
    inputs = rest[2 * pieces : 2 * pieces + 4]
    contexts = rest[2 * pieces + 4 : 2 * pieces + 8]
    branches = rest[2 * pieces + 8 : 2 * pieces + 12]
    weight, other_ref, own_ref, kept_ref, sent_ref, joined, turned, context_turned, branch = rest[2 * pieces + 12 :]

    def total(parts):
        blocks = [p[0] if len(p.shape) == 3 else p[...] for p in parts]
        return sum(b.astype(F32) for b in blocks).T.astype(BF16)

    joined[:, :WIDTH] = query_grad[...]
    joined[:, WIDTH : 2 * WIDTH] = total(keys)
    joined[:, 2 * WIDTH :] = total(values)
    for i, ref in ((1, sent_ref.at[0]), (2, sent_ref.at[1]), (3, kept_ref.at[1]), (0, kept_ref.at[0])):
        ref[...] = dot(joined[i * ROWS : (i + 1) * ROWS, :], weight[...], TURNED).astype(BF16)
    for i, x in enumerate(inputs):
        at = slice(i * ROWS, (i + 1) * ROWS)
        turned[:, at] = x[...].T
        context_turned[:, at] = contexts[i][...].T
        branch[at, :] = branches[i][...]
    sums = jnp.concatenate(
        [column_sum(joined[...].astype(F32)), jnp.zeros((BIAS_ROWS - 1, 3 * WIDTH), F32)], axis=0
    ).astype(BF16)
    half = turned.shape[0] // 2
    for ref, core in halves_of(spot, other_ref, own_ref):
        value = dot(turned[pl.ds(pl.multiple_of(core * half, half), half), :], joined[...]).astype(BF16)
        strip = WIDTH // 2
        out = dot(context_turned[pl.ds(pl.multiple_of(core * strip, 32), strip), :], branch[...])
        for quarter in range(4):
            ref[quarter, :TALL, :] = value[quarter * TALL : (quarter + 1) * TALL]
            block = out[quarter * SHORT : (quarter + 1) * SHORT]
            last = jnp.concatenate([block[k * 8 : k * 8 + 8, 3 * WIDTH :] for k in range(3)], axis=1)
            packed = jnp.concatenate([block[:, : 3 * WIDTH], last], axis=0)
            ref[quarter, TALL : TALL + PACKED, :] = packed.astype(BF16)
            ref[quarter, TALL + PACKED :, :] = sums


def joined_grads(spot, query_grad, keys, values, inputs, contexts, branches, weight):
    width = weight.shape[0]
    part, pair = shaped((4, TALL + PACKED + BIAS_ROWS, 3 * WIDTH)), shaped((2, ROWS, width))
    tokens = GROUPS * ROWS
    scratch = (
        pltpu.VMEM((tokens, 3 * WIDTH), BF16),
        pltpu.VMEM((width, tokens), BF16),
        pltpu.VMEM((WIDTH, tokens), BF16),
        pltpu.VMEM((tokens, width), BF16),
    )
    args = (spot, query_grad, *keys, *values, *inputs, *contexts, *branches, weight)
    kernel = functools.partial(joined_grad_kernel, len(keys))
    return kernel_call(kernel, "joined_grad", (part, part, pair, pair), args, 16, 6, 1, (), scratch)


def place_down_kernel(spot, *refs):
    down_ref = refs[-1]
    for quarter, g, block in placed(spot, refs[:-1]):
        place = quarter * GROUPS + g
        down_ref[pl.ds(pl.multiple_of(place * TALL, 8), TALL), :] = block.astype(F32)


def place_joined_kernel(spot, *refs):
    weight_ref, bias_ref, kept_ref, sent_ref = refs[-4:]
    core = spot[2]
    width = weight_ref.shape[1] // 3
    found = list(placed(spot, refs[:-4]))
    rows = TALL
    for i in range(4):
        quarter = found[i * GROUPS][0]
        blocks = [block.astype(F32) for _, _, block in found[i * GROUPS : (i + 1) * GROUPS]]
        at = pl.ds(pl.multiple_of(quarter * rows, 16), rows)
        for part in range(3):
            value = jnp.concatenate([b[:, part * WIDTH : (part + 1) * WIDTH] for b in blocks], axis=1)
            weight_ref[at, part * width : (part + 1) * width] = value[:rows]
            if i == 0:
                line = value[rows + PACKED : rows + PACKED + 1]
                bias_ref[part : part + 1, :] = jnp.where(core == 0, line[:, : width // 2], line[:, width // 2 :])
        for g, block in enumerate(blocks):
            last = block[rows + SHORT : rows + PACKED]
            last = jnp.concatenate([last[:, k * WIDTH : (k + 1) * WIDTH] for k in range(3)], axis=0)
            strip = jnp.concatenate([block[rows : rows + SHORT], last], axis=1).astype(BF16)
            target = g // 2

            @pl.when(core == target)
            def _():
                kept_ref[g % 2, quarter] = strip

            @pl.when(core != target)
            def _():
                sent_ref[g % 2, quarter] = strip


def place_out_kernel(spot, kept, received, out_ref):
    core = spot[2]
    for g in range(2):
        for ref, side in ((kept, core), (received, 1 - core)):
            for quarter in range(4):
                start = g * WIDTH + side * (WIDTH // 2) + quarter * SHORT
                out_ref[pl.ds(pl.multiple_of(start, 8), SHORT), :] = ref[g, quarter].astype(F32)


def body(
    tokens,
    cotangent,
    lengths,
    qkv_weight,
    query_bias,
    value_bias,
    out_weight,
    out_bias,
    first_gain,
    first_shift,
    up_weight,
    up_bias,
    down_weight,
    down_bias,
    second_gain,
    second_shift,
):
    row_count, model_width = tokens.shape[1], tokens.shape[2]
    hidden_width = up_weight.shape[1]
    places = Places(lax.axis_size("seq"))
    plane_size, rest = places.plane_size, places.rest
    rank = lax.axis_index("seq")
    core = lax.axis_index("shard")
    group, position = rank // plane_size, rank % plane_size
    quarter = position // rest
    spot = jnp.stack([group, quarter, core]).astype(jnp.int32)
    length = lengths[core]
    inputs = tokens[0]
    column_rows = GROUPS * row_count
    half = model_width // 2
    turns = range(1, GROUPS)

    column_inputs = (inputs, *(places.column_swap(inputs, i) for i in turns))

    def both(block):
        return lax.all_gather(block, "shard", axis=0, tiled=True)

    def own_columns(w):
        at = group * WIDTH
        parts = [lax.dynamic_slice_in_dim(w, at + i * model_width, WIDTH, w.ndim - 1) for i in range(3)]
        return jnp.concatenate(parts, axis=-1)

    group_weight = both(own_columns(qkv_weight))
    vectors = [query_bias, value_bias, out_bias, first_gain, first_shift, down_bias, second_gain, second_shift]
    stacked = jnp.concatenate([jnp.stack(vectors), up_bias.reshape(-1, half)])
    stacked = lax.all_gather(stacked, "shard", axis=0).astype(F32)
    whole = jnp.transpose(stacked[:, : len(vectors)], (1, 0, 2)).reshape(len(vectors), model_width)
    up_offset = stacked[:, len(vectors) :].reshape(1, hidden_width)
    out_matrix = in_hbm(both(out_weight))
    up_matrix = in_hbm(both(up_weight))
    down_matrix = in_hbm(both(down_weight))

    offset = own_columns(jnp.concatenate([whole[0], jnp.zeros_like(whole[0]), whole[1]])).reshape(1, -1)
    query, key_value = kernel_call(
        project_kernel,
        "project",
        (shaped((column_rows, WIDTH)), shaped((column_rows, 2 * WIDTH))),
        (*column_inputs, group_weight, offset),
        16,
        2,
    )

    def masks(who):
        groups = group ^ jnp.arange(GROUPS)
        starts = (groups[None, :] * plane_size + who[:, None]) * row_count
        tokens_at = starts[:, :, None] + jnp.arange(row_count)
        return jnp.where(tokens_at.reshape(1, -1) < length, 0.0, MASKED).astype(F32)

    if plane_size == 4:
        chunks = 1
        key_values = (key_value, *(places.swap(key_value, i) for i in turns))
        bias = tuple(masks((position ^ i)[None]) for i in range(4))
    else:
        chunks = plane_size // 4
        gathered = lax.all_gather(key_value, "seq", axis=0, axis_index_groups=places.planes)
        key_values = (gathered.reshape(-1, 2 * WIDTH),)
        bias = (masks(jnp.arange(plane_size)),)
    context, log_total, context_lows = attend(query, key_values, bias, chunks)
    contexts = (context_lows[0], *(places.column_swap(context_lows[i], i) for i in turns))

    (layer_out, one_grad, branch_low), context_grads, up_parts, down_parts = dense(
        spot, contexts, inputs, cotangent[0], whole, up_offset, out_matrix, up_matrix, down_matrix
    )
    def after(value, *others):
        return lax.optimization_barrier((value, *others))[0]

    def to_other(block):
        return lax.ppermute(block, "shard", [(0, 1), (1, 0)])

    def rest_sum(total):
        return lax.psum(total, "seq", axis_index_groups=places.rests) if rest > 1 else total

    def add(left, right):
        return (left.astype(F32) + right.astype(F32)).astype(BF16)

    def column_total(kept, sent):
        near = places.column_swap(sent, 1)
        far = places.column_swap(add(kept[1], near[1]), 3)
        return kept[0].astype(F32) + near[0].astype(F32) + far.astype(F32)

    def four_total(kept, sent):
        near = places.four_swap(sent, 1)
        far = places.four_swap(add(kept[1], near[1]), 2)
        return kept[0].astype(F32) + near[0].astype(F32) + far.astype(F32)

    def column_gather(part):
        pair = jnp.stack([part, places.column_swap(part, 3)])
        return jnp.concatenate([pair, places.column_swap(pair, 1)])

    def plane_gather(column, *others):
        first, second = places.four_swap(column, 1), places.four_swap(column, 2)
        halves = (first[:2], second[2:])
        if others:
            halves = after(halves, *others)
        return column, first, second, places.four_swap(halves[0], 2), places.four_swap(halves[1], 1)

    context_grads = (context_grads[0], *(places.column_swap(context_grads[i], i) for i in turns))
    down_parts = (down_parts[0], *(places.four_swap(down_parts[i], i) for i in turns))
    query_grad, parts = attend_grad(query, context, context_grads, log_total, key_values, bias, chunks)
    if plane_size == 4:
        own_key, own_value, turned_key, turned_value, key_x, value_y = parts
        key_x, value_y = first_step = places.swap(key_x, 1), places.swap(value_y, 2)
        keys = (own_key, key_x, places.swap(add(turned_key, key_x[1]), 2))
        values = (own_value, value_y, places.swap(add(turned_value, value_y[1]), 1))
    else:
        blocks = jnp.stack(parts).reshape(2 * WIDTH, plane_size, column_rows)
        blocks = places.exchange(jnp.transpose(blocks, (1, 0, 2)), places.planes)
        blocks = jnp.sum(blocks.astype(F32), axis=0)
        keys, values = first_step = (blocks[:WIDTH],), (blocks[WIDTH:],)
    branch_low = after(branch_low, first_step)
    far = places.column_swap(branch_low, 3)
    branches = (branch_low, places.column_swap(branch_low, 1), places.column_swap(far, 1), far)
    down_parts = after(down_parts, query_grad)
    other, own = down_grad_parts(spot, down_parts, model_width)
    down_pieces = pair_sums(spot, own, to_other(other), "down_sum")
    down_part = rest_sum(column_total(*down_pieces))
    up_parts = after(up_parts, query_grad)
    up_parts = (up_parts[0], *(places.four_swap(up_parts[i], i) for i in turns))
    keys, values = after((keys, values), down_part, up_parts)
    down_column = column_gather(down_part[:TALL].astype(BF16))
    other, own, kept, sent = joined_grads(
        spot, query_grad, keys, values, column_inputs, context_lows, branches, group_weight
    )
    input_grad = one_grad + column_total(kept, sent)
    joined_pieces = pair_sums(spot, own, to_other(other), "joined_sum", 1, (1, 3, 2, 0))
    joined_part = rest_sum(four_total(*joined_pieces)).astype(BF16)
    up_parts = after(up_parts, kept)
    other, own = up_grad_parts(spot, up_parts, model_width)
    up_part = rest_sum(column_total(*pair_sums(spot, own, to_other(other), "up_sum"))).astype(BF16)
    down_all = plane_gather(down_column)
    down_grad = kernel_call(
        place_down_kernel,
        "place_down",
        shaped((hidden_width // 2, model_width), F32),
        (spot, *down_all),
        16,
        5,
        1,
    )
    up_all = plane_gather(after(column_gather(up_part), down_all), down_grad)
    joined_all = plane_gather(after(column_gather(joined_part), down_all), down_grad)
    strips = shaped((2, 4, SHORT, model_width))
    qkv_grad, bias_grad, out_kept, out_sent = kernel_call(
        place_joined_kernel,
        "place_joined",
        (shaped((half, 3 * model_width), F32), shaped((8, half), F32), strips, strips),
        (spot, *joined_all),
        16,
        5,
        1,
    )
    out_grad = kernel_call(
        place_out_kernel, "place_out", shaped((half, model_width), F32), (spot, out_kept, to_other(out_sent)), 8, 2, 1
    )
    up_grad = kernel_call(
        place_up_kernel,
        "place_up",
        shaped((half, hidden_width), F32),
        (spot, *up_all),
        16,
        4,
        1,
    )

    extra = down_part[TALL:]
    up_bias_grad = jnp.concatenate([extra[6, :half], extra[7, :half], extra[0, half:], extra[1, half:]])
    shape = (1, row_count, model_width)
    return (
        layer_out.reshape(shape),
        input_grad.reshape(shape),
        qkv_grad,
        bias_grad[0],
        bias_grad[2],
        out_grad,
        extra[0, :half],
        extra[1, :half],
        extra[2, :half],
        up_grad,
        up_bias_grad,
        down_grad,
        extra[3, :half],
        extra[4, :half],
        extra[5, :half],
    )


def solution(mesh):
    rows, halves, whole = P("shard", "seq", None), P("shard", None), P("shard")
    in_specs = (rows, rows, P(), halves, whole, whole, halves, whole, whole, whole, halves, whole, halves, whole, whole, whole)
    out_specs = (rows, rows, halves, whole, whole, halves, whole, whole, whole, halves, whole, halves, whole, whole, whole)
    return jax.shard_map(body, mesh=mesh, in_specs=in_specs, out_specs=out_specs, check_vma=False)
```

```python
import functools

import jax
import jax.numpy as jnp
from jax import lax
from jax.experimental import pallas as pl
from jax.experimental.pallas import tpu as pltpu
from jax.sharding import PartitionSpec as P

HEADS = 12
HEAD_DIM = 64
GROUPS = 4
GROUP_HEADS = HEADS // GROUPS
WIDTH = GROUP_HEADS * HEAD_DIM
EPSILON = 1e-12
MASKED = -1e30
F32 = jnp.float32
BF16 = jnp.bfloat16
MIB = 2**20
ROWS = 128
TURNED = ((1,), (1,))
FIRST = ((1,), (0,))


def dot(left, right, dims=FIRST):
    return lax.dot_general(left, right, (dims, ((), ())), preferred_element_type=F32)


def kernel_call(kernel, name, outs, args, vmem, micros, smem=0, left=(), scratch=(), after=()):
    spaces = [
        pl.BlockSpec(memory_space=pltpu.SMEM if i < smem else pltpu.HBM if i in left else pltpu.VMEM)
        for i in range(len(args))
    ]
    count = len(args)

    def run(*refs):
        kernel(*refs[:count], *refs[count + len(after) :])

    return pl.pallas_call(
        run if after else kernel,
        out_shape=outs,
        in_specs=spaces + [pl.BlockSpec(memory_space=pl.ANY)] * len(after),
        scratch_shapes=list(scratch),
        compiler_params=pltpu.CompilerParams(vmem_limit_bytes=vmem * MIB),
        cost_estimate=pl.CostEstimate(flops=0, bytes_accessed=int(micros * 3_500_000), transcendentals=0),
        name=name,
    )(*args, *after)


def in_hbm(array):
    return pltpu.with_memory_space_constraint(array, pltpu.HBM)


def shaped(shape, dtype=BF16):
    return jax.ShapeDtypeStruct(shape, dtype)


class Places:
    def __init__(self, size):
        self.size = size
        self.plane_size = size // GROUPS
        self.rest = self.plane_size // 4
        index = lambda g, q, m: (g * 4 + q) * self.rest + m
        groups, quarters, members = range(GROUPS), range(4), range(self.rest)
        self.columns = [[index(g, q, m) for g in groups] for q in quarters for m in members]
        self.planes = [[index(g, q, m) for q in quarters for m in members] for g in groups]
        self.fours = [[index(g, q, m) for q in quarters] for g in groups for m in members]
        self.sixteens = [[index(g, q, m) for g in groups for q in quarters] for m in members]
        self.rests = [[index(g, q, m) for m in members] for g in groups for q in quarters]

    def swap(self, block, bits):
        return lax.ppermute(block, "seq", [(i, i ^ bits) for i in range(self.size)])

    def column_swap(self, block, turn):
        return self.swap(block, turn * self.plane_size)

    def four_swap(self, block, turn):
        return self.swap(block, turn * self.rest)

    def exchange(self, blocks, groups):
        return lax.all_to_all(blocks, "seq", 0, 0, axis_index_groups=groups, tiled=True)


def project_kernel(x0, x1, x2, x3, weight, offset, query_ref, key_value_ref):
    for i, x in enumerate((x0, x1, x2, x3)):
        at = slice(i * ROWS, (i + 1) * ROWS)
        joined = (dot(x[...], weight[...]) + offset[...]).astype(BF16)
        query_ref[at, :] = joined[:, :WIDTH] * jnp.asarray(0.125, BF16)
        key_value_ref[at, :] = joined[:, WIDTH:]


SPAN = 512


def attend_kernel(pieces, chunks, *refs):
    q_ref = refs[0]
    key_value_refs, bias_refs = refs[1 : 1 + pieces], refs[1 + pieces : 1 + 2 * pieces]
    context_ref, log_ref = refs[1 + 2 * pieces : 3 + 2 * pieces]
    low_refs = refs[3 + 2 * pieces :]
    rows = q_ref.shape[0]
    chunk = key_value_refs[0].shape[0] // chunks
    for block in range(rows // SPAN):
        at = slice(block * SPAN, (block + 1) * SPAN)
        for head in range(GROUP_HEADS):
            columns = slice(head * HEAD_DIM, (head + 1) * HEAD_DIM)
            value_columns = slice(WIDTH + head * HEAD_DIM, WIDTH + (head + 1) * HEAD_DIM)
            query = q_ref[at, columns]

            def step(index, state):
                highest, total, mix = state
                here = pl.ds(pl.multiple_of(index * chunk, chunk), chunk)
                scores = [dot(query, k[here, columns], TURNED) + b[:, here] for k, b in zip(key_value_refs, bias_refs)]
                peak = functools.reduce(jnp.maximum, [jnp.max(s, axis=1, keepdims=True) for s in scores])
                raised = jnp.maximum(highest, peak)
                weights = [jnp.exp(s - raised) for s in scores]
                factor = jnp.exp(highest - raised)
                total = total * factor + sum(jnp.sum(w, axis=1, keepdims=True) for w in weights)
                mix = mix * factor + sum(
                    dot(w.astype(BF16), v[here, value_columns]) for w, v in zip(weights, key_value_refs)
                )
                return raised, total, mix

            state = (
                jnp.full((SPAN, 1), MASKED, F32),
                jnp.zeros((SPAN, 1), F32),
                jnp.zeros((SPAN, HEAD_DIM), F32),
            )
            highest, total, mix = step(0, state) if chunks == 1 else lax.fori_loop(0, chunks, step, state)
            context = mix / total
            context_ref[at, columns] = context
            for part in range(SPAN // ROWS):
                low = context[part * ROWS : (part + 1) * ROWS].astype(BF16)
                low_refs[block * (SPAN // ROWS) + part][:, columns] = low
            log_ref[at, head : head + 1] = highest + jnp.log(total)


def attend(query, key_values, bias, chunks):
    rows = query.shape[0]
    outs = (shaped((rows, WIDTH), F32), shaped((rows, 128), F32)) + (shaped((ROWS, WIDTH)),) * GROUPS
    kernel = functools.partial(attend_kernel, len(key_values), chunks)
    found = kernel_call(kernel, "attend", outs, (query, *key_values, *bias), 24 if chunks == 1 else 60, 9)
    return found[0], found[1], found[2:]


def attend_grad_kernel(pieces, chunks, *refs):
    q_ref, context_ref, log_ref = refs[:3]
    grad_refs = refs[3:7]
    key_value_refs, bias_refs = refs[7 : 7 + pieces], refs[7 + pieces : 7 + 2 * pieces]
    query_grad_ref = refs[7 + 2 * pieces]
    outs = refs[8 + 2 * pieces :]
    if pieces == 4:
        own_key, own_value, turned_key, turned_value, key_x, value_y = outs
        key_outs = (own_key, key_x.at[0], turned_key, key_x.at[1])
        value_outs = (own_value, turned_value, value_y.at[0], value_y.at[1])
    else:
        key_outs, value_outs = outs[:1], outs[1:]
    rows = q_ref.shape[0]
    chunk = key_value_refs[0].shape[0] // chunks
    for head in range(GROUP_HEADS):
        columns = slice(head * HEAD_DIM, (head + 1) * HEAD_DIM)
        value_columns = slice(WIDTH + head * HEAD_DIM, WIDTH + (head + 1) * HEAD_DIM)
        query = q_ref[:, columns]
        grad = jnp.concatenate([g[:, columns] for g in grad_refs], axis=0)
        correction = jnp.sum(grad.astype(F32) * context_ref[:, columns], axis=1, keepdims=True)
        log_total = log_ref[:, head : head + 1]
        query_turned = query.T
        grad_turned = grad.T

        def step(index, query_grad):
            here = pl.ds(pl.multiple_of(index * chunk, chunk), chunk)
            for both, b, key_out, value_out in zip(key_value_refs, bias_refs, key_outs, value_outs):
                key = both[here, columns]
                probs = jnp.exp(dot(query, key, TURNED) + b[:, here] - log_total)
                probs_grad = dot(grad, both[here, value_columns], TURNED)
                score_grad = (probs * (probs_grad - correction)).astype(BF16)
                query_grad = query_grad + dot(score_grad, key)
                key_out[columns, here] = dot(query_turned, score_grad).astype(BF16)
                value_out[columns, here] = dot(grad_turned, probs.astype(BF16)).astype(BF16)
            return query_grad

        total = jnp.zeros((rows, HEAD_DIM), F32)
        total = step(0, total) if chunks == 1 else lax.fori_loop(0, chunks, step, total)
        query_grad_ref[:, columns] = (total * 0.125).astype(BF16)


def attend_grad(query, context, grads, log_total, key_values, bias, chunks):
    rows, keys = query.shape[0], key_values[0].shape[0]
    one, two = shaped((WIDTH, keys)), shaped((2, WIDTH, keys))
    outs = (shaped((rows, WIDTH)),) + ((one, one, one, one, two, two) if len(key_values) == 4 else (one, one))
    kernel = functools.partial(attend_grad_kernel, len(key_values), chunks)
    args = (query, context, log_total, *grads, *key_values, *bias)
    found = kernel_call(kernel, "attend_grad", outs, args, 32 if chunks == 1 else 60, 11)
    return found[0], found[1:]


def normalize(hidden):
    center = hidden - jnp.mean(hidden, axis=1, keepdims=True)
    scale = lax.rsqrt(jnp.mean(center * center, axis=1, keepdims=True) + EPSILON)
    return center * scale, scale


def normalize_grad(grad, normal, scale):
    return scale * (
        grad
        - jnp.mean(grad, axis=1, keepdims=True)
        - normal * jnp.mean(grad * normal, axis=1, keepdims=True)
    )


def column_sum(values):
    return jnp.sum(values, axis=0, keepdims=True)


TALL, SHORT, EXTRA = 96, 24, 8
PACKED = 32


def dense_kernel(width, spot, c0, c1, c2, c3, x_ref, grad_ref, vectors, up_offset, out_hbm, up_hbm, down_hbm, *rest):
    layer_ref, one_grad_ref = rest[:2]
    branch_ref = rest[2]
    context_grads, up_parts, down_parts = rest[3:7], rest[7:11], rest[11:15]
    out_w, up_w, down_w, slope, active_ref, inner_ref, sums_ref, sems = rest[15:]
    copies = [
        pltpu.make_async_copy(source, target, sems.at[i])
        for i, (source, target) in enumerate(((out_hbm, out_w), (up_hbm, up_w), (down_hbm, down_w)))
    ]
    for copy in copies:
        copy.start()
    hidden = up_w.shape[1]
    half = width // 2
    out_offset, gain_one, shift_one, down_offset, gain_two, shift_two = (vectors[i : i + 1, :] for i in range(2, 8))
    group, quarter = spot[0], spot[1]
    contexts = (c0, c1, c2, c3)

    def turned(i):
        return pl.ds(pl.multiple_of((group ^ i) * WIDTH, WIDTH), WIDTH)

    copies[0].wait()
    branch = sum(dot(c[...], out_w[turned(i), :]) for i, c in enumerate(contexts)) + out_offset
    normal_one, scale_one = normalize(x_ref[...].astype(F32) + branch)
    normed_low = (normal_one * gain_one + shift_one).astype(BF16)
    for ref in up_parts:
        ref[:, :width] = normed_low
    copies[1].wait()
    step = 768
    for start in range(0, hidden, step):
        at = slice(start, start + step)
        inner = dot(normed_low, up_w[:, at]) + up_offset[:, at]
        share = 0.5 + 0.5 * lax.erf(inner * 0.7071067811865476)
        density = 0.3989422804014327 * jnp.exp(-0.5 * inner * inner)
        slope[:, at] = share + inner * density
        active_ref[:, at] = (inner * share).astype(BF16)
    copies[2].wait()
    second = dot(active_ref[...], down_w[...]) + down_offset
    normal_two, scale_two = normalize(normed_low.astype(F32) + second)
    layer_ref[...] = (normal_two * gain_two + shift_two).astype(BF16)
    grad = grad_ref[...].astype(F32)
    gain_two_grad, shift_two_grad = column_sum(grad * normal_two), column_sum(grad)
    two_grad = normalize_grad(grad * gain_two, normal_two, scale_two)
    second_low = two_grad.astype(BF16)
    down_bias_grad = column_sum(second_low.astype(F32))
    normed_grad = two_grad
    for start in range(0, hidden, step):
        at = slice(start, start + step)
        inner_low = (dot(second_low, down_w[at, :], TURNED) * slope[:, at]).astype(BF16)
        inner_ref[:, at] = inner_low
        up_sum = column_sum(inner_low.astype(F32))
        for piece in range(step // half):
            place = start // half + piece
            per_core = hidden // 2 // half
            row, core = 6 + place % per_core, place // per_core
            sums_ref[row : row + 1, core * half : (core + 1) * half] = up_sum[:, piece * half : (piece + 1) * half]
        normed_grad = normed_grad + dot(inner_low, up_w[:, at], TURNED)
    gain_one_grad, shift_one_grad = column_sum(normed_grad * normal_one), column_sum(normed_grad)
    one_grad = normalize_grad(normed_grad * gain_one, normal_one, scale_one)
    one_grad_ref[...] = one_grad
    branch_low = one_grad.astype(BF16)
    branch_ref[...] = branch_low
    for i, ref in enumerate(context_grads):
        ref[...] = dot(branch_low, out_w[turned(i), :], TURNED).astype(BF16)
    out_bias_grad = column_sum(branch_low.astype(F32))
    sums = (out_bias_grad, gain_one_grad, shift_one_grad, down_bias_grad, gain_two_grad, shift_two_grad)
    for i, total in enumerate(sums):
        sums_ref[i : i + 1, :] = total
    sums_ref[10:16, :] = jnp.zeros((6, width), F32)
    share = hidden // 8
    for i in range(4):
        for core in range(2):
            at = pl.ds(pl.multiple_of(core * (hidden // 2) + (quarter ^ i) * share, share), share)
            to = slice(width + core * share, width + (core + 1) * share)
            up_parts[i][:, to] = inner_ref[:, at]
            down_parts[i][:ROWS, to] = active_ref[:, at]
        down_parts[i][:ROWS, :width] = second_low
        down_parts[i][ROWS:, :width] = sums_ref[...].astype(BF16)


def dense(spot, contexts, inputs, grad, vectors, up_offset, out_matrix, up_matrix, down_matrix):
    width, hidden = up_matrix.shape
    outs = (
        (shaped((ROWS, width)), shaped((ROWS, width), F32), shaped((ROWS, width)))
        + (shaped((ROWS, WIDTH)),) * GROUPS
        + (shaped((ROWS, width + hidden // 4)),) * 4
        + (shaped((ROWS + 16, width + hidden // 4)),) * 4
    )
    scratch = (
        pltpu.VMEM(out_matrix.shape, BF16),
        pltpu.VMEM(up_matrix.shape, BF16),
        pltpu.VMEM(down_matrix.shape, BF16),
        pltpu.VMEM((ROWS, hidden), F32),
        pltpu.VMEM((ROWS, hidden), BF16),
        pltpu.VMEM((ROWS, hidden), BF16),
        pltpu.VMEM((16, width), F32),
        pltpu.SemaphoreType.DMA((3,)),
    )
    args = (spot, *contexts, inputs, grad, vectors, up_offset, out_matrix, up_matrix, down_matrix)
    found = kernel_call(
        functools.partial(dense_kernel, width), "dense", outs, args, 22, 10, 1, (9, 10, 11), scratch
    )
    return found[:3], found[3:7], found[7:11], found[11:15]


def halves_of(spot, first, second):
    return ((first, 1 - spot[2]), (second, spot[2]))


def up_grad_kernel(spot, p0, p1, p2, p3, other_ref, own_ref, turned, inner):
    width = turned.shape[0]
    for i, part in enumerate((p0, p1, p2, p3)):
        turned[:, i * ROWS : (i + 1) * ROWS] = part[:, :width].T
        inner[i * ROWS : (i + 1) * ROWS, :] = part[:, width:]
    half = width // 2
    for ref, core in halves_of(spot, other_ref, own_ref):
        value = dot(turned[pl.ds(pl.multiple_of(core * half, half), half), :], inner[...]).astype(BF16)
        for g in range(GROUPS):
            ref[g] = value[g * TALL : (g + 1) * TALL]


def up_grad_parts(spot, parts, width):
    tokens, columns = 4 * ROWS, parts[0].shape[1] - width
    out = shaped((GROUPS, TALL, columns))
    scratch = (pltpu.VMEM((width, tokens), BF16), pltpu.VMEM((tokens, columns), BF16))
    return kernel_call(up_grad_kernel, "up_grad", (out, out), (spot, *parts), 16, 4, 1, (), scratch)


def down_grad_kernel(spot, p0, p1, p2, p3, other_ref, own_ref, turned, second, sums):
    parts = (p0, p1, p2, p3)
    width = second.shape[1]
    tall = GROUPS * TALL
    for i, part in enumerate(parts):
        rows = slice(i * ROWS, (i + 1) * ROWS)
        turned[:, rows] = part[:ROWS, width:].T
        second[rows, :] = part[:ROWS, :width]
    total = sum(part[ROWS:, :width].astype(F32) for part in parts)
    for core in range(2):
        start = core * (width // 2)
        sums[core] = jnp.concatenate(
            [total[:EXTRA, start : start + width // 2], total[EXTRA:, start : start + width // 2]], axis=1
        )
    for ref, core in halves_of(spot, other_ref, own_ref):
        down = dot(turned[pl.ds(pl.multiple_of(core * tall, tall), tall), :], second[...])
        for g in range(GROUPS):
            ref[g] = jnp.concatenate([down[g * TALL : (g + 1) * TALL], sums[core]], axis=0).astype(BF16)


def down_grad_parts(spot, parts, width):
    tokens = 4 * ROWS
    out = shaped((GROUPS, TALL + EXTRA, width))
    scratch = (
        pltpu.VMEM((2 * GROUPS * TALL, tokens), BF16),
        pltpu.VMEM((tokens, width), BF16),
        pltpu.VMEM((2, EXTRA, width), F32),
    )
    return kernel_call(down_grad_kernel, "down_grad", (out, out), (spot, *parts), 16, 5, 1, (), scratch)


def pair_sum_kernel(which, turns, spot, own, received, kept, sent):
    for i, out in zip(turns, (sent.at[0], sent.at[1], kept.at[1], kept.at[0])):
        at = spot[which] ^ i
        out[...] = (own[at].astype(F32) + received[at].astype(F32)).astype(BF16)


def pair_sums(spot, own, received, name, which=0, turns=(1, 2, 3, 0)):
    pair = shaped((2, *own.shape[1:]))
    kernel = functools.partial(pair_sum_kernel, which, turns)
    return kernel_call(kernel, name, (pair, pair), (spot, own, received), 16, 2, 1)


def placed(spot, pieces):
    group, quarter = spot[0], spot[1]
    for i in range(4):
        for g in range(GROUPS):
            turn = group ^ g
            at = ((turn & 1) << 1) ^ ((turn >> 1) * 3)
            if i < 3:
                block = pieces[i][at]
            else:
                block = jnp.where(at < 2, pieces[3][at & 1], pieces[4][at & 1])
            yield quarter ^ i, g, block


def place_up_kernel(spot, *refs):
    up_ref = refs[-1]
    for quarter, g, block in placed(spot, refs[:-1]):
        share = block.shape[1] // 2
        block = block.astype(F32)
        for core in range(2):
            at = pl.ds(pl.multiple_of(core * 4 * share + quarter * share, 128), share)
            up_ref[g * TALL : (g + 1) * TALL, at] = block[:, core * share : (core + 1) * share]


BIAS_ROWS = 16


def joined_grad_kernel(pieces, spot, query_grad, *rest):
    keys, values = rest[:pieces], rest[pieces : 2 * pieces]
    inputs = rest[2 * pieces : 2 * pieces + 4]
    contexts = rest[2 * pieces + 4 : 2 * pieces + 8]
    branches = rest[2 * pieces + 8 : 2 * pieces + 12]
    weight, other_ref, own_ref, kept_ref, sent_ref, joined, turned, context_turned, branch = rest[2 * pieces + 12 :]

    def total(parts):
        blocks = [p[0] if len(p.shape) == 3 else p[...] for p in parts]
        return sum(b.astype(F32) for b in blocks).T.astype(BF16)

    joined[:, :WIDTH] = query_grad[...]
    joined[:, WIDTH : 2 * WIDTH] = total(keys)
    joined[:, 2 * WIDTH :] = total(values)
    for i, ref in ((1, sent_ref.at[0]), (2, sent_ref.at[1]), (3, kept_ref.at[1]), (0, kept_ref.at[0])):
        ref[...] = dot(joined[i * ROWS : (i + 1) * ROWS, :], weight[...], TURNED).astype(BF16)
    for i, x in enumerate(inputs):
        at = slice(i * ROWS, (i + 1) * ROWS)
        turned[:, at] = x[...].T
        context_turned[:, at] = contexts[i][...].T
        branch[at, :] = branches[i][...]
    sums = jnp.concatenate(
        [column_sum(joined[...].astype(F32)), jnp.zeros((BIAS_ROWS - 1, 3 * WIDTH), F32)], axis=0
    ).astype(BF16)
    half = turned.shape[0] // 2
    for ref, core in halves_of(spot, other_ref, own_ref):
        value = dot(turned[pl.ds(pl.multiple_of(core * half, half), half), :], joined[...]).astype(BF16)
        strip = WIDTH // 2
        out = dot(context_turned[pl.ds(pl.multiple_of(core * strip, 32), strip), :], branch[...])
        for quarter in range(4):
            ref[quarter, :TALL, :] = value[quarter * TALL : (quarter + 1) * TALL]
            block = out[quarter * SHORT : (quarter + 1) * SHORT]
            last = jnp.concatenate([block[k * 8 : k * 8 + 8, 3 * WIDTH :] for k in range(3)], axis=1)
            packed = jnp.concatenate([block[:, : 3 * WIDTH], last], axis=0)
            ref[quarter, TALL : TALL + PACKED, :] = packed.astype(BF16)
            ref[quarter, TALL + PACKED :, :] = sums


def joined_grads(spot, query_grad, keys, values, inputs, contexts, branches, weight):
    width = weight.shape[0]
    part, pair = shaped((4, TALL + PACKED + BIAS_ROWS, 3 * WIDTH)), shaped((2, ROWS, width))
    tokens = GROUPS * ROWS
    scratch = (
        pltpu.VMEM((tokens, 3 * WIDTH), BF16),
        pltpu.VMEM((width, tokens), BF16),
        pltpu.VMEM((WIDTH, tokens), BF16),
        pltpu.VMEM((tokens, width), BF16),
    )
    args = (spot, query_grad, *keys, *values, *inputs, *contexts, *branches, weight)
    kernel = functools.partial(joined_grad_kernel, len(keys))
    return kernel_call(kernel, "joined_grad", (part, part, pair, pair), args, 16, 6, 1, (), scratch)


def place_down_kernel(spot, *refs):
    down_ref = refs[-1]
    for quarter, g, block in placed(spot, refs[:-1]):
        place = quarter * GROUPS + g
        down_ref[pl.ds(pl.multiple_of(place * TALL, 8), TALL), :] = block.astype(F32)


def place_joined_kernel(spot, *refs):
    weight_ref, bias_ref, kept_ref, sent_ref = refs[-4:]
    core = spot[2]
    width = weight_ref.shape[1] // 3
    found = list(placed(spot, refs[:-4]))
    rows = TALL
    for i in range(4):
        quarter = found[i * GROUPS][0]
        blocks = [block.astype(F32) for _, _, block in found[i * GROUPS : (i + 1) * GROUPS]]
        at = pl.ds(pl.multiple_of(quarter * rows, 16), rows)
        for part in range(3):
            value = jnp.concatenate([b[:, part * WIDTH : (part + 1) * WIDTH] for b in blocks], axis=1)
            weight_ref[at, part * width : (part + 1) * width] = value[:rows]
            if i == 0:
                line = value[rows + PACKED : rows + PACKED + 1]
                bias_ref[part : part + 1, :] = jnp.where(core == 0, line[:, : width // 2], line[:, width // 2 :])
        for g, block in enumerate(blocks):
            last = block[rows + SHORT : rows + PACKED]
            last = jnp.concatenate([last[:, k * WIDTH : (k + 1) * WIDTH] for k in range(3)], axis=0)
            strip = jnp.concatenate([block[rows : rows + SHORT], last], axis=1).astype(BF16)
            target = g // 2

            @pl.when(core == target)
            def _():
                kept_ref[g % 2, quarter] = strip

            @pl.when(core != target)
            def _():
                sent_ref[g % 2, quarter] = strip


def place_out_kernel(spot, kept, received, out_ref):
    core = spot[2]
    for g in range(2):
        for ref, side in ((kept, core), (received, 1 - core)):
            for quarter in range(4):
                start = g * WIDTH + side * (WIDTH // 2) + quarter * SHORT
                out_ref[pl.ds(pl.multiple_of(start, 8), SHORT), :] = ref[g, quarter].astype(F32)


def body(
    tokens,
    cotangent,
    lengths,
    qkv_weight,
    query_bias,
    value_bias,
    out_weight,
    out_bias,
    first_gain,
    first_shift,
    up_weight,
    up_bias,
    down_weight,
    down_bias,
    second_gain,
    second_shift,
):
    row_count, model_width = tokens.shape[1], tokens.shape[2]
    hidden_width = up_weight.shape[1]
    places = Places(lax.axis_size("seq"))
    plane_size, rest = places.plane_size, places.rest
    rank = lax.axis_index("seq")
    core = lax.axis_index("shard")
    group, position = rank // plane_size, rank % plane_size
    quarter = position // rest
    spot = jnp.stack([group, quarter, core]).astype(jnp.int32)
    length = lengths[core]
    inputs = tokens[0]
    column_rows = GROUPS * row_count
    half = model_width // 2
    turns = range(1, GROUPS)

    column_inputs = (inputs, *(places.column_swap(inputs, i) for i in turns))

    def both(block):
        return lax.all_gather(block, "shard", axis=0, tiled=True)

    def own_columns(w):
        at = group * WIDTH
        parts = [lax.dynamic_slice_in_dim(w, at + i * model_width, WIDTH, w.ndim - 1) for i in range(3)]
        return jnp.concatenate(parts, axis=-1)

    group_weight = both(own_columns(qkv_weight))
    vectors = [query_bias, value_bias, out_bias, first_gain, first_shift, down_bias, second_gain, second_shift]
    stacked = jnp.concatenate([jnp.stack(vectors), up_bias.reshape(-1, half)])
    stacked = lax.all_gather(stacked, "shard", axis=0).astype(F32)
    whole = jnp.transpose(stacked[:, : len(vectors)], (1, 0, 2)).reshape(len(vectors), model_width)
    up_offset = stacked[:, len(vectors) :].reshape(1, hidden_width)
    out_matrix = in_hbm(both(out_weight))
    up_matrix = in_hbm(both(up_weight))
    down_matrix = in_hbm(both(down_weight))

    offset = own_columns(jnp.concatenate([whole[0], jnp.zeros_like(whole[0]), whole[1]])).reshape(1, -1)
    query, key_value = kernel_call(
        project_kernel,
        "project",
        (shaped((column_rows, WIDTH)), shaped((column_rows, 2 * WIDTH))),
        (*column_inputs, group_weight, offset),
        16,
        2,
    )

    def masks(who):
        groups = group ^ jnp.arange(GROUPS)
        starts = (groups[None, :] * plane_size + who[:, None]) * row_count
        tokens_at = starts[:, :, None] + jnp.arange(row_count)
        return jnp.where(tokens_at.reshape(1, -1) < length, 0.0, MASKED).astype(F32)

    if plane_size == 4:
        chunks = 1
        key_values = (key_value, *(places.swap(key_value, i) for i in turns))
        bias = tuple(masks((position ^ i)[None]) for i in range(4))
    else:
        chunks = plane_size // 4
        gathered = lax.all_gather(key_value, "seq", axis=0, axis_index_groups=places.planes)
        key_values = (gathered.reshape(-1, 2 * WIDTH),)
        bias = (masks(jnp.arange(plane_size)),)
    context, log_total, context_lows = attend(query, key_values, bias, chunks)
    contexts = (context_lows[0], *(places.column_swap(context_lows[i], i) for i in turns))

    (layer_out, one_grad, branch_low), context_grads, up_parts, down_parts = dense(
        spot, contexts, inputs, in_hbm(cotangent[0]), whole, up_offset, out_matrix, up_matrix, down_matrix
    )
    def after(value, *others):
        return lax.optimization_barrier((value, *others))[0]

    def to_other(block):
        return lax.ppermute(block, "shard", [(0, 1), (1, 0)])

    def rest_sum(total):
        return lax.psum(total, "seq", axis_index_groups=places.rests) if rest > 1 else total

    def add(left, right):
        return (left.astype(F32) + right.astype(F32)).astype(BF16)

    def column_total(kept, sent):
        near = places.column_swap(sent, 1)
        far = places.column_swap(add(kept[1], near[1]), 3)
        return kept[0].astype(F32) + near[0].astype(F32) + far.astype(F32)

    def four_total(kept, sent):
        near = places.four_swap(sent, 1)
        far = places.four_swap(add(kept[1], near[1]), 2)
        return kept[0].astype(F32) + near[0].astype(F32) + far.astype(F32)

    def column_gather(part):
        pair = jnp.stack([part, places.column_swap(part, 3)])
        return jnp.concatenate([pair, places.column_swap(pair, 1)])

    def plane_gather(column, *others):
        first, second = places.four_swap(column, 1), places.four_swap(column, 2)
        halves = (first[:2], second[2:])
        if others:
            halves = after(halves, *others)
        return column, first, second, places.four_swap(halves[0], 2), places.four_swap(halves[1], 1)

    context_grads = (context_grads[0], *(places.column_swap(context_grads[i], i) for i in turns))
    down_parts = (down_parts[0], *(places.four_swap(down_parts[i], i) for i in turns))
    query_grad, parts = attend_grad(query, context, context_grads, log_total, key_values, bias, chunks)
    if plane_size == 4:
        own_key, own_value, turned_key, turned_value, key_x, value_y = parts
        key_x, value_y = first_step = places.swap(key_x, 1), places.swap(value_y, 2)
        keys = (own_key, key_x, places.swap(add(turned_key, key_x[1]), 2))
        values = (own_value, value_y, places.swap(add(turned_value, value_y[1]), 1))
    else:
        blocks = jnp.stack(parts).reshape(2 * WIDTH, plane_size, column_rows)
        blocks = places.exchange(jnp.transpose(blocks, (1, 0, 2)), places.planes)
        blocks = jnp.sum(blocks.astype(F32), axis=0)
        keys, values = first_step = (blocks[:WIDTH],), (blocks[WIDTH:],)
    branch_low = after(branch_low, first_step)
    far = places.column_swap(branch_low, 3)
    branches = (branch_low, places.column_swap(branch_low, 1), places.column_swap(far, 1), far)
    down_parts = after(down_parts, query_grad)
    other, own = down_grad_parts(spot, down_parts, model_width)
    down_pieces = pair_sums(spot, own, to_other(other), "down_sum")
    down_part = rest_sum(column_total(*down_pieces))
    up_parts = after(up_parts, query_grad)
    up_parts = (up_parts[0], *(places.four_swap(up_parts[i], i) for i in turns))
    keys, values = after((keys, values), down_part, up_parts)
    down_column = column_gather(down_part[:TALL].astype(BF16))
    other, own, kept, sent = joined_grads(
        spot, query_grad, keys, values, column_inputs, context_lows, branches, group_weight
    )
    input_grad = one_grad + column_total(kept, sent)
    joined_pieces = pair_sums(spot, own, to_other(other), "joined_sum", 1, (1, 3, 2, 0))
    joined_part = rest_sum(four_total(*joined_pieces)).astype(BF16)
    up_parts = after(up_parts, kept)
    other, own = up_grad_parts(spot, up_parts, model_width)
    up_part = rest_sum(column_total(*pair_sums(spot, own, to_other(other), "up_sum"))).astype(BF16)
    down_all = plane_gather(down_column)
    down_grad = kernel_call(
        place_down_kernel,
        "place_down",
        shaped((hidden_width // 2, model_width), F32),
        (spot, *down_all),
        16,
        5,
        1,
    )
    up_all = plane_gather(after(column_gather(up_part), down_all), down_grad)
    joined_all = plane_gather(after(column_gather(joined_part), down_all), down_grad)
    strips = shaped((2, 4, SHORT, model_width))
    qkv_grad, bias_grad, out_kept, out_sent = kernel_call(
        place_joined_kernel,
        "place_joined",
        (shaped((half, 3 * model_width), F32), shaped((8, half), F32), strips, strips),
        (spot, *joined_all),
        16,
        5,
        1,
    )
    out_grad = kernel_call(
        place_out_kernel, "place_out", shaped((half, model_width), F32), (spot, out_kept, to_other(out_sent)), 8, 2, 1
    )
    up_grad = kernel_call(
        place_up_kernel,
        "place_up",
        shaped((half, hidden_width), F32),
        (spot, *up_all),
        16,
        4,
        1,
    )

    extra = down_part[TALL:]
    up_bias_grad = jnp.concatenate([extra[6, :half], extra[7, :half], extra[0, half:], extra[1, half:]])
    shape = (1, row_count, model_width)
    return (
        layer_out.reshape(shape),
        input_grad.reshape(shape),
        qkv_grad,
        bias_grad[0],
        bias_grad[2],
        out_grad,
        extra[0, :half],
        extra[1, :half],
        extra[2, :half],
        up_grad,
        up_bias_grad,
        down_grad,
        extra[3, :half],
        extra[4, :half],
        extra[5, :half],
    )


def solution(mesh):
    rows, halves, whole = P("shard", "seq", None), P("shard", None), P("shard")
    in_specs = (rows, rows, P(), halves, whole, whole, halves, whole, whole, whole, halves, whole, halves, whole, whole, whole)
    out_specs = (rows, rows, halves, whole, whole, halves, whole, whole, whole, halves, whole, halves, whole, whole, whole)
    return jax.shard_map(body, mesh=mesh, in_specs=in_specs, out_specs=out_specs, check_vma=False)
```

```python
import functools

import jax
import jax.numpy as jnp
from jax import lax
from jax.experimental import pallas as pl
from jax.experimental.pallas import tpu as pltpu
from jax.sharding import PartitionSpec as P

HEADS = 12
HEAD_DIM = 64
GROUPS = 4
GROUP_HEADS = HEADS // GROUPS
WIDTH = GROUP_HEADS * HEAD_DIM
EPSILON = 1e-12
MASKED = -1e30
F32 = jnp.float32
BF16 = jnp.bfloat16
MIB = 2**20
ROWS = 128
TURNED = ((1,), (1,))
FIRST = ((1,), (0,))


def dot(left, right, dims=FIRST):
    return lax.dot_general(left, right, (dims, ((), ())), preferred_element_type=F32)


def kernel_call(kernel, name, outs, args, vmem, micros, smem=0, left=(), scratch=(), after=()):
    spaces = [
        pl.BlockSpec(memory_space=pltpu.SMEM if i < smem else pltpu.HBM if i in left else pltpu.VMEM)
        for i in range(len(args))
    ]
    count = len(args)

    def run(*refs):
        kernel(*refs[:count], *refs[count + len(after) :])

    return pl.pallas_call(
        run if after else kernel,
        out_shape=outs,
        in_specs=spaces + [pl.BlockSpec(memory_space=pl.ANY)] * len(after),
        scratch_shapes=list(scratch),
        compiler_params=pltpu.CompilerParams(vmem_limit_bytes=vmem * MIB),
        cost_estimate=pl.CostEstimate(flops=0, bytes_accessed=int(micros * 3_500_000), transcendentals=0),
        name=name,
    )(*args, *after)


def in_hbm(array):
    return pltpu.with_memory_space_constraint(array, pltpu.HBM)


def shaped(shape, dtype=BF16):
    return jax.ShapeDtypeStruct(shape, dtype)


class Places:
    def __init__(self, size):
        self.size = size
        self.plane_size = size // GROUPS
        self.rest = self.plane_size // 4
        index = lambda g, q, m: (g * 4 + q) * self.rest + m
        groups, quarters, members = range(GROUPS), range(4), range(self.rest)
        self.columns = [[index(g, q, m) for g in groups] for q in quarters for m in members]
        self.planes = [[index(g, q, m) for q in quarters for m in members] for g in groups]
        self.fours = [[index(g, q, m) for q in quarters] for g in groups for m in members]
        self.sixteens = [[index(g, q, m) for g in groups for q in quarters] for m in members]
        self.rests = [[index(g, q, m) for m in members] for g in groups for q in quarters]

    def swap(self, block, bits):
        return lax.ppermute(block, "seq", [(i, i ^ bits) for i in range(self.size)])

    def column_swap(self, block, turn):
        return self.swap(block, turn * self.plane_size)

    def four_swap(self, block, turn):
        return self.swap(block, turn * self.rest)

    def exchange(self, blocks, groups):
        return lax.all_to_all(blocks, "seq", 0, 0, axis_index_groups=groups, tiled=True)


def project_kernel(x0, x1, x2, x3, weight, offset, query_ref, key_value_ref):
    for i, x in enumerate((x0, x1, x2, x3)):
        at = slice(i * ROWS, (i + 1) * ROWS)
        joined = (dot(x[...], weight[...]) + offset[...]).astype(BF16)
        query_ref[at, :] = joined[:, :WIDTH] * jnp.asarray(0.125, BF16)
        key_value_ref[at, :] = joined[:, WIDTH:]


SPAN = 512


def attend_kernel(pieces, chunks, *refs):
    q_ref = refs[0]
    key_value_refs, bias_refs = refs[1 : 1 + pieces], refs[1 + pieces : 1 + 2 * pieces]
    context_ref, log_ref = refs[1 + 2 * pieces : 3 + 2 * pieces]
    low_refs = refs[3 + 2 * pieces :]
    rows = q_ref.shape[0]
    chunk = key_value_refs[0].shape[0] // chunks
    for block in range(rows // SPAN):
        at = slice(block * SPAN, (block + 1) * SPAN)
        for head in range(GROUP_HEADS):
            columns = slice(head * HEAD_DIM, (head + 1) * HEAD_DIM)
            value_columns = slice(WIDTH + head * HEAD_DIM, WIDTH + (head + 1) * HEAD_DIM)
            query = q_ref[at, columns]

            def step(index, state):
                highest, total, mix = state
                here = pl.ds(pl.multiple_of(index * chunk, chunk), chunk)
                scores = [dot(query, k[here, columns], TURNED) + b[:, here] for k, b in zip(key_value_refs, bias_refs)]
                peak = functools.reduce(jnp.maximum, [jnp.max(s, axis=1, keepdims=True) for s in scores])
                raised = jnp.maximum(highest, peak)
                weights = [jnp.exp(s - raised) for s in scores]
                factor = jnp.exp(highest - raised)
                total = total * factor + sum(jnp.sum(w, axis=1, keepdims=True) for w in weights)
                mix = mix * factor + sum(
                    dot(w.astype(BF16), v[here, value_columns]) for w, v in zip(weights, key_value_refs)
                )
                return raised, total, mix

            state = (
                jnp.full((SPAN, 1), MASKED, F32),
                jnp.zeros((SPAN, 1), F32),
                jnp.zeros((SPAN, HEAD_DIM), F32),
            )
            highest, total, mix = step(0, state) if chunks == 1 else lax.fori_loop(0, chunks, step, state)
            context = mix / total
            context_ref[at, columns] = context
            for part in range(SPAN // ROWS):
                low = context[part * ROWS : (part + 1) * ROWS].astype(BF16)
                low_refs[block * (SPAN // ROWS) + part][:, columns] = low
            log_ref[at, head : head + 1] = highest + jnp.log(total)


def attend(query, key_values, bias, chunks):
    rows = query.shape[0]
    outs = (shaped((rows, WIDTH), F32), shaped((rows, 128), F32)) + (shaped((ROWS, WIDTH)),) * GROUPS
    kernel = functools.partial(attend_kernel, len(key_values), chunks)
    found = kernel_call(kernel, "attend", outs, (query, *key_values, *bias), 24 if chunks == 1 else 60, 9)
    return found[0], found[1], found[2:]


def attend_grad_kernel(pieces, chunks, *refs):
    q_ref, context_ref, log_ref = refs[:3]
    grad_refs = refs[3:7]
    key_value_refs, bias_refs = refs[7 : 7 + pieces], refs[7 + pieces : 7 + 2 * pieces]
    query_grad_ref = refs[7 + 2 * pieces]
    outs = refs[8 + 2 * pieces :]
    if pieces == 4:
        own_key, own_value, turned_key, turned_value, key_x, value_y = outs
        key_outs = (own_key, key_x.at[0], turned_key, key_x.at[1])
        value_outs = (own_value, turned_value, value_y.at[0], value_y.at[1])
    else:
        key_outs, value_outs = outs[:1], outs[1:]
    rows = q_ref.shape[0]
    chunk = key_value_refs[0].shape[0] // chunks
    for head in range(GROUP_HEADS):
        columns = slice(head * HEAD_DIM, (head + 1) * HEAD_DIM)
        value_columns = slice(WIDTH + head * HEAD_DIM, WIDTH + (head + 1) * HEAD_DIM)
        query = q_ref[:, columns]
        grad = jnp.concatenate([g[:, columns] for g in grad_refs], axis=0)
        correction = jnp.sum(grad.astype(F32) * context_ref[:, columns], axis=1, keepdims=True)
        log_total = log_ref[:, head : head + 1]
        query_turned = query.T
        grad_turned = grad.T

        def step(index, query_grad):
            here = pl.ds(pl.multiple_of(index * chunk, chunk), chunk)
            for both, b, key_out, value_out in zip(key_value_refs, bias_refs, key_outs, value_outs):
                key = both[here, columns]
                probs = jnp.exp(dot(query, key, TURNED) + b[:, here] - log_total)
                probs_grad = dot(grad, both[here, value_columns], TURNED)
                score_grad = (probs * (probs_grad - correction)).astype(BF16)
                query_grad = query_grad + dot(score_grad, key)
                key_out[columns, here] = dot(query_turned, score_grad).astype(BF16)
                value_out[columns, here] = dot(grad_turned, probs.astype(BF16)).astype(BF16)
            return query_grad

        total = jnp.zeros((rows, HEAD_DIM), F32)
        total = step(0, total) if chunks == 1 else lax.fori_loop(0, chunks, step, total)
        query_grad_ref[:, columns] = (total * 0.125).astype(BF16)


def attend_grad(query, context, grads, log_total, key_values, bias, chunks):
    rows, keys = query.shape[0], key_values[0].shape[0]
    one, two = shaped((WIDTH, keys)), shaped((2, WIDTH, keys))
    outs = (shaped((rows, WIDTH)),) + ((one, one, one, one, two, two) if len(key_values) == 4 else (one, one))
    kernel = functools.partial(attend_grad_kernel, len(key_values), chunks)
    args = (query, context, log_total, *grads, *key_values, *bias)
    found = kernel_call(kernel, "attend_grad", outs, args, 32 if chunks == 1 else 60, 11)
    return found[0], found[1:]


def normalize(hidden):
    center = hidden - jnp.mean(hidden, axis=1, keepdims=True)
    scale = lax.rsqrt(jnp.mean(center * center, axis=1, keepdims=True) + EPSILON)
    return center * scale, scale


def normalize_grad(grad, normal, scale):
    return scale * (
        grad
        - jnp.mean(grad, axis=1, keepdims=True)
        - normal * jnp.mean(grad * normal, axis=1, keepdims=True)
    )


def column_sum(values):
    return jnp.sum(values, axis=0, keepdims=True)


TALL, SHORT, EXTRA = 96, 24, 8
PACKED = 32


def dense_kernel(width, spot, c0, c1, c2, c3, x_ref, grad_ref, vectors, up_offset, out_hbm, up_hbm, down_hbm, *rest):
    layer_ref, one_grad_ref = rest[:2]
    branch_ref = rest[2]
    context_grads, up_parts, down_parts = rest[3:7], rest[7:11], rest[11:15]
    out_w, up_w, down_w, slope, active_ref, inner_ref, sums_ref, sems = rest[15:]
    copies = [
        pltpu.make_async_copy(source, target, sems.at[i])
        for i, (source, target) in enumerate(((out_hbm, out_w), (up_hbm, up_w), (down_hbm, down_w)))
    ]
    for copy in copies:
        copy.start()
    hidden = up_w.shape[1]
    half = width // 2
    out_offset, gain_one, shift_one, down_offset, gain_two, shift_two = (vectors[i : i + 1, :] for i in range(2, 8))
    group, quarter = spot[0], spot[1]
    contexts = (c0, c1, c2, c3)

    def turned(i):
        return pl.ds(pl.multiple_of((group ^ i) * WIDTH, WIDTH), WIDTH)

    copies[0].wait()
    branch = sum(dot(c[...], out_w[turned(i), :]) for i, c in enumerate(contexts)) + out_offset
    normal_one, scale_one = normalize(x_ref[...].astype(F32) + branch)
    normed_low = (normal_one * gain_one + shift_one).astype(BF16)
    for ref in up_parts:
        ref[:, :width] = normed_low
    copies[1].wait()
    step = 1536
    for start in range(0, hidden, step):
        at = slice(start, start + step)
        inner = dot(normed_low, up_w[:, at]) + up_offset[:, at]
        share = 0.5 + 0.5 * lax.erf(inner * 0.7071067811865476)
        density = 0.3989422804014327 * jnp.exp(-0.5 * inner * inner)
        slope[:, at] = share + inner * density
        active_ref[:, at] = (inner * share).astype(BF16)
    copies[2].wait()
    second = dot(active_ref[...], down_w[...]) + down_offset
    normal_two, scale_two = normalize(normed_low.astype(F32) + second)
    layer_ref[...] = (normal_two * gain_two + shift_two).astype(BF16)
    grad = grad_ref[...].astype(F32)
    gain_two_grad, shift_two_grad = column_sum(grad * normal_two), column_sum(grad)
    two_grad = normalize_grad(grad * gain_two, normal_two, scale_two)
    second_low = two_grad.astype(BF16)
    down_bias_grad = column_sum(second_low.astype(F32))
    normed_grad = two_grad
    for start in range(0, hidden, step):
        at = slice(start, start + step)
        inner_low = (dot(second_low, down_w[at, :], TURNED) * slope[:, at]).astype(BF16)
        inner_ref[:, at] = inner_low
        up_sum = column_sum(inner_low.astype(F32))
        for piece in range(step // half):
            place = start // half + piece
            per_core = hidden // 2 // half
            row, core = 6 + place % per_core, place // per_core
            sums_ref[row : row + 1, core * half : (core + 1) * half] = up_sum[:, piece * half : (piece + 1) * half]
        normed_grad = normed_grad + dot(inner_low, up_w[:, at], TURNED)
    gain_one_grad, shift_one_grad = column_sum(normed_grad * normal_one), column_sum(normed_grad)
    one_grad = normalize_grad(normed_grad * gain_one, normal_one, scale_one)
    one_grad_ref[...] = one_grad
    branch_low = one_grad.astype(BF16)
    branch_ref[...] = branch_low
    for i, ref in enumerate(context_grads):
        ref[...] = dot(branch_low, out_w[turned(i), :], TURNED).astype(BF16)
    out_bias_grad = column_sum(branch_low.astype(F32))
    sums = (out_bias_grad, gain_one_grad, shift_one_grad, down_bias_grad, gain_two_grad, shift_two_grad)
    for i, total in enumerate(sums):
        sums_ref[i : i + 1, :] = total
    sums_ref[10:16, :] = jnp.zeros((6, width), F32)
    share = hidden // 8
    for i in range(4):
        for core in range(2):
            at = pl.ds(pl.multiple_of(core * (hidden // 2) + (quarter ^ i) * share, share), share)
            to = slice(width + core * share, width + (core + 1) * share)
            up_parts[i][:, to] = inner_ref[:, at]
            down_parts[i][:ROWS, to] = active_ref[:, at]
        down_parts[i][:ROWS, :width] = second_low
        down_parts[i][ROWS:, :width] = sums_ref[...].astype(BF16)


def dense(spot, contexts, inputs, grad, vectors, up_offset, out_matrix, up_matrix, down_matrix):
    width, hidden = up_matrix.shape
    outs = (
        (shaped((ROWS, width)), shaped((ROWS, width), F32), shaped((ROWS, width)))
        + (shaped((ROWS, WIDTH)),) * GROUPS
        + (shaped((ROWS, width + hidden // 4)),) * 4
        + (shaped((ROWS + 16, width + hidden // 4)),) * 4
    )
    scratch = (
        pltpu.VMEM(out_matrix.shape, BF16),
        pltpu.VMEM(up_matrix.shape, BF16),
        pltpu.VMEM(down_matrix.shape, BF16),
        pltpu.VMEM((ROWS, hidden), F32),
        pltpu.VMEM((ROWS, hidden), BF16),
        pltpu.VMEM((ROWS, hidden), BF16),
        pltpu.VMEM((16, width), F32),
        pltpu.SemaphoreType.DMA((3,)),
    )
    args = (spot, *contexts, inputs, grad, vectors, up_offset, out_matrix, up_matrix, down_matrix)
    found = kernel_call(
        functools.partial(dense_kernel, width), "dense", outs, args, 22, 10, 1, (9, 10, 11), scratch
    )
    return found[:3], found[3:7], found[7:11], found[11:15]


def halves_of(spot, first, second):
    return ((first, 1 - spot[2]), (second, spot[2]))


def up_grad_kernel(spot, p0, p1, p2, p3, other_ref, own_ref, turned, inner):
    width = turned.shape[0]
    for i, part in enumerate((p0, p1, p2, p3)):
        turned[:, i * ROWS : (i + 1) * ROWS] = part[:, :width].T
        inner[i * ROWS : (i + 1) * ROWS, :] = part[:, width:]
    half = width // 2
    for ref, core in halves_of(spot, other_ref, own_ref):
        value = dot(turned[pl.ds(pl.multiple_of(core * half, half), half), :], inner[...]).astype(BF16)
        for g in range(GROUPS):
            ref[g] = value[g * TALL : (g + 1) * TALL]


def up_grad_parts(spot, parts, width):
    tokens, columns = 4 * ROWS, parts[0].shape[1] - width
    out = shaped((GROUPS, TALL, columns))
    scratch = (pltpu.VMEM((width, tokens), BF16), pltpu.VMEM((tokens, columns), BF16))
    return kernel_call(up_grad_kernel, "up_grad", (out, out), (spot, *parts), 16, 4, 1, (), scratch)


def down_grad_kernel(spot, p0, p1, p2, p3, other_ref, own_ref, turned, second, sums):
    parts = (p0, p1, p2, p3)
    width = second.shape[1]
    tall = GROUPS * TALL
    for i, part in enumerate(parts):
        rows = slice(i * ROWS, (i + 1) * ROWS)
        turned[:, rows] = part[:ROWS, width:].T
        second[rows, :] = part[:ROWS, :width]
    total = sum(part[ROWS:, :width].astype(F32) for part in parts)
    for core in range(2):
        start = core * (width // 2)
        sums[core] = jnp.concatenate(
            [total[:EXTRA, start : start + width // 2], total[EXTRA:, start : start + width // 2]], axis=1
        )
    for ref, core in halves_of(spot, other_ref, own_ref):
        down = dot(turned[pl.ds(pl.multiple_of(core * tall, tall), tall), :], second[...])
        for g in range(GROUPS):
            ref[g] = jnp.concatenate([down[g * TALL : (g + 1) * TALL], sums[core]], axis=0).astype(BF16)


def down_grad_parts(spot, parts, width):
    tokens = 4 * ROWS
    out = shaped((GROUPS, TALL + EXTRA, width))
    scratch = (
        pltpu.VMEM((2 * GROUPS * TALL, tokens), BF16),
        pltpu.VMEM((tokens, width), BF16),
        pltpu.VMEM((2, EXTRA, width), F32),
    )
    return kernel_call(down_grad_kernel, "down_grad", (out, out), (spot, *parts), 16, 5, 1, (), scratch)


def pair_sum_kernel(which, turns, spot, own, received, kept, sent):
    for i, out in zip(turns, (sent.at[0], sent.at[1], kept.at[1], kept.at[0])):
        at = spot[which] ^ i
        out[...] = (own[at].astype(F32) + received[at].astype(F32)).astype(BF16)


def pair_sums(spot, own, received, name, which=0, turns=(1, 2, 3, 0)):
    pair = shaped((2, *own.shape[1:]))
    kernel = functools.partial(pair_sum_kernel, which, turns)
    return kernel_call(kernel, name, (pair, pair), (spot, own, received), 16, 2, 1)


def placed(spot, pieces):
    group, quarter = spot[0], spot[1]
    for i in range(4):
        for g in range(GROUPS):
            turn = group ^ g
            at = ((turn & 1) << 1) ^ ((turn >> 1) * 3)
            if i < 3:
                block = pieces[i][at]
            else:
                block = jnp.where(at < 2, pieces[3][at & 1], pieces[4][at & 1])
            yield quarter ^ i, g, block


def place_up_kernel(spot, *refs):
    up_ref = refs[-1]
    for quarter, g, block in placed(spot, refs[:-1]):
        share = block.shape[1] // 2
        block = block.astype(F32)
        for core in range(2):
            at = pl.ds(pl.multiple_of(core * 4 * share + quarter * share, 128), share)
            up_ref[g * TALL : (g + 1) * TALL, at] = block[:, core * share : (core + 1) * share]


BIAS_ROWS = 16


def joined_grad_kernel(pieces, spot, query_grad, *rest):
    keys, values = rest[:pieces], rest[pieces : 2 * pieces]
    inputs = rest[2 * pieces : 2 * pieces + 4]
    contexts = rest[2 * pieces + 4 : 2 * pieces + 8]
    branches = rest[2 * pieces + 8 : 2 * pieces + 12]
    weight, other_ref, own_ref, kept_ref, sent_ref, joined, turned, context_turned, branch = rest[2 * pieces + 12 :]

    def total(parts):
        blocks = [p[0] if len(p.shape) == 3 else p[...] for p in parts]
        return sum(b.astype(F32) for b in blocks).T.astype(BF16)

    joined[:, :WIDTH] = query_grad[...]
    joined[:, WIDTH : 2 * WIDTH] = total(keys)
    joined[:, 2 * WIDTH :] = total(values)
    for i, ref in ((1, sent_ref.at[0]), (2, sent_ref.at[1]), (3, kept_ref.at[1]), (0, kept_ref.at[0])):
        ref[...] = dot(joined[i * ROWS : (i + 1) * ROWS, :], weight[...], TURNED).astype(BF16)
    for i, x in enumerate(inputs):
        at = slice(i * ROWS, (i + 1) * ROWS)
        turned[:, at] = x[...].T
        context_turned[:, at] = contexts[i][...].T
        branch[at, :] = branches[i][...]
    sums = jnp.concatenate(
        [column_sum(joined[...].astype(F32)), jnp.zeros((BIAS_ROWS - 1, 3 * WIDTH), F32)], axis=0
    ).astype(BF16)
    half = turned.shape[0] // 2
    for ref, core in halves_of(spot, other_ref, own_ref):
        value = dot(turned[pl.ds(pl.multiple_of(core * half, half), half), :], joined[...]).astype(BF16)
        strip = WIDTH // 2
        out = dot(context_turned[pl.ds(pl.multiple_of(core * strip, 32), strip), :], branch[...])
        for quarter in range(4):
            ref[quarter, :TALL, :] = value[quarter * TALL : (quarter + 1) * TALL]
            block = out[quarter * SHORT : (quarter + 1) * SHORT]
            last = jnp.concatenate([block[k * 8 : k * 8 + 8, 3 * WIDTH :] for k in range(3)], axis=1)
            packed = jnp.concatenate([block[:, : 3 * WIDTH], last], axis=0)
            ref[quarter, TALL : TALL + PACKED, :] = packed.astype(BF16)
            ref[quarter, TALL + PACKED :, :] = sums


def joined_grads(spot, query_grad, keys, values, inputs, contexts, branches, weight):
    width = weight.shape[0]
    part, pair = shaped((4, TALL + PACKED + BIAS_ROWS, 3 * WIDTH)), shaped((2, ROWS, width))
    tokens = GROUPS * ROWS
    scratch = (
        pltpu.VMEM((tokens, 3 * WIDTH), BF16),
        pltpu.VMEM((width, tokens), BF16),
        pltpu.VMEM((WIDTH, tokens), BF16),
        pltpu.VMEM((tokens, width), BF16),
    )
    args = (spot, query_grad, *keys, *values, *inputs, *contexts, *branches, weight)
    kernel = functools.partial(joined_grad_kernel, len(keys))
    return kernel_call(kernel, "joined_grad", (part, part, pair, pair), args, 16, 6, 1, (), scratch)


def place_down_kernel(spot, *refs):
    down_ref = refs[-1]
    for quarter, g, block in placed(spot, refs[:-1]):
        place = quarter * GROUPS + g
        down_ref[pl.ds(pl.multiple_of(place * TALL, 8), TALL), :] = block.astype(F32)


def place_joined_kernel(spot, *refs):
    weight_ref, bias_ref, kept_ref, sent_ref = refs[-4:]
    core = spot[2]
    width = weight_ref.shape[1] // 3
    found = list(placed(spot, refs[:-4]))
    rows = TALL
    for i in range(4):
        quarter = found[i * GROUPS][0]
        blocks = [block.astype(F32) for _, _, block in found[i * GROUPS : (i + 1) * GROUPS]]
        at = pl.ds(pl.multiple_of(quarter * rows, 16), rows)
        for part in range(3):
            value = jnp.concatenate([b[:, part * WIDTH : (part + 1) * WIDTH] for b in blocks], axis=1)
            weight_ref[at, part * width : (part + 1) * width] = value[:rows]
            if i == 0:
                line = value[rows + PACKED : rows + PACKED + 1]
                bias_ref[part : part + 1, :] = jnp.where(core == 0, line[:, : width // 2], line[:, width // 2 :])
        for g, block in enumerate(blocks):
            last = block[rows + SHORT : rows + PACKED]
            last = jnp.concatenate([last[:, k * WIDTH : (k + 1) * WIDTH] for k in range(3)], axis=0)
            strip = jnp.concatenate([block[rows : rows + SHORT], last], axis=1).astype(BF16)
            target = g // 2

            @pl.when(core == target)
            def _():
                kept_ref[g % 2, quarter] = strip

            @pl.when(core != target)
            def _():
                sent_ref[g % 2, quarter] = strip


def place_out_kernel(spot, kept, received, out_ref):
    core = spot[2]
    for g in range(2):
        for ref, side in ((kept, core), (received, 1 - core)):
            for quarter in range(4):
                start = g * WIDTH + side * (WIDTH // 2) + quarter * SHORT
                out_ref[pl.ds(pl.multiple_of(start, 8), SHORT), :] = ref[g, quarter].astype(F32)


def body(
    tokens,
    cotangent,
    lengths,
    qkv_weight,
    query_bias,
    value_bias,
    out_weight,
    out_bias,
    first_gain,
    first_shift,
    up_weight,
    up_bias,
    down_weight,
    down_bias,
    second_gain,
    second_shift,
):
    row_count, model_width = tokens.shape[1], tokens.shape[2]
    hidden_width = up_weight.shape[1]
    places = Places(lax.axis_size("seq"))
    plane_size, rest = places.plane_size, places.rest
    rank = lax.axis_index("seq")
    core = lax.axis_index("shard")
    group, position = rank // plane_size, rank % plane_size
    quarter = position // rest
    spot = jnp.stack([group, quarter, core]).astype(jnp.int32)
    length = lengths[core]
    inputs = tokens[0]
    column_rows = GROUPS * row_count
    half = model_width // 2
    turns = range(1, GROUPS)

    column_inputs = (inputs, *(places.column_swap(inputs, i) for i in turns))

    def both(block):
        return lax.all_gather(block, "shard", axis=0, tiled=True)

    def own_columns(w):
        at = group * WIDTH
        parts = [lax.dynamic_slice_in_dim(w, at + i * model_width, WIDTH, w.ndim - 1) for i in range(3)]
        return jnp.concatenate(parts, axis=-1)

    group_weight = both(own_columns(qkv_weight))
    vectors = [query_bias, value_bias, out_bias, first_gain, first_shift, down_bias, second_gain, second_shift]
    stacked = jnp.concatenate([jnp.stack(vectors), up_bias.reshape(-1, half)])
    stacked = lax.all_gather(stacked, "shard", axis=0).astype(F32)
    whole = jnp.transpose(stacked[:, : len(vectors)], (1, 0, 2)).reshape(len(vectors), model_width)
    up_offset = stacked[:, len(vectors) :].reshape(1, hidden_width)
    out_matrix = in_hbm(both(out_weight))
    up_matrix = in_hbm(both(up_weight))
    down_matrix = in_hbm(both(down_weight))

    offset = own_columns(jnp.concatenate([whole[0], jnp.zeros_like(whole[0]), whole[1]])).reshape(1, -1)
    query, key_value = kernel_call(
        project_kernel,
        "project",
        (shaped((column_rows, WIDTH)), shaped((column_rows, 2 * WIDTH))),
        (*column_inputs, group_weight, offset),
        16,
        2,
    )

    def masks(who):
        groups = group ^ jnp.arange(GROUPS)
        starts = (groups[None, :] * plane_size + who[:, None]) * row_count
        tokens_at = starts[:, :, None] + jnp.arange(row_count)
        return jnp.where(tokens_at.reshape(1, -1) < length, 0.0, MASKED).astype(F32)

    if plane_size == 4:
        chunks = 1
        key_values = (key_value, *(places.swap(key_value, i) for i in turns))
        bias = tuple(masks((position ^ i)[None]) for i in range(4))
    else:
        chunks = plane_size // 4
        gathered = lax.all_gather(key_value, "seq", axis=0, axis_index_groups=places.planes)
        key_values = (gathered.reshape(-1, 2 * WIDTH),)
        bias = (masks(jnp.arange(plane_size)),)
    context, log_total, context_lows = attend(query, key_values, bias, chunks)
    contexts = (context_lows[0], *(places.column_swap(context_lows[i], i) for i in turns))

    (layer_out, one_grad, branch_low), context_grads, up_parts, down_parts = dense(
        spot, contexts, inputs, in_hbm(cotangent[0]), whole, up_offset, out_matrix, up_matrix, down_matrix
    )
    def after(value, *others):
        return lax.optimization_barrier((value, *others))[0]

    def to_other(block):
        return lax.ppermute(block, "shard", [(0, 1), (1, 0)])

    def rest_sum(total):
        return lax.psum(total, "seq", axis_index_groups=places.rests) if rest > 1 else total

    def add(left, right):
        return (left.astype(F32) + right.astype(F32)).astype(BF16)

    def column_total(kept, sent):
        near = places.column_swap(sent, 1)
        far = places.column_swap(add(kept[1], near[1]), 3)
        return kept[0].astype(F32) + near[0].astype(F32) + far.astype(F32)

    def four_total(kept, sent):
        near = places.four_swap(sent, 1)
        far = places.four_swap(add(kept[1], near[1]), 2)
        return kept[0].astype(F32) + near[0].astype(F32) + far.astype(F32)

    def column_gather(part):
        pair = jnp.stack([part, places.column_swap(part, 3)])
        return jnp.concatenate([pair, places.column_swap(pair, 1)])

    def plane_gather(column, *others):
        first, second = places.four_swap(column, 1), places.four_swap(column, 2)
        halves = (first[:2], second[2:])
        if others:
            halves = after(halves, *others)
        return column, first, second, places.four_swap(halves[0], 2), places.four_swap(halves[1], 1)

    context_grads = (context_grads[0], *(places.column_swap(context_grads[i], i) for i in turns))
    down_parts = (down_parts[0], *(places.four_swap(down_parts[i], i) for i in turns))
    query_grad, parts = attend_grad(query, context, context_grads, log_total, key_values, bias, chunks)
    if plane_size == 4:
        own_key, own_value, turned_key, turned_value, key_x, value_y = parts
        key_x, value_y = first_step = places.swap(key_x, 1), places.swap(value_y, 2)
        keys = (own_key, key_x, places.swap(add(turned_key, key_x[1]), 2))
        values = (own_value, value_y, places.swap(add(turned_value, value_y[1]), 1))
    else:
        blocks = jnp.stack(parts).reshape(2 * WIDTH, plane_size, column_rows)
        blocks = places.exchange(jnp.transpose(blocks, (1, 0, 2)), places.planes)
        blocks = jnp.sum(blocks.astype(F32), axis=0)
        keys, values = first_step = (blocks[:WIDTH],), (blocks[WIDTH:],)
    branch_low = after(branch_low, first_step)
    far = places.column_swap(branch_low, 3)
    branches = (branch_low, places.column_swap(branch_low, 1), places.column_swap(far, 1), far)
    down_parts = after(down_parts, query_grad)
    other, own = down_grad_parts(spot, down_parts, model_width)
    down_pieces = pair_sums(spot, own, to_other(other), "down_sum")
    down_part = rest_sum(column_total(*down_pieces))
    up_parts = after(up_parts, query_grad)
    up_parts = (up_parts[0], *(places.four_swap(up_parts[i], i) for i in turns))
    keys, values = after((keys, values), down_part, up_parts)
    down_column = column_gather(down_part[:TALL].astype(BF16))
    other, own, kept, sent = joined_grads(
        spot, query_grad, keys, values, column_inputs, context_lows, branches, group_weight
    )
    input_grad = one_grad + column_total(kept, sent)
    joined_pieces = pair_sums(spot, own, to_other(other), "joined_sum", 1, (1, 3, 2, 0))
    joined_part = rest_sum(four_total(*joined_pieces)).astype(BF16)
    up_parts = after(up_parts, kept)
    other, own = up_grad_parts(spot, up_parts, model_width)
    up_part = rest_sum(column_total(*pair_sums(spot, own, to_other(other), "up_sum"))).astype(BF16)
    down_all = plane_gather(down_column)
    down_grad = kernel_call(
        place_down_kernel,
        "place_down",
        shaped((hidden_width // 2, model_width), F32),
        (spot, *down_all),
        16,
        5,
        1,
    )
    up_all = plane_gather(after(column_gather(up_part), down_all), down_grad)
    joined_all = plane_gather(after(column_gather(joined_part), down_all), down_grad)
    strips = shaped((2, 4, SHORT, model_width))
    qkv_grad, bias_grad, out_kept, out_sent = kernel_call(
        place_joined_kernel,
        "place_joined",
        (shaped((half, 3 * model_width), F32), shaped((8, half), F32), strips, strips),
        (spot, *joined_all),
        16,
        5,
        1,
    )
    out_grad = kernel_call(
        place_out_kernel, "place_out", shaped((half, model_width), F32), (spot, out_kept, to_other(out_sent)), 8, 2, 1
    )
    up_grad = kernel_call(
        place_up_kernel,
        "place_up",
        shaped((half, hidden_width), F32),
        (spot, *up_all),
        16,
        4,
        1,
    )

    extra = down_part[TALL:]
    up_bias_grad = jnp.concatenate([extra[6, :half], extra[7, :half], extra[0, half:], extra[1, half:]])
    shape = (1, row_count, model_width)
    return (
        layer_out.reshape(shape),
        input_grad.reshape(shape),
        qkv_grad,
        bias_grad[0],
        bias_grad[2],
        out_grad,
        extra[0, :half],
        extra[1, :half],
        extra[2, :half],
        up_grad,
        up_bias_grad,
        down_grad,
        extra[3, :half],
        extra[4, :half],
        extra[5, :half],
    )


def solution(mesh):
    rows, halves, whole = P("shard", "seq", None), P("shard", None), P("shard")
    in_specs = (rows, rows, P(), halves, whole, whole, halves, whole, whole, whole, halves, whole, halves, whole, whole, whole)
    out_specs = (rows, rows, halves, whole, whole, halves, whole, whole, whole, halves, whole, halves, whole, whole, whole)
    return jax.shard_map(body, mesh=mesh, in_specs=in_specs, out_specs=out_specs, check_vma=False)
```
